32 devices in a mesh: batch: 16 (over z, x, core), blk: 2 (over y).
Axes of the slice: x: 2, y: 2, z: 4, core: 2. Of those that a mesh axis runs over, the one named last changes fastest.
Arguments:
- inputs: bfloat16 [32, 1024, 1024], P('batch', 'blk'), may hold values from -6 to 6
- memory: bfloat16 [32, 1024, 1024], P('batch', 'blk'), may hold values from -6 to 6
- target_ids: int32 [32, 1024], P('batch', 'blk'), may hold values from 0 to 1, as said below
- memory_ids: int32 [32, 1024], P('batch', 'blk'), may hold values from 0 to 1, as said below
- cotangent: bfloat16 [32, 1024, 1024], P('batch', 'blk'), may hold values from -6 to 6
- w_self_qkv: bfloat16 [1024, 3072], P('batch'), may hold values from -0.25 to 0.25
- w_self_out: bfloat16 [1024, 1024], P('batch'), may hold values from -2 to 2
- w_cross_q: bfloat16 [1024, 1024], P('batch'), may hold values from -0.25 to 0.25
- w_cross_kv: bfloat16 [1024, 2048], P('batch'), may hold values from -0.25 to 0.25
- w_cross_out: bfloat16 [1024, 1024], P('batch'), may hold values from -2 to 2
- w_up: bfloat16 [1024, 4096], P('batch'), may hold values from -0.1875 to 0.1875
- w_down: bfloat16 [4096, 1024], P('batch'), may hold values from -0.5 to 0.5
- b_up: bfloat16 [4096], P('batch'), may hold values from -3 to 3
- gains: bfloat16 [3, 1024], P(None, 'batch'), may hold values from 0.25 to 1.75
- shifts: bfloat16 [4, 1024], P(None, 'batch'), may hold values from -3 to 3
Outputs:
- output: bfloat16 [32, 1024, 1024], P('batch', 'blk')
- d_input: float32 [32, 1024, 1024], P('batch', 'blk')
- d_memory: float32 [32, 1024, 1024], P('batch', 'blk')
- d_w_self_qkv: float32 [1024, 3072], P('batch')
- d_w_self_out: float32 [1024, 1024], P('batch')
- d_w_cross_q: float32 [1024, 1024], P('batch')
- d_w_cross_kv: float32 [1024, 2048], P('batch')
- d_w_cross_out: float32 [1024, 1024], P('batch')
- d_w_up: float32 [1024, 4096], P('batch')
- d_w_down: float32 [4096, 1024], P('batch')
- d_b_up: float32 [4096], P('batch')
- d_gains: float32 [3, 1024], P(None, 'batch')
- d_shifts: float32 [4, 1024], P(None, 'batch')
The draws below stay inside these ranges and needn't reach their ends.
Inputs may be any that keep to these rules, and one draw needn't show every extreme that they name: `target_ids`: two packed documents a row: ids are 0 before a cut and 1 from it on, so each document has one token or more. `memory_ids`: two packed documents a memory row, numbered as those of the target row: 0 before a cut and 1 from it on, each with one token or more.
All inputs are finite; a program needn't handle non-finite values.
Results may differ from the reference program's by a relative error of at most 0.03.
The reference program's roundings to bfloat16 on the way count: a program that leaves them out, or rounds other values in their place, can miss the bound.
Values may be sent and summed in bfloat16 or wider, within the bound.
No kernel may reach another device: no remote copies, remote signals or barrier semaphores. Data moves between devices by JAX's collectives and lax.ppermute only.
A program may use at most 312 MiB of HBM per device.

```python
import jax
import jax.numpy as jnp
from jax import lax

D = 1024
FF = 4096
NH = 16
HD = 64
SEQ = 1024
MEM = 1024
TOK_DEV = 512
ROWS = 32


def two_documents(key, length):
    coin_key, place_key = jax.random.split(key)
    coin_flips = jax.random.randint(coin_key, (ROWS, 1), 0, 2)
    offsets = jax.random.randint(place_key, (ROWS, 1), 1, TOK_DEV)
    cut_place = jnp.where(coin_flips == 1, offsets, length - offsets)
    places = jnp.arange(length, dtype=jnp.int32)[None, :]
    return (places >= cut_place).astype(jnp.int32)


def draw_target_ids(key, part):
    key = jax.random.fold_in(key, 11)
    return two_documents(key, SEQ)


def draw_memory_ids(key, part):
    key = jax.random.fold_in(key, 23)
    return two_documents(key, MEM)


def steps_of(rng, dims, shards, smallest, top_value):
    gain = 1.0
    for dim, parts in shards:
        heights = jax.random.uniform(jax.random.fold_in(jax.random.fold_in(rng, 6), dim), (parts,), jnp.float32, smallest / len(shards), top_value / len(shards))
        gain = gain * jnp.repeat(jnp.exp(heights), dims[dim] // parts).reshape((-1,) + (1,) * (len(dims) - 1 - dim))
    return gain


def gaussian(rng, shape, deviation, reach, pieces=(), held_as=jnp.bfloat16):
    entries = jax.random.normal(rng, shape, jnp.float32) * deviation
    if len(pieces) > 0:
        entries = steps_of(rng, shape, pieces, -0.22, 0.18) * entries
    return jnp.clip(entries, min=-reach, max=reach).astype(held_as)


def setup_inputs(seed: int = 0) -> dict:
    key_list = jax.random.split(jax.random.key(seed), 16)
    return {
        "inputs": gaussian(key_list[0], (ROWS, SEQ, D), 1.0, 6.0, ((0, 16), (1, 2))),
        "memory": gaussian(key_list[1], (ROWS, MEM, D), 1.0, 6.0, ((0, 16), (1, 2))),
        "target_ids": draw_target_ids(jax.random.fold_in(key_list[15], 71), 0),
        "memory_ids": draw_memory_ids(jax.random.fold_in(key_list[15], 71), 0),
        "cotangent": gaussian(key_list[4], (ROWS, SEQ, D), 1.0, 6.0, ((0, 16), (1, 2))),
        "w_self_qkv": gaussian(key_list[5], (D, 3 * D), (D // 2) ** -0.5, 0.25, ((0, 16),)),
        "w_self_out": gaussian(key_list[6], (D, D), (D // 128) ** -0.5, 2.0, ((0, 16),)),
        "w_cross_q": gaussian(key_list[7], (D, D), (D // 2) ** -0.5, 0.25, ((0, 16),)),
        "w_cross_kv": gaussian(key_list[8], (D, 2 * D), (D // 2) ** -0.5, 0.25, ((0, 16),)),
        "w_cross_out": gaussian(key_list[9], (D, D), (D // 128) ** -0.5, 2.0, ((0, 16),)),
        "w_up": gaussian(key_list[10], (D, FF), D ** -0.5, 0.1875, ((0, 16),)),
        "w_down": gaussian(key_list[11], (FF, D), (FF // 32) ** -0.5, 0.5, ((0, 16),)),
        "b_up": gaussian(key_list[12], (FF,), 0.5, 3.0, ((0, 16),)),
        "gains": jnp.clip(1.0 + 0.15 * jax.random.normal(key_list[13], (3, D), jnp.float32), 0.25, 1.75).astype(jnp.bfloat16),
        "shifts": gaussian(key_list[14], (4, D), 0.5, 3.0, ((1, 16),)),
    }


@jax.custom_vjp
def low(v):
    return lax.optimization_barrier(v.astype(jnp.bfloat16)).astype(jnp.float32)

@jax.custom_vjp
def low_back(v):
    return v

def low_keep(v):
    return (low(v), None)

def low_pass(kept, grad):
    return (grad,)

def back_keep(v):
    return (v, None)

def back_low(kept, grad):
    return (low(grad),)
low.defvjp(low_keep, low_pass)
low_back.defvjp(back_keep, back_low)
ALPHA = 300.0 ** 0.25
MASKED = -1e+30
EPSILON = 1e-05

def product(left, right):
    return jnp.dot(left, right, precision=lax.Precision.HIGHEST, preferred_element_type=jnp.float32)

def layer_norm(summed, gain_row, shift_row):
    average = lax.optimization_barrier(jnp.mean(summed, axis=-1, keepdims=True))
    centred = summed - average
    spread = lax.optimization_barrier(jnp.mean(centred * centred, axis=-1, keepdims=True))
    return centred * lax.rsqrt(spread + EPSILON) * gain_row + shift_row

def attend(queries, key_rows, value_rows, allowed):
    query_count = queries.shape[0]
    query_heads = queries.reshape(query_count, NH, HD)
    key_heads = key_rows.reshape(key_rows.shape[0], NH, HD)
    value_heads = value_rows.reshape(value_rows.shape[0], NH, HD)
    scores = jnp.einsum('qhd,khd->hqk', query_heads, key_heads, precision=lax.Precision.HIGHEST) * HD ** (-0.5)
    scores = jnp.where(allowed[None], low_back(scores), MASKED)
    row_peak = lax.optimization_barrier(jnp.max(scores, axis=-1, keepdims=True))
    raised = jnp.exp(scores - row_peak)
    probabilities = low(raised / lax.optimization_barrier(jnp.sum(raised, axis=-1, keepdims=True)))
    attended = jnp.einsum('hqk,khd->qhd', probabilities, value_heads, precision=lax.Precision.HIGHEST)
    return low_back(low(attended.reshape(query_count, NH * HD)))

def forward(params, given_rows, memory_rows, target_rows, memory_segs):
    w_qkv, w_out, w_cq, w_ckv, w_cout, w_first, w_second, bias_up, gain_rows, shift_rows = params
    row_count, length, model_width = given_rows.shape
    memory_length = memory_rows.shape[1]
    flat_in = given_rows.reshape(-1, model_width)
    projected = low_back(low(product(flat_in, w_qkv))).reshape(row_count, length, 3 * model_width)
    places = jnp.arange(length)
    causal = places[None, :] <= places[:, None]

    def self_row(item):
        proj_row, seg_row = item
        allowed = (seg_row[:, None] == seg_row[None, :]) & causal
        return attend(proj_row[:, :model_width], proj_row[:, model_width:2 * model_width], proj_row[:, 2 * model_width:], allowed)
    self_mixed = lax.map(jax.checkpoint(self_row), (projected, target_rows))
    branch_one = low_back(product(self_mixed.reshape(-1, model_width), w_out))
    first = layer_norm(ALPHA * flat_in + branch_one, gain_rows[0], shift_rows[0])
    cross_query = low_back(low(product(low(first), w_cq))).reshape(row_count, length, model_width)
    memory_pairs = low_back(low(product(memory_rows.reshape(-1, model_width), w_ckv)))
    memory_pairs = memory_pairs.reshape(row_count, memory_length, 2 * model_width)

    def cross_row(item):
        query_row, pair_row, seg_row, memory_seg_row = item
        allowed = seg_row[:, None] == memory_seg_row[None, :]
        return attend(query_row, pair_row[:, :model_width], pair_row[:, model_width:], allowed)
    cross_mixed = lax.map(jax.checkpoint(cross_row), (cross_query, memory_pairs, target_rows, memory_segs))
    branch_two = low_back(product(cross_mixed.reshape(-1, model_width), w_cout))
    second = layer_norm(ALPHA * first + branch_two, gain_rows[1], shift_rows[1])
    hidden_pre = low_back(product(low(second), w_first) + bias_up)
    hidden = low_back(low(jax.nn.gelu(hidden_pre)))
    branch_three = low_back(product(hidden, w_second) + shift_rows[3])
    result = layer_norm(ALPHA * second + branch_three, gain_rows[2], shift_rows[2])
    return result.reshape(row_count, length, model_width)

def reference(inputs, memory, target_ids, memory_ids, cotangent, w_self_qkv, w_self_out, w_cross_q, w_cross_kv, w_cross_out, w_up, w_down, b_up, gains, shifts):
    weights = tuple((item.astype(jnp.float32) for item in (w_self_qkv, w_self_out, w_cross_q, w_cross_kv, w_cross_out, w_up, w_down, b_up, gains, shifts)))
    row_group = 4 if ROWS % 4 == 0 else 1

    def regroup(array):
        return array.reshape((ROWS // row_group, row_group) + array.shape[1:])

    def scan_step(totals, batch_item):
        rows_in, rows_memory, rows_target, rows_memory_ids, rows_cotangent = batch_item

        def forward_rows(params, given_rows, memory_rows):
            return forward(params, given_rows, memory_rows, rows_target, rows_memory_ids)
        result, pullback = jax.vjp(forward_rows, weights, rows_in.astype(jnp.float32), rows_memory.astype(jnp.float32))
        grad_params, grad_in, grad_memory = pullback(rows_cotangent.astype(jnp.float32))
        totals = jax.tree.map(jnp.add, totals, grad_params)
        return (totals, (result.astype(jnp.bfloat16), grad_in, grad_memory))
    zero_grads = jax.tree.map(jnp.zeros_like, weights)
    totals, (result, grad_in, grad_memory) = lax.scan(scan_step, zero_grads, (regroup(inputs), regroup(memory), regroup(target_ids), regroup(memory_ids), regroup(cotangent)))
    return (result.reshape(ROWS, SEQ, D), grad_in.reshape(ROWS, SEQ, D), grad_memory.reshape(ROWS, MEM, D), totals[0], totals[1], totals[2], totals[3], totals[4], totals[5], totals[6], totals[7], totals[8], totals[9])
```

```python
import functools

import jax
import jax.numpy as jnp
from jax import lax
from jax.experimental import pallas as pl
from jax.experimental.pallas import tpu as pltpu
from jax.sharding import PartitionSpec as P

D = 1024
NH = 16
HD = 64
MB_ROWS = 1
MICRO = 2
ALPHA = 300.0**0.25
MASKED = -1e30
EPSILON = 1e-05
PAIR = 2 * HD
BLOCK = 256
MASK_STEP = -(2.0**100)


def nt(left, right):
    return lax.dot_general(left, right, (((1,), (1,)), ((), ())), preferred_element_type=jnp.float32)


def nn(left, right):
    return lax.dot_general(left, right, (((1,), (0,)), ((), ())), preferred_element_type=jnp.float32)


def lane_of(rows):
    return lax.broadcasted_iota(jnp.int32, (rows, PAIR), 1)


def attention_fwd_kernel(causal, q_ref, k_ref, v_ref, fq_ref, fk_ref, out_ref, lse_ref):
    length = q_ref.shape[0]
    mem = k_ref.shape[0]
    low_q = lane_of(length) < HD
    low_k = lane_of(mem) < HD
    q = q_ref[...] * jnp.bfloat16(HD**-0.5)
    k = k_ref[...]
    v = v_ref[...]
    fq = fq_ref[...]
    fk = fk_ref[...]
    ones = jnp.ones_like(v)
    queries = (jnp.where(low_q, q, fq), jnp.where(low_q, fq, q))
    keys = (jnp.where(low_k, k, fk), jnp.where(low_k, fk, k))
    values = (jnp.where(low_k, v, ones), jnp.where(low_k, ones, v))
    low_blk = lane_of(BLOCK) < HD
    for i in range(length // BLOCK):
        seen = (i + 1) * BLOCK if causal else mem
        rows = slice(i * BLOCK, (i + 1) * BLOCK)
        accs, peaks = [], []
        for h in range(2):
            scores = nt(queries[h][rows], keys[h][:seen])
            if causal:
                tri = lax.broadcasted_iota(jnp.int32, (BLOCK, BLOCK), 0) >= lax.broadcasted_iota(
                    jnp.int32, (BLOCK, BLOCK), 1
                )
                diag = jnp.where(tri, scores[:, seen - BLOCK :], MASK_STEP)
                scores = diag if i == 0 else jnp.concatenate([scores[:, : seen - BLOCK], diag], axis=1)
            peak = jnp.max(scores, axis=1, keepdims=True)
            raised = jnp.exp(scores - peak).astype(jnp.bfloat16)
            accs.append(nn(raised, values[h][:seen]))
            peaks.append(peak)
        total = pltpu.roll(jnp.where(low_blk, accs[1], accs[0]), HD, 1)
        out_ref[rows, :] = (jnp.where(low_blk, accs[0], accs[1]) / total).astype(out_ref.dtype)
        lse_ref[rows, :] = jnp.where(low_blk, peaks[0], peaks[1]) + jnp.log(total)


def split3(value):
    hi = value.astype(jnp.bfloat16)
    rest = value - hi.astype(jnp.float32)
    mid = rest.astype(jnp.bfloat16)
    lo = (rest - mid.astype(jnp.float32)).astype(jnp.bfloat16)
    return hi, mid, lo


def placed(lane, start, pieces, other):
    for n, piece in enumerate(pieces):
        other = jnp.where(lane == start + n, piece, other)
    return other


def attention_bwd_kernel(causal, q_ref, k_ref, v_ref, fq_ref, fk_ref, out_ref, lse_ref, do_ref, dq_ref, dk_ref, dv_ref, dk_acc, dv_acc, dq_acc):
    length = q_ref.shape[0]
    mem = k_ref.shape[0]
    lane_q = lane_of(length)
    lane_k = lane_of(mem)
    low_q = lane_q < HD
    low_k = lane_k < HD
    scale = jnp.bfloat16(HD**-0.5)
    q = q_ref[...] * scale
    k = k_ref[...]
    v = v_ref[...]
    do = do_ref[...]
    fq = fq_ref[...]
    fk = fk_ref[...]
    zero_q = jnp.zeros_like(q)
    zero_k = jnp.zeros_like(k)
    one_k = jnp.ones_like(k)
    prod = do.astype(jnp.float32) * out_ref[...].astype(jnp.float32)
    sum_a = jnp.sum(jnp.where(low_q, prod, 0.0), axis=1, keepdims=True)
    sum_b = jnp.sum(jnp.where(low_q, 0.0, prod), axis=1, keepdims=True)
    inner = jnp.where(low_q, sum_b, sum_a)
    lse = pltpu.roll(lse_ref[...], HD, 1)
    half_q = lane_q & (HD - 1)
    half_k = lane_k & (HD - 1)
    fq = placed(half_q, 2, split3(-lse), fq)
    fk = jnp.where((half_k >= 2) & (half_k < 5), one_k, fk)
    fd = placed(half_q, 0, split3(-inner), zero_q)
    fv = jnp.where(half_k < 3, one_k, zero_k)
    queries = (jnp.where(low_q, q, fq), jnp.where(low_q, fq, q))
    keys = (jnp.where(low_k, k, fk), jnp.where(low_k, fk, k))
    grads = (jnp.where(low_q, do, fd), jnp.where(low_q, fd, do))
    values = (jnp.where(low_k, v, fv), jnp.where(low_k, fv, v))
    plain_q = (jnp.where(low_q, q, zero_q), jnp.where(low_q, zero_q, q))
    plain_do = (jnp.where(low_q, do, zero_q), jnp.where(low_q, zero_q, do))
    k_t = k.T
    blocks = length // BLOCK
    for i in range(blocks):
        rows = slice(i * BLOCK, (i + 1) * BLOCK)
        seen = (i + 1) * BLOCK if causal else mem
        probs, d_scores = [], []
        for h in range(2):
            p = jnp.exp(nt(keys[h][:seen], queries[h][rows]))
            if causal:
                tri = lax.broadcasted_iota(jnp.int32, (BLOCK, BLOCK), 0) <= lax.broadcasted_iota(
                    jnp.int32, (BLOCK, BLOCK), 1
                )
                diag = jnp.where(tri, p[seen - BLOCK :], 0.0)
                p = diag if i == 0 else jnp.concatenate([p[: seen - BLOCK], diag], axis=0)
            ds = (p * nt(values[h][:seen], grads[h][rows])).astype(jnp.bfloat16)
            probs.append(p.astype(jnp.bfloat16))
            d_scores.append(ds)
            dq_acc[h * HD : (h + 1) * HD, rows] = nn(k_t[h * HD : (h + 1) * HD, :seen], ds)
        dv = nn(probs[0], plain_do[0][rows]) + nn(probs[1], plain_do[1][rows])
        dk = nn(d_scores[0], plain_q[0][rows]) + nn(d_scores[1], plain_q[1][rows])
        if i == 0:
            dv_acc[:seen] = dv
            dk_acc[:seen] = dk
        elif causal:
            dv_acc[: seen - BLOCK] += dv[: seen - BLOCK]
            dk_acc[: seen - BLOCK] += dk[: seen - BLOCK]
            dv_acc[seen - BLOCK : seen] = dv[seen - BLOCK :]
            dk_acc[seen - BLOCK : seen] = dk[seen - BLOCK :]
        else:
            dv_acc[...] += dv
            dk_acc[...] += dk
    dq_ref[...] = (dq_acc[...].T * (HD**-0.5)).astype(dq_ref.dtype)
    dk_ref[...] = dk_acc[...].astype(dk_ref.dtype)
    dv_ref[...] = dv_acc[...].astype(dv_ref.dtype)


def cols(length, first):
    return pl.BlockSpec((length, PAIR), lambda j: (0, first + j))


def whole(length):
    return pl.BlockSpec((length, PAIR), lambda j: (0, 0))


def attention_forward(q_src, q_at, kv_src, k_at, v_at, fq, fk, causal):
    length, mem = q_src.shape[0], kv_src.shape[0]
    pairs = NH // 2
    return pl.pallas_call(
        functools.partial(attention_fwd_kernel, causal),
        grid=(pairs,),
        in_specs=[cols(length, q_at), cols(mem, k_at), cols(mem, v_at), whole(length), whole(mem)],
        out_specs=[cols(length, 0), cols(length, 0)],
        out_shape=[
            jax.ShapeDtypeStruct((length, D), jnp.bfloat16),
            jax.ShapeDtypeStruct((length, D), jnp.float32),
        ],
        compiler_params=pltpu.CompilerParams(vmem_limit_bytes=48 * 2**20),
        name="attention_forward",
    )(q_src, kv_src, kv_src, fq, fk)


def attention_backward(q_src, q_at, kv_src, k_at, v_at, fq, fk, mixed, lse, d_mixed, causal):
    length, mem = q_src.shape[0], kv_src.shape[0]
    pairs = NH // 2
    return pl.pallas_call(
        functools.partial(attention_bwd_kernel, causal),
        grid=(pairs,),
        in_specs=[cols(length, q_at), cols(mem, k_at), cols(mem, v_at), whole(length), whole(mem),
                  cols(length, 0), cols(length, 0), cols(length, 0)],
        out_specs=[cols(length, 0), cols(mem, 0), cols(mem, 0)],
        out_shape=[
            jax.ShapeDtypeStruct((length, D), jnp.bfloat16),
            jax.ShapeDtypeStruct((mem, D), jnp.bfloat16),
            jax.ShapeDtypeStruct((mem, D), jnp.bfloat16),
        ],
        scratch_shapes=[
            pltpu.VMEM((mem, PAIR), jnp.float32),
            pltpu.VMEM((mem, PAIR), jnp.float32),
            pltpu.VMEM((PAIR, length), jnp.float32),
        ],
        compiler_params=pltpu.CompilerParams(vmem_limit_bytes=48 * 2**20),
        name="attention_backward",
    )(q_src, kv_src, kv_src, fq, fk, mixed, lse, d_mixed)


def document_features(query_ids, key_ids):
    half = jnp.arange(PAIR, dtype=jnp.int32)[None, :] % HD
    fq = (half == query_ids[:, None]).astype(jnp.bfloat16)
    fk = jnp.where((half < 2) & (half != key_ids[:, None]), MASK_STEP, 0.0).astype(jnp.bfloat16)
    return fq, fk


def shortened(array):
    return jax.tree.map(lambda a: a.astype(jnp.bfloat16) if a.dtype == jnp.float32 else a, array)


def layer_norm(summed, gain_row, shift_row):
    average = jnp.mean(summed, axis=-1, keepdims=True)
    centred = summed - average
    spread = jnp.mean(centred * centred, axis=-1, keepdims=True)
    return centred * lax.rsqrt(spread + EPSILON) * gain_row + shift_row


def split_heads(array_in):
    return array_in.reshape(array_in.shape[0], array_in.shape[1], NH, HD)


def weight_grad(left_rows, right_rows):
    return jnp.einsum("tk,tn->kn", left_rows, right_rows, preferred_element_type=jnp.float32)


def back_prod(grad_rows, matrix):
    return jnp.einsum("tn,kn->tk", grad_rows, matrix, preferred_element_type=jnp.float32)


def attention_scores(queries, key_rows, allowed):
    scores = jnp.einsum(
        "rqhd,rkhd->rhqk",
        split_heads(queries),
        split_heads(key_rows),
        preferred_element_type=jnp.float32,
    ) * HD ** (-0.5)
    return jnp.where(allowed[:, None], scores, MASKED)


def plain_attention_forward(queries, key_rows, value_rows, allowed):
    scores = attention_scores(queries, key_rows, allowed)
    row_peak = jnp.max(scores, axis=-1, keepdims=True)
    raised = jnp.exp(scores - row_peak)
    row_total = jnp.sum(raised, axis=-1, keepdims=True)
    probabilities = (raised / row_total).astype(jnp.bfloat16)
    attended = jnp.einsum(
        "rhqk,rkhd->rqhd",
        probabilities,
        split_heads(value_rows),
        preferred_element_type=jnp.float32,
    )
    return (attended.reshape(queries.shape).astype(jnp.bfloat16), row_peak, row_total)


def plain_attention_backward(queries, key_rows, value_rows, allowed, row_peak, row_total, d_attended):
    scores = attention_scores(queries, key_rows, allowed)
    probabilities = jnp.exp(scores - row_peak) / row_total
    d_heads = split_heads(d_attended)
    d_values = jnp.einsum(
        "rhqk,rqhd->rkhd",
        probabilities.astype(jnp.bfloat16),
        d_heads,
        preferred_element_type=jnp.float32,
    )
    d_probs = jnp.einsum(
        "rqhd,rkhd->rhqk", d_heads, split_heads(value_rows), preferred_element_type=jnp.float32
    )
    inner_sum = jnp.sum(probabilities * d_probs, axis=-1, keepdims=True)
    d_scores = (probabilities * (d_probs - inner_sum)).astype(jnp.bfloat16)
    d_queries = jnp.einsum(
        "rhqk,rkhd->rqhd", d_scores, split_heads(key_rows), preferred_element_type=jnp.float32
    ) * HD ** (-0.5)
    d_keys = jnp.einsum(
        "rhqk,rqhd->rkhd", d_scores, split_heads(queries), preferred_element_type=jnp.float32
    ) * HD ** (-0.5)
    d_pairs = jnp.concatenate(
        [d_keys.reshape(key_rows.shape), d_values.reshape(value_rows.shape)], axis=2
    )
    return (d_queries.reshape(queries.shape), d_pairs)


def add_terms(running, fresh):
    if running is None:
        return fresh
    return tuple((first_term + second_term for first_term, second_term in zip(running, fresh)))


def split_row_device(
    inputs,
    memory,
    target_ids,
    memory_ids,
    cotangent,
    w_self_qkv,
    w_self_out,
    w_cross_q,
    w_cross_kv,
    w_cross_out,
    w_up,
    w_down,
    b_up,
    gains,
    shifts,
):
    tokens_here = inputs.shape[1]
    length = tokens_here * lax.axis_size("blk")
    token_count = MB_ROWS * tokens_here
    query_places = lax.axis_index("blk") * tokens_here + jnp.arange(tokens_here, dtype=jnp.int32)
    key_places = jnp.arange(length, dtype=jnp.int32)
    causal = key_places[None, :] <= query_places[:, None]
    outputs, input_grads, memory_grads = ([], [], [])
    attn_total = None
    ffn_total = None
    for micro_step in range(MICRO):
        row_range = slice(micro_step * MB_ROWS, (micro_step + 1) * MB_ROWS)
        qkv_full, out_full, cross_q_full, cross_kv_full, cross_out_full, gain_low, shift_low = (
            lax.all_gather(w_self_qkv, "batch", axis=0, tiled=True),
            lax.all_gather(w_self_out, "batch", axis=0, tiled=True),
            lax.all_gather(w_cross_q, "batch", axis=0, tiled=True),
            lax.all_gather(w_cross_kv, "batch", axis=0, tiled=True),
            lax.all_gather(w_cross_out, "batch", axis=0, tiled=True),
            lax.all_gather(gains, "batch", axis=1, tiled=True),
            lax.all_gather(shifts, "batch", axis=1, tiled=True),
        )
        gain_full = gain_low.astype(jnp.float32)
        shift_full = shift_low.astype(jnp.float32)
        x_flat = inputs[row_range].reshape(token_count, D)
        memory_flat = memory[row_range].reshape(token_count, D)
        seg_rows = target_ids[row_range]
        memory_seg_rows = memory_ids[row_range]
        projected = (
            jnp.dot(x_flat, qkv_full, preferred_element_type=jnp.float32)
            .astype(jnp.bfloat16)
            .reshape(MB_ROWS, tokens_here, 3 * D)
        )
        self_queries = projected[:, :, :D]
        key_pairs, key_segs = (
            lax.all_gather(projected[:, :, D:], "blk", axis=1, tiled=True),
            lax.all_gather(seg_rows, "blk", axis=1, tiled=True),
        )
        self_allowed = (seg_rows[:, :, None] == key_segs[:, None, :]) & causal[None]
        self_mixed, self_peak, self_total = plain_attention_forward(
            self_queries, key_pairs[:, :, :D], key_pairs[:, :, D:], self_allowed
        )
        mixed_flat = self_mixed.reshape(token_count, D)
        first_sum = ALPHA * x_flat.astype(jnp.float32) + jnp.dot(
            mixed_flat, out_full, preferred_element_type=jnp.float32
        )
        first = layer_norm(first_sum, gain_full[0], shift_full[0])
        first_low = first.astype(jnp.bfloat16)
        cross_queries = (
            jnp.dot(first_low, cross_q_full, preferred_element_type=jnp.float32)
            .astype(jnp.bfloat16)
            .reshape(MB_ROWS, tokens_here, D)
        )
        memory_local = (
            jnp.dot(memory_flat, cross_kv_full, preferred_element_type=jnp.float32)
            .astype(jnp.bfloat16)
            .reshape(MB_ROWS, tokens_here, 2 * D)
        )
        memory_pairs, memory_segs = (
            lax.all_gather(memory_local, "blk", axis=1, tiled=True),
            lax.all_gather(memory_seg_rows, "blk", axis=1, tiled=True),
        )
        cross_allowed = seg_rows[:, :, None] == memory_segs[:, None, :]
        cross_mixed, cross_peak, cross_total = plain_attention_forward(
            cross_queries, memory_pairs[:, :, :D], memory_pairs[:, :, D:], cross_allowed
        )
        cross_flat = cross_mixed.reshape(token_count, D)
        second_sum = ALPHA * first + jnp.dot(
            cross_flat, cross_out_full, preferred_element_type=jnp.float32
        )
        second = layer_norm(second_sum, gain_full[1], shift_full[1])
        second_low = second.astype(jnp.bfloat16)
        up_full, down_full, bias_full = (
            lax.all_gather(w_up, "batch", axis=0, tiled=True),
            lax.all_gather(w_down, "batch", axis=0, tiled=True),
            lax.all_gather(b_up, "batch", axis=0, tiled=True),
        )
        hidden_pre = jnp.dot(
            second_low, up_full, preferred_element_type=jnp.float32
        ) + bias_full.astype(jnp.float32)
        hidden_low = jax.nn.gelu(hidden_pre).astype(jnp.bfloat16)
        third_sum = (
            ALPHA * second
            + jnp.dot(hidden_low, down_full, preferred_element_type=jnp.float32)
            + shift_full[3]
        )
        result, third_back = jax.vjp(layer_norm, third_sum, gain_full[2], shift_full[2])
        outputs.append(result.astype(jnp.bfloat16).reshape(MB_ROWS, tokens_here, D))
        cot_flat = cotangent[row_range].reshape(token_count, D).astype(jnp.float32)
        d_third, d_gain_three, d_shift_three = third_back(cot_flat)
        d_branch_three = d_third.astype(jnp.bfloat16)
        grad_down = weight_grad(hidden_low, d_branch_three)
        grad_bias_down = jnp.sum(d_branch_three.astype(jnp.float32), axis=0)
        d_hidden = back_prod(d_branch_three, down_full).astype(jnp.bfloat16)
        gelu_back = jax.vjp(jax.nn.gelu, hidden_pre)[1]
        d_pre = gelu_back(d_hidden.astype(jnp.float32))[0].astype(jnp.bfloat16)
        grad_up = weight_grad(second_low, d_pre)
        grad_bias_up = jnp.sum(d_pre.astype(jnp.float32), axis=0)
        d_second = ALPHA * d_third + back_prod(d_pre, up_full)
        ffn_terms = (grad_up, grad_down, grad_bias_up)
        ffn_share = (
            lax.psum_scatter(
                ffn_terms[0].astype(jnp.bfloat16), "batch", scatter_dimension=0, tiled=True
            ).astype(jnp.float32),
            lax.psum_scatter(
                ffn_terms[1].astype(jnp.bfloat16), "batch", scatter_dimension=0, tiled=True
            ).astype(jnp.float32),
            lax.psum_scatter(
                ffn_terms[2].astype(jnp.bfloat16), "batch", scatter_dimension=0, tiled=True
            ).astype(jnp.float32),
        )
        ffn_total = add_terms(ffn_total, ffn_share)
        second_back = jax.vjp(layer_norm, second_sum, gain_full[1], shift_full[1])[1]
        d_second_sum, d_gain_two, d_shift_two = second_back(d_second)
        d_branch_two = d_second_sum.astype(jnp.bfloat16)
        grad_cross_out = weight_grad(cross_flat, d_branch_two)
        d_cross = (
            back_prod(d_branch_two, cross_out_full)
            .astype(jnp.bfloat16)
            .reshape(MB_ROWS, tokens_here, D)
        )
        d_cross_queries, d_memory_all = plain_attention_backward(
            cross_queries,
            memory_pairs[:, :, :D],
            memory_pairs[:, :, D:],
            cross_allowed,
            cross_peak,
            cross_total,
            d_cross,
        )
        d_memory_pairs = lax.psum_scatter(
            d_memory_all.astype(jnp.bfloat16), "blk", scatter_dimension=1, tiled=True
        ).reshape(token_count, 2 * D)
        grad_cross_kv = weight_grad(memory_flat, d_memory_pairs)
        memory_grads.append(
            back_prod(d_memory_pairs, cross_kv_full).reshape(MB_ROWS, tokens_here, D)
        )
        d_cross_low = d_cross_queries.astype(jnp.bfloat16).reshape(token_count, D)
        grad_cross_q = weight_grad(first_low, d_cross_low)
        d_first = ALPHA * d_second_sum + back_prod(d_cross_low, cross_q_full)
        first_back = jax.vjp(layer_norm, first_sum, gain_full[0], shift_full[0])[1]
        d_first_sum, d_gain_one, d_shift_one = first_back(d_first)
        d_branch_one = d_first_sum.astype(jnp.bfloat16)
        grad_self_out = weight_grad(mixed_flat, d_branch_one)
        d_self = (
            back_prod(d_branch_one, out_full).astype(jnp.bfloat16).reshape(MB_ROWS, tokens_here, D)
        )
        d_self_queries, d_key_all = plain_attention_backward(
            self_queries,
            key_pairs[:, :, :D],
            key_pairs[:, :, D:],
            self_allowed,
            self_peak,
            self_total,
            d_self,
        )
        d_self_pairs = lax.psum_scatter(
            d_key_all.astype(jnp.bfloat16), "blk", scatter_dimension=1, tiled=True
        )
        d_projected = jnp.concatenate(
            [d_self_queries.astype(jnp.bfloat16), d_self_pairs], axis=2
        ).reshape(token_count, 3 * D)
        grad_self_qkv = weight_grad(x_flat, d_projected)
        input_grads.append(
            (ALPHA * d_first_sum + back_prod(d_projected, qkv_full)).reshape(
                MB_ROWS, tokens_here, D
            )
        )
        grad_gains = jnp.stack([d_gain_one, d_gain_two, d_gain_three])
        grad_shifts = jnp.stack([d_shift_one, d_shift_two, d_shift_three, grad_bias_down])
        attn_terms = (
            grad_self_qkv,
            grad_self_out,
            grad_cross_q,
            grad_cross_kv,
            grad_cross_out,
            grad_gains,
            grad_shifts,
        )
        attn_share = (
            lax.psum_scatter(
                attn_terms[0].astype(jnp.bfloat16), "batch", scatter_dimension=0, tiled=True
            ).astype(jnp.float32),
            lax.psum_scatter(
                attn_terms[1].astype(jnp.bfloat16), "batch", scatter_dimension=0, tiled=True
            ).astype(jnp.float32),
            lax.psum_scatter(
                attn_terms[2].astype(jnp.bfloat16), "batch", scatter_dimension=0, tiled=True
            ).astype(jnp.float32),
            lax.psum_scatter(
                attn_terms[3].astype(jnp.bfloat16), "batch", scatter_dimension=0, tiled=True
            ).astype(jnp.float32),
            lax.psum_scatter(
                attn_terms[4].astype(jnp.bfloat16), "batch", scatter_dimension=0, tiled=True
            ).astype(jnp.float32),
            lax.psum_scatter(
                attn_terms[5].astype(jnp.bfloat16), "batch", scatter_dimension=1, tiled=True
            ).astype(jnp.float32),
            lax.psum_scatter(
                attn_terms[6].astype(jnp.bfloat16), "batch", scatter_dimension=1, tiled=True
            ).astype(jnp.float32),
        )
        attn_total = add_terms(attn_total, attn_share)
    grad_parts = tuple(attn_total) + tuple(ffn_total)
    totals = jax.tree.map(
        lambda part: part.astype(jnp.float32), lax.psum(shortened(grad_parts), "blk")
    )
    output = jnp.concatenate(outputs, axis=0)
    d_input = jnp.concatenate(input_grads, axis=0)
    d_memory = jnp.concatenate(memory_grads, axis=0)
    return (
        output,
        d_input,
        d_memory,
        totals[0],
        totals[1],
        totals[2],
        totals[3],
        totals[4],
        totals[7],
        totals[8],
        totals[9],
        totals[5],
        totals[6],
    )


def swap_pair(array):
    return lax.ppermute(array, "blk", [(0, 1), (1, 0)])


def rows_in(array):
    count = lax.axis_size("blk")
    here = array.shape[0] // count
    parts = array.reshape((count, here) + array.shape[1:])
    if count == 1:
        return parts[0]
    if count == 2:
        me = lax.axis_index("blk")
        kept = lax.dynamic_index_in_dim(parts, me, 0, keepdims=False)
        got = swap_pair(lax.dynamic_index_in_dim(parts, 1 - me, 0, keepdims=False))
        first = jnp.where(me == 0, kept, got)
        second = jnp.where(me == 0, got, kept)
        return jnp.concatenate([first, second], axis=1)
    moved = lax.all_to_all(parts, "blk", 0, 0)
    moved = jnp.moveaxis(moved, 0, 1)
    return moved.reshape((here, count * array.shape[1]) + array.shape[2:])


def rows_out(array, kind):
    count = lax.axis_size("blk")
    here, length = array.shape[:2]
    tokens = length // count
    parts = array.reshape((here, count, tokens) + array.shape[2:])
    if count == 1:
        return parts[:, 0].astype(kind)
    if count == 2:
        me = lax.axis_index("blk")
        kept = lax.dynamic_index_in_dim(parts, me, 1, keepdims=False).astype(kind)
        sent = lax.dynamic_index_in_dim(parts, 1 - me, 1, keepdims=False).astype(jnp.bfloat16)
        got = swap_pair(sent).astype(kind)
        first = jnp.where(me == 0, kept, got)
        second = jnp.where(me == 0, got, kept)
        return jnp.concatenate([first, second], axis=0)
    moved = lax.all_to_all(jnp.moveaxis(parts, 1, 0).astype(jnp.bfloat16), "blk", 0, 0)
    return moved.reshape((count * here, tokens) + array.shape[2:]).astype(kind)


def gathered(shard, axis=0):
    return lax.all_gather(shard, "batch", axis=axis, tiled=True)


def shared_out(grad, axis=0):
    part = lax.psum_scatter(
        grad.astype(jnp.bfloat16), "batch", scatter_dimension=axis, tiled=True
    )
    return lax.psum(part, "blk").astype(jnp.float32)


def each_row(function, rows, *arrays):
    if rows == 1:
        return function(*arrays)
    cut = [a.reshape((rows, a.shape[0] // rows) + a.shape[1:]) for a in arrays]
    results = [function(*(c[n] for c in cut)) for n in range(rows)]
    return tuple(jnp.concatenate(group, axis=0) for group in zip(*results))


def dot32(left, right):
    return jnp.dot(left, right, preferred_element_type=jnp.float32)


def whole_row_device(
    inputs,
    memory,
    target_ids,
    memory_ids,
    cotangent,
    w_self_qkv,
    w_self_out,
    w_cross_q,
    w_cross_kv,
    w_cross_out,
    w_up,
    w_down,
    b_up,
    gains,
    shifts,
):
    low = jnp.bfloat16
    x_rows = rows_in(inputs)
    rows, length = x_rows.shape[:2]
    x_flat = x_rows.reshape(-1, D)
    memory_flat = rows_in(memory).reshape(-1, D)
    ids = rows_in(jnp.stack([target_ids, memory_ids], axis=2))
    target_flat = ids[:, :, 0].reshape(-1)
    memory_id_flat = ids[:, :, 1].reshape(-1)
    cot_flat = rows_in(cotangent).reshape(-1, D).astype(jnp.float32)

    qkv_full = gathered(w_self_qkv)
    out_full = gathered(w_self_out)
    cross_q_full = gathered(w_cross_q)
    cross_kv_full = gathered(w_cross_kv)
    cross_out_full = gathered(w_cross_out)
    up_full = gathered(w_up)
    down_full = gathered(w_down)
    small = gathered(jnp.concatenate([gains, shifts], axis=0), 1).astype(jnp.float32)
    gain_full, shift_full = small[:3], small[3:]
    bias_full = gathered(b_up).astype(jnp.float32)

    projected = dot32(x_flat, qkv_full).astype(low)

    def self_forward(rows_proj, rows_ids):
        fq, fk = document_features(rows_ids, rows_ids)
        return attention_forward(rows_proj, 0, rows_proj, 8, 16, fq, fk, True)

    mixed_flat, self_lse = each_row(self_forward, rows, projected, target_flat)
    first_sum = ALPHA * x_flat.astype(jnp.float32) + dot32(mixed_flat, out_full)
    first = layer_norm(first_sum, gain_full[0], shift_full[0])
    first_low = first.astype(low)
    cross_queries = dot32(first_low, cross_q_full).astype(low)
    memory_pairs = dot32(memory_flat, cross_kv_full).astype(low)

    def cross_forward(rows_q, rows_kv, rows_ids, rows_memory_ids):
        fq, fk = document_features(rows_ids, rows_memory_ids)
        return attention_forward(rows_q, 0, rows_kv, 0, 8, fq, fk, False)

    cross_flat, cross_lse = each_row(
        cross_forward, rows, cross_queries, memory_pairs, target_flat, memory_id_flat
    )
    second_sum = ALPHA * first + dot32(cross_flat, cross_out_full)
    second = layer_norm(second_sum, gain_full[1], shift_full[1])
    second_low = second.astype(low)
    hidden_pre = dot32(second_low, up_full) + bias_full
    hidden_low = jax.nn.gelu(hidden_pre).astype(low)
    third_sum = ALPHA * second + dot32(hidden_low, down_full) + shift_full[3]
    result, third_back = jax.vjp(layer_norm, third_sum, gain_full[2], shift_full[2])
    output = rows_out(result.reshape(rows, length, D), low)

    d_third, d_gain_three, d_shift_three = third_back(cot_flat)
    d_branch_three = d_third.astype(low)
    grad_down = shared_out(weight_grad(hidden_low, d_branch_three))
    grad_bias_down = jnp.sum(d_branch_three.astype(jnp.float32), axis=0)
    d_hidden = back_prod(d_branch_three, down_full).astype(low)
    gelu_back = jax.vjp(jax.nn.gelu, hidden_pre)[1]
    d_pre = gelu_back(d_hidden.astype(jnp.float32))[0].astype(low)
    grad_up = shared_out(weight_grad(second_low, d_pre))
    grad_bias_up = shared_out(jnp.sum(d_pre.astype(jnp.float32), axis=0))
    d_second = ALPHA * d_third + back_prod(d_pre, up_full)
    second_back = jax.vjp(layer_norm, second_sum, gain_full[1], shift_full[1])[1]
    d_second_sum, d_gain_two, d_shift_two = second_back(d_second)
    d_branch_two = d_second_sum.astype(low)
    grad_cross_out = shared_out(weight_grad(cross_flat, d_branch_two))
    d_cross = back_prod(d_branch_two, cross_out_full).astype(low)

    def cross_backward(rows_q, rows_kv, rows_ids, rows_memory_ids, mixed, lse, d_mixed):
        fq, fk = document_features(rows_ids, rows_memory_ids)
        return attention_backward(rows_q, 0, rows_kv, 0, 8, fq, fk, mixed, lse, d_mixed, False)

    d_cross_low, d_memory_keys, d_memory_values = each_row(
        cross_backward,
        rows,
        cross_queries,
        memory_pairs,
        target_flat,
        memory_id_flat,
        cross_flat,
        cross_lse,
        d_cross,
    )
    d_memory_pairs = jnp.concatenate([d_memory_keys, d_memory_values], axis=1)
    grad_cross_kv = shared_out(weight_grad(memory_flat, d_memory_pairs))
    d_memory = rows_out(
        back_prod(d_memory_pairs, cross_kv_full).reshape(rows, length, D), jnp.float32
    )
    grad_cross_q = shared_out(weight_grad(first_low, d_cross_low))
    d_first = ALPHA * d_second_sum + back_prod(d_cross_low, cross_q_full)
    first_back = jax.vjp(layer_norm, first_sum, gain_full[0], shift_full[0])[1]
    d_first_sum, d_gain_one, d_shift_one = first_back(d_first)
    d_branch_one = d_first_sum.astype(low)
    grad_self_out = shared_out(weight_grad(mixed_flat, d_branch_one))
    d_self = back_prod(d_branch_one, out_full).astype(low)

    def self_backward(rows_proj, rows_ids, mixed, lse, d_mixed):
        fq, fk = document_features(rows_ids, rows_ids)
        return attention_backward(
            rows_proj, 0, rows_proj, 8, 16, fq, fk, mixed, lse, d_mixed, True
        )

    d_projected = jnp.concatenate(
        each_row(self_backward, rows, projected, target_flat, mixed_flat, self_lse, d_self), axis=1
    )
    grad_self_qkv = shared_out(weight_grad(x_flat, d_projected))
    d_input = rows_out(
        (ALPHA * d_first_sum + back_prod(d_projected, qkv_full)).reshape(rows, length, D),
        jnp.float32,
    )
    grad_rows = jnp.stack(
        [
            d_gain_one,
            d_gain_two,
            d_gain_three,
            d_shift_one,
            d_shift_two,
            d_shift_three,
            grad_bias_down,
        ]
    )
    grad_rows = shared_out(grad_rows, 1)
    return (
        output,
        d_input,
        d_memory,
        grad_self_qkv,
        grad_self_out,
        grad_cross_q,
        grad_cross_kv,
        grad_cross_out,
        grad_up,
        grad_down,
        grad_bias_up,
        grad_rows[:3],
        grad_rows[3:],
    )


def per_device(inputs, *others):
    if inputs.shape[0] % lax.axis_size("blk") == 0:
        return whole_row_device(inputs, *others)
    return split_row_device(inputs, *others)


def solution(mesh):
    return jax.shard_map(
        per_device,
        mesh=mesh,
        in_specs=(
            P("batch", "blk", None),
            P("batch", "blk", None),
            P("batch", "blk"),
            P("batch", "blk"),
            P("batch", "blk", None),
            P("batch", None),
            P("batch", None),
            P("batch", None),
            P("batch", None),
            P("batch", None),
            P("batch", None),
            P("batch", None),
            P("batch"),
            P(None, "batch"),
            P(None, "batch"),
        ),
        out_specs=(
            P("batch", "blk", None),
            P("batch", "blk", None),
            P("batch", "blk", None),
            P("batch", None),
            P("batch", None),
            P("batch", None),
            P("batch", None),
            P("batch", None),
            P("batch", None),
            P("batch", None),
            P("batch"),
            P(None, "batch"),
            P(None, "batch"),
        ),
        check_vma=False,
    )
```

```python
import functools

import jax
import jax.numpy as jnp
from jax import lax
from jax.experimental import pallas as pl
from jax.experimental.pallas import tpu as pltpu
from jax.sharding import PartitionSpec as P

D = 1024
NH = 16
HD = 64
MB_ROWS = 1
MICRO = 2
ALPHA = 300.0**0.25
MASKED = -1e30
EPSILON = 1e-05
PAIR = 2 * HD
BLOCK = 256
MASK_STEP = -(2.0**100)


def nt(left, right):
    return lax.dot_general(left, right, (((1,), (1,)), ((), ())), preferred_element_type=jnp.float32)


def nn(left, right):
    return lax.dot_general(left, right, (((1,), (0,)), ((), ())), preferred_element_type=jnp.float32)


def lane_of(rows):
    return lax.broadcasted_iota(jnp.int32, (rows, PAIR), 1)


def attention_fwd_kernel(causal, q_ref, k_ref, v_ref, fq_ref, fk_ref, out_ref, lse_ref):
    length = q_ref.shape[0]
    mem = k_ref.shape[0]
    low_q = lane_of(length) < HD
    low_k = lane_of(mem) < HD
    q = q_ref[...] * jnp.bfloat16(HD**-0.5)
    k = k_ref[...]
    v = v_ref[...]
    fq = fq_ref[...]
    fk = fk_ref[...]
    ones = jnp.ones_like(v)
    queries = (jnp.where(low_q, q, fq), jnp.where(low_q, fq, q))
    keys = (jnp.where(low_k, k, fk), jnp.where(low_k, fk, k))
    values = (jnp.where(low_k, v, ones), jnp.where(low_k, ones, v))
    low_blk = lane_of(BLOCK) < HD
    for i in range(length // BLOCK):
        seen = (i + 1) * BLOCK if causal else mem
        rows = slice(i * BLOCK, (i + 1) * BLOCK)
        accs, peaks = [], []
        for h in range(2):
            scores = nt(queries[h][rows], keys[h][:seen])
            if causal:
                tri = lax.broadcasted_iota(jnp.int32, (BLOCK, BLOCK), 0) >= lax.broadcasted_iota(
                    jnp.int32, (BLOCK, BLOCK), 1
                )
                diag = jnp.where(tri, scores[:, seen - BLOCK :], MASK_STEP)
                scores = diag if i == 0 else jnp.concatenate([scores[:, : seen - BLOCK], diag], axis=1)
            peak = jnp.max(scores, axis=1, keepdims=True)
            raised = jnp.exp(scores - peak).astype(jnp.bfloat16)
            accs.append(nn(raised, values[h][:seen]))
            peaks.append(peak)
        total = pltpu.roll(jnp.where(low_blk, accs[1], accs[0]), HD, 1)
        out_ref[rows, :] = (jnp.where(low_blk, accs[0], accs[1]) / total).astype(out_ref.dtype)
        lse_ref[rows, :] = jnp.where(low_blk, peaks[0], peaks[1]) + jnp.log(total)


def split3(value):
    hi = value.astype(jnp.bfloat16)
    rest = value - hi.astype(jnp.float32)
    mid = rest.astype(jnp.bfloat16)
    lo = (rest - mid.astype(jnp.float32)).astype(jnp.bfloat16)
    return hi, mid, lo


def placed(lane, start, pieces, other):
    for n, piece in enumerate(pieces):
        other = jnp.where(lane == start + n, piece, other)
    return other


def attention_bwd_kernel(causal, q_ref, k_ref, v_ref, fq_ref, fk_ref, out_ref, lse_ref, do_ref, dq_ref, dk_ref, dv_ref, dk_acc, dv_acc, dq_acc):
    length = q_ref.shape[0]
    mem = k_ref.shape[0]
    lane_q = lane_of(length)
    lane_k = lane_of(mem)
    low_q = lane_q < HD
    low_k = lane_k < HD
    scale = jnp.bfloat16(HD**-0.5)
    q = q_ref[...] * scale
    k = k_ref[...]
    v = v_ref[...]
    do = do_ref[...]
    fq = fq_ref[...]
    fk = fk_ref[...]
    zero_q = jnp.zeros_like(q)
    zero_k = jnp.zeros_like(k)
    one_k = jnp.ones_like(k)
    prod = do.astype(jnp.float32) * out_ref[...].astype(jnp.float32)
    sum_a = jnp.sum(jnp.where(low_q, prod, 0.0), axis=1, keepdims=True)
    sum_b = jnp.sum(jnp.where(low_q, 0.0, prod), axis=1, keepdims=True)
    inner = jnp.where(low_q, sum_b, sum_a)
    lse = pltpu.roll(lse_ref[...], HD, 1)
    half_q = lane_q & (HD - 1)
    half_k = lane_k & (HD - 1)
    fq = placed(half_q, 2, split3(-lse), fq)
    fk = jnp.where((half_k >= 2) & (half_k < 5), one_k, fk)
    fd = placed(half_q, 0, split3(-inner), zero_q)
    fv = jnp.where(half_k < 3, one_k, zero_k)
    queries = (jnp.where(low_q, q, fq), jnp.where(low_q, fq, q))
    keys = (jnp.where(low_k, k, fk), jnp.where(low_k, fk, k))
    grads = (jnp.where(low_q, do, fd), jnp.where(low_q, fd, do))
    values = (jnp.where(low_k, v, fv), jnp.where(low_k, fv, v))
    plain_q = (jnp.where(low_q, q, zero_q), jnp.where(low_q, zero_q, q))
    plain_do = (jnp.where(low_q, do, zero_q), jnp.where(low_q, zero_q, do))
    k_t = k.T
    blocks = length // BLOCK
    for i in range(blocks):
        rows = slice(i * BLOCK, (i + 1) * BLOCK)
        seen = (i + 1) * BLOCK if causal else mem
        probs, d_scores = [], []
        for h in range(2):
            p = jnp.exp(nt(keys[h][:seen], queries[h][rows]))
            if causal:
                tri = lax.broadcasted_iota(jnp.int32, (BLOCK, BLOCK), 0) <= lax.broadcasted_iota(
                    jnp.int32, (BLOCK, BLOCK), 1
                )
                diag = jnp.where(tri, p[seen - BLOCK :], 0.0)
                p = diag if i == 0 else jnp.concatenate([p[: seen - BLOCK], diag], axis=0)
            ds = (p * nt(values[h][:seen], grads[h][rows])).astype(jnp.bfloat16)
            probs.append(p.astype(jnp.bfloat16))
            d_scores.append(ds)
            dq_acc[h * HD : (h + 1) * HD, rows] = nn(k_t[h * HD : (h + 1) * HD, :seen], ds)
        dv = nn(probs[0], plain_do[0][rows]) + nn(probs[1], plain_do[1][rows])
        dk = nn(d_scores[0], plain_q[0][rows]) + nn(d_scores[1], plain_q[1][rows])
        if i == 0:
            dv_acc[:seen] = dv
            dk_acc[:seen] = dk
        elif causal:
            dv_acc[: seen - BLOCK] += dv[: seen - BLOCK]
            dk_acc[: seen - BLOCK] += dk[: seen - BLOCK]
            dv_acc[seen - BLOCK : seen] = dv[seen - BLOCK :]
            dk_acc[seen - BLOCK : seen] = dk[seen - BLOCK :]
        else:
            dv_acc[...] += dv
            dk_acc[...] += dk
    dq_ref[...] = (dq_acc[...].T * (HD**-0.5)).astype(dq_ref.dtype)
    dk_ref[...] = dk_acc[...].astype(dk_ref.dtype)
    dv_ref[...] = dv_acc[...].astype(dv_ref.dtype)


def cols(length, first):
    return pl.BlockSpec((length, PAIR), lambda j: (0, first + j))


def whole(length):
    return pl.BlockSpec((length, PAIR), lambda j: (0, 0))


SHORT = pl.CostEstimate(flops=1024, bytes_accessed=1024, transcendentals=0)


def attention_call(kernel, name, pairs, causal, arrays, shared, outs, scratch, into):
    first, count = pairs
    into = [] if into is None else list(into)

    def body(*refs):
        kernel(causal, *refs[: len(arrays) + 2], *refs[len(arrays) + 2 + len(into) :])

    return pl.pallas_call(
        body,
        grid=(count,),
        in_specs=[cols(a.shape[0], first) for a in arrays[:3]]
        + [whole(a.shape[0]) for a in shared]
        + [cols(a.shape[0], first) for a in arrays[3:]]
        + [pl.BlockSpec(memory_space=pl.ANY)] * len(into),
        out_specs=[cols(o.shape[0], first) for o in outs],
        out_shape=outs,
        scratch_shapes=scratch,
        input_output_aliases={len(arrays) + 2 + n: n for n in range(len(into))},
        compiler_params=pltpu.CompilerParams(vmem_limit_bytes=48 * 2**20),
        cost_estimate=SHORT,
        name=name,
    )(*arrays[:3], *shared, *arrays[3:], *into)


def attention_forward(queries, keys, values, fq, fk, causal, pairs, into):
    length = queries.shape[0]
    outs = [
        jax.ShapeDtypeStruct(queries.shape, jnp.bfloat16),
        jax.ShapeDtypeStruct(queries.shape, jnp.float32),
    ]
    arrays = (queries, keys, values)
    return attention_call(
        attention_fwd_kernel, "attention_forward", pairs, causal, arrays, (fq, fk), outs, [], into
    )


def attention_backward(fq, fk, queries, keys, values, mixed, lse, d_mixed, causal, pairs, into):
    length, mem = queries.shape[0], keys.shape[0]
    outs = [jax.ShapeDtypeStruct(a.shape, jnp.bfloat16) for a in (queries, keys, values)]
    scratch = [
        pltpu.VMEM((mem, PAIR), jnp.float32),
        pltpu.VMEM((mem, PAIR), jnp.float32),
        pltpu.VMEM((PAIR, length), jnp.float32),
    ]
    arrays = (queries, keys, values, mixed, lse, d_mixed)
    return attention_call(
        attention_bwd_kernel,
        "attention_backward",
        pairs,
        causal,
        arrays,
        (fq, fk),
        outs,
        scratch,
        into,
    )


def gelu_kernel(left_ref, right_ref, bias_ref, hidden_ref, slope_ref):
    slope_in = 0.7978845608028654
    right = right_ref[...].reshape(-1, right_ref.shape[-1])
    bias = bias_ref[...]
    step = min(256, left_ref.shape[0])
    for first in range(0, left_ref.shape[0], step):
        rows = slice(first, first + step)
        pre = nn(left_ref[rows, :], right) + bias
        square = pre * pre
        bent = jnp.tanh(slope_in * (pre + 0.044715 * (square * pre)))
        gate = 0.5 * (1.0 + bent)
        hidden_ref[rows, :] = (pre * gate).astype(hidden_ref.dtype)
        bend = (1.0 - bent * bent) * (slope_in + (slope_in * 0.134145) * square)
        slope_ref[rows, :] = gate + (0.5 * pre) * bend


def gelu_rows(left, ffn, bias):
    rows, inner = left.shape
    count, parts, tall_shard, wide = ffn.shape
    columns = wide * parts // 2
    tall = min(rows, 1024)
    return pl.pallas_call(
        gelu_kernel,
        grid=(rows // tall, parts // 2),
        in_specs=[
            pl.BlockSpec((tall, inner), lambda i, j: (i, 0)),
            pl.BlockSpec((count, 1, tall_shard, wide), lambda i, j: (0, j, 0, 0)),
            pl.BlockSpec((1, wide), lambda i, j: (0, j)),
        ],
        out_specs=[pl.BlockSpec((tall, wide), lambda i, j: (i, j))] * 2,
        out_shape=[
            jax.ShapeDtypeStruct((rows, columns), jnp.bfloat16),
            jax.ShapeDtypeStruct((rows, columns), jnp.float32),
        ],
        compiler_params=pltpu.CompilerParams(vmem_limit_bytes=56 * 2**20),
        cost_estimate=SHORT,
        name="gelu_rows",
    )(left, ffn, bias.reshape(1, columns))


def down_kernel(left_ref, right_ref, out_ref):
    right = right_ref[...].reshape(-1, right_ref.shape[-1])
    out_ref[...] = nn(left_ref[...], right)


def down_rows(left, ffn):
    rows, inner = left.shape
    count, parts, tall_shard, columns = ffn.shape
    tall, wide = min(rows, 1024), 256
    return pl.pallas_call(
        down_kernel,
        grid=(rows // tall, columns // wide),
        in_specs=[
            pl.BlockSpec((tall, inner), lambda i, j: (i, 0)),
            pl.BlockSpec((count, parts // 2, tall_shard, wide), lambda i, j: (0, 1, 0, j)),
        ],
        out_specs=pl.BlockSpec((tall, wide), lambda i, j: (i, j)),
        out_shape=jax.ShapeDtypeStruct((rows, columns), jnp.float32),
        compiler_params=pltpu.CompilerParams(vmem_limit_bytes=48 * 2**20),
        cost_estimate=SHORT,
        name="down_rows",
    )(left, ffn)


def up_back_kernel(left_ref, right_ref, out_ref):
    _, parts, _, wide = right_ref.shape
    total = None
    for n in range(parts):
        right = right_ref[:, n].reshape(-1, wide)
        part = nt(left_ref[:, n * wide : (n + 1) * wide], right)
        total = part if total is None else total + part
    out_ref[...] = total


def up_back_rows(left, ffn):
    rows, inner = left.shape
    count, parts, tall_shard, wide = ffn.shape
    tall, group = min(rows, 1024), 4
    return pl.pallas_call(
        up_back_kernel,
        grid=(rows // tall, count // group),
        in_specs=[
            pl.BlockSpec((tall, inner), lambda i, j: (i, 0)),
            pl.BlockSpec((group, parts // 2, tall_shard, wide), lambda i, j: (j, 0, 0, 0)),
        ],
        out_specs=pl.BlockSpec((tall, group * tall_shard), lambda i, j: (i, j)),
        out_shape=jax.ShapeDtypeStruct((rows, count * tall_shard), jnp.float32),
        compiler_params=pltpu.CompilerParams(vmem_limit_bytes=48 * 2**20),
        cost_estimate=SHORT,
        name="up_back_rows",
    )(left, ffn)


def gelu_back_kernel(left_ref, right_ref, slope_ref, out_ref, sum_ref):
    right = right_ref[...].reshape(-1, right_ref.shape[-1])
    step = min(256, left_ref.shape[0])
    total = None
    for first in range(0, left_ref.shape[0], step):
        rows = slice(first, first + step)
        d_hidden = nt(left_ref[rows, :], right).astype(jnp.bfloat16).astype(jnp.float32)
        d_pre = (d_hidden * slope_ref[rows, :]).astype(jnp.bfloat16)
        out_ref[rows, :] = d_pre
        part = jnp.sum(d_pre.astype(jnp.float32), axis=0, keepdims=True)
        total = part if total is None else total + part
    sum_ref[...] = total[None]


def gelu_back_rows(left, ffn, slope):
    rows, inner = left.shape
    count, parts, tall_shard, _ = ffn.shape
    columns = count * parts // 2 * tall_shard
    tall, group = min(rows, 1024), 2
    wide = group * parts // 2 * tall_shard
    out, sums = pl.pallas_call(
        gelu_back_kernel,
        grid=(rows // tall, columns // wide),
        in_specs=[
            pl.BlockSpec((tall, inner), lambda i, j: (i, 0)),
            pl.BlockSpec((group, parts // 2, tall_shard, inner), lambda i, j: (j, 1, 0, 0)),
            pl.BlockSpec((tall, wide), lambda i, j: (i, j)),
        ],
        out_specs=[
            pl.BlockSpec((tall, wide), lambda i, j: (i, j)),
            pl.BlockSpec((1, 1, wide), lambda i, j: (i, 0, j)),
        ],
        out_shape=[
            jax.ShapeDtypeStruct((rows, columns), jnp.bfloat16),
            jax.ShapeDtypeStruct((rows // tall, 1, columns), jnp.float32),
        ],
        compiler_params=pltpu.CompilerParams(vmem_limit_bytes=48 * 2**20),
        cost_estimate=SHORT,
        name="gelu_back_rows",
    )(left, ffn, slope)
    return out, jnp.sum(sums, axis=(0, 1))


def document_features(query_ids, key_ids):
    half = jnp.arange(PAIR, dtype=jnp.int32)[None, :] % HD
    fq = (half == query_ids[:, None]).astype(jnp.bfloat16)
    fk = jnp.where((half < 2) & (half != key_ids[:, None]), MASK_STEP, 0.0).astype(jnp.bfloat16)
    return fq, fk


def shortened(array):
    return jax.tree.map(lambda a: a.astype(jnp.bfloat16) if a.dtype == jnp.float32 else a, array)


def layer_norm(summed, gain_row, shift_row):
    average = jnp.mean(summed, axis=-1, keepdims=True)
    centred = summed - average
    spread = jnp.mean(centred * centred, axis=-1, keepdims=True)
    return centred * lax.rsqrt(spread + EPSILON) * gain_row + shift_row


def split_heads(array_in):
    return array_in.reshape(array_in.shape[0], array_in.shape[1], NH, HD)


def weight_grad(left_rows, right_rows):
    return jnp.einsum("tk,tn->kn", left_rows, right_rows, preferred_element_type=jnp.float32)


def back_prod(grad_rows, matrix):
    return jnp.einsum("tn,kn->tk", grad_rows, matrix, preferred_element_type=jnp.float32)


def attention_scores(queries, key_rows, allowed):
    scores = jnp.einsum(
        "rqhd,rkhd->rhqk",
        split_heads(queries),
        split_heads(key_rows),
        preferred_element_type=jnp.float32,
    ) * HD ** (-0.5)
    return jnp.where(allowed[:, None], scores, MASKED)


def plain_attention_forward(queries, key_rows, value_rows, allowed):
    scores = attention_scores(queries, key_rows, allowed)
    row_peak = jnp.max(scores, axis=-1, keepdims=True)
    raised = jnp.exp(scores - row_peak)
    row_total = jnp.sum(raised, axis=-1, keepdims=True)
    probabilities = (raised / row_total).astype(jnp.bfloat16)
    attended = jnp.einsum(
        "rhqk,rkhd->rqhd",
        probabilities,
        split_heads(value_rows),
        preferred_element_type=jnp.float32,
    )
    return (attended.reshape(queries.shape).astype(jnp.bfloat16), row_peak, row_total)


def plain_attention_backward(queries, key_rows, value_rows, allowed, row_peak, row_total, d_attended):
    scores = attention_scores(queries, key_rows, allowed)
    probabilities = jnp.exp(scores - row_peak) / row_total
    d_heads = split_heads(d_attended)
    d_values = jnp.einsum(
        "rhqk,rqhd->rkhd",
        probabilities.astype(jnp.bfloat16),
        d_heads,
        preferred_element_type=jnp.float32,
    )
    d_probs = jnp.einsum(
        "rqhd,rkhd->rhqk", d_heads, split_heads(value_rows), preferred_element_type=jnp.float32
    )
    inner_sum = jnp.sum(probabilities * d_probs, axis=-1, keepdims=True)
    d_scores = (probabilities * (d_probs - inner_sum)).astype(jnp.bfloat16)
    d_queries = jnp.einsum(
        "rhqk,rkhd->rqhd", d_scores, split_heads(key_rows), preferred_element_type=jnp.float32
    ) * HD ** (-0.5)
    d_keys = jnp.einsum(
        "rhqk,rqhd->rkhd", d_scores, split_heads(queries), preferred_element_type=jnp.float32
    ) * HD ** (-0.5)
    d_pairs = jnp.concatenate(
        [d_keys.reshape(key_rows.shape), d_values.reshape(value_rows.shape)], axis=2
    )
    return (d_queries.reshape(queries.shape), d_pairs)


def add_terms(running, fresh):
    if running is None:
        return fresh
    return tuple((first_term + second_term for first_term, second_term in zip(running, fresh)))


def split_row_device(
    inputs,
    memory,
    target_ids,
    memory_ids,
    cotangent,
    w_self_qkv,
    w_self_out,
    w_cross_q,
    w_cross_kv,
    w_cross_out,
    w_up,
    w_down,
    b_up,
    gains,
    shifts,
):
    tokens_here = inputs.shape[1]
    length = tokens_here * lax.axis_size("blk")
    token_count = MB_ROWS * tokens_here
    query_places = lax.axis_index("blk") * tokens_here + jnp.arange(tokens_here, dtype=jnp.int32)
    key_places = jnp.arange(length, dtype=jnp.int32)
    causal = key_places[None, :] <= query_places[:, None]
    outputs, input_grads, memory_grads = ([], [], [])
    attn_total = None
    ffn_total = None
    for micro_step in range(MICRO):
        row_range = slice(micro_step * MB_ROWS, (micro_step + 1) * MB_ROWS)
        qkv_full, out_full, cross_q_full, cross_kv_full, cross_out_full, gain_low, shift_low = (
            lax.all_gather(w_self_qkv, "batch", axis=0, tiled=True),
            lax.all_gather(w_self_out, "batch", axis=0, tiled=True),
            lax.all_gather(w_cross_q, "batch", axis=0, tiled=True),
            lax.all_gather(w_cross_kv, "batch", axis=0, tiled=True),
            lax.all_gather(w_cross_out, "batch", axis=0, tiled=True),
            lax.all_gather(gains, "batch", axis=1, tiled=True),
            lax.all_gather(shifts, "batch", axis=1, tiled=True),
        )
        gain_full = gain_low.astype(jnp.float32)
        shift_full = shift_low.astype(jnp.float32)
        x_flat = inputs[row_range].reshape(token_count, D)
        memory_flat = memory[row_range].reshape(token_count, D)
        seg_rows = target_ids[row_range]
        memory_seg_rows = memory_ids[row_range]
        projected = (
            jnp.dot(x_flat, qkv_full, preferred_element_type=jnp.float32)
            .astype(jnp.bfloat16)
            .reshape(MB_ROWS, tokens_here, 3 * D)
        )
        self_queries = projected[:, :, :D]
        key_pairs, key_segs = (
            lax.all_gather(projected[:, :, D:], "blk", axis=1, tiled=True),
            lax.all_gather(seg_rows, "blk", axis=1, tiled=True),
        )
        self_allowed = (seg_rows[:, :, None] == key_segs[:, None, :]) & causal[None]
        self_mixed, self_peak, self_total = plain_attention_forward(
            self_queries, key_pairs[:, :, :D], key_pairs[:, :, D:], self_allowed
        )
        mixed_flat = self_mixed.reshape(token_count, D)
        first_sum = ALPHA * x_flat.astype(jnp.float32) + jnp.dot(
            mixed_flat, out_full, preferred_element_type=jnp.float32
        )
        first = layer_norm(first_sum, gain_full[0], shift_full[0])
        first_low = first.astype(jnp.bfloat16)
        cross_queries = (
            jnp.dot(first_low, cross_q_full, preferred_element_type=jnp.float32)
            .astype(jnp.bfloat16)
            .reshape(MB_ROWS, tokens_here, D)
        )
        memory_local = (
            jnp.dot(memory_flat, cross_kv_full, preferred_element_type=jnp.float32)
            .astype(jnp.bfloat16)
            .reshape(MB_ROWS, tokens_here, 2 * D)
        )
        memory_pairs, memory_segs = (
            lax.all_gather(memory_local, "blk", axis=1, tiled=True),
            lax.all_gather(memory_seg_rows, "blk", axis=1, tiled=True),
        )
        cross_allowed = seg_rows[:, :, None] == memory_segs[:, None, :]
        cross_mixed, cross_peak, cross_total = plain_attention_forward(
            cross_queries, memory_pairs[:, :, :D], memory_pairs[:, :, D:], cross_allowed
        )
        cross_flat = cross_mixed.reshape(token_count, D)
        second_sum = ALPHA * first + jnp.dot(
            cross_flat, cross_out_full, preferred_element_type=jnp.float32
        )
        second = layer_norm(second_sum, gain_full[1], shift_full[1])
        second_low = second.astype(jnp.bfloat16)
        up_full, down_full, bias_full = (
            lax.all_gather(w_up, "batch", axis=0, tiled=True),
            lax.all_gather(w_down, "batch", axis=0, tiled=True),
            lax.all_gather(b_up, "batch", axis=0, tiled=True),
        )
        hidden_pre = jnp.dot(
            second_low, up_full, preferred_element_type=jnp.float32
        ) + bias_full.astype(jnp.float32)
        hidden_low = jax.nn.gelu(hidden_pre).astype(jnp.bfloat16)
        third_sum = (
            ALPHA * second
            + jnp.dot(hidden_low, down_full, preferred_element_type=jnp.float32)
            + shift_full[3]
        )
        result, third_back = jax.vjp(layer_norm, third_sum, gain_full[2], shift_full[2])
        outputs.append(result.astype(jnp.bfloat16).reshape(MB_ROWS, tokens_here, D))
        cot_flat = cotangent[row_range].reshape(token_count, D).astype(jnp.float32)
        d_third, d_gain_three, d_shift_three = third_back(cot_flat)
        d_branch_three = d_third.astype(jnp.bfloat16)
        grad_down = weight_grad(hidden_low, d_branch_three)
        grad_bias_down = jnp.sum(d_branch_three.astype(jnp.float32), axis=0)
        d_hidden = back_prod(d_branch_three, down_full).astype(jnp.bfloat16)
        gelu_back = jax.vjp(jax.nn.gelu, hidden_pre)[1]
        d_pre = gelu_back(d_hidden.astype(jnp.float32))[0].astype(jnp.bfloat16)
        grad_up = weight_grad(second_low, d_pre)
        grad_bias_up = jnp.sum(d_pre.astype(jnp.float32), axis=0)
        d_second = ALPHA * d_third + back_prod(d_pre, up_full)
        ffn_terms = (grad_up, grad_down, grad_bias_up)
        ffn_share = (
            lax.psum_scatter(
                ffn_terms[0].astype(jnp.bfloat16), "batch", scatter_dimension=0, tiled=True
            ).astype(jnp.float32),
            lax.psum_scatter(
                ffn_terms[1].astype(jnp.bfloat16), "batch", scatter_dimension=0, tiled=True
            ).astype(jnp.float32),
            lax.psum_scatter(
                ffn_terms[2].astype(jnp.bfloat16), "batch", scatter_dimension=0, tiled=True
            ).astype(jnp.float32),
        )
        ffn_total = add_terms(ffn_total, ffn_share)
        second_back = jax.vjp(layer_norm, second_sum, gain_full[1], shift_full[1])[1]
        d_second_sum, d_gain_two, d_shift_two = second_back(d_second)
        d_branch_two = d_second_sum.astype(jnp.bfloat16)
        grad_cross_out = weight_grad(cross_flat, d_branch_two)
        d_cross = (
            back_prod(d_branch_two, cross_out_full)
            .astype(jnp.bfloat16)
            .reshape(MB_ROWS, tokens_here, D)
        )
        d_cross_queries, d_memory_all = plain_attention_backward(
            cross_queries,
            memory_pairs[:, :, :D],
            memory_pairs[:, :, D:],
            cross_allowed,
            cross_peak,
            cross_total,
            d_cross,
        )
        d_memory_pairs = lax.psum_scatter(
            d_memory_all.astype(jnp.bfloat16), "blk", scatter_dimension=1, tiled=True
        ).reshape(token_count, 2 * D)
        grad_cross_kv = weight_grad(memory_flat, d_memory_pairs)
        memory_grads.append(
            back_prod(d_memory_pairs, cross_kv_full).reshape(MB_ROWS, tokens_here, D)
        )
        d_cross_low = d_cross_queries.astype(jnp.bfloat16).reshape(token_count, D)
        grad_cross_q = weight_grad(first_low, d_cross_low)
        d_first = ALPHA * d_second_sum + back_prod(d_cross_low, cross_q_full)
        first_back = jax.vjp(layer_norm, first_sum, gain_full[0], shift_full[0])[1]
        d_first_sum, d_gain_one, d_shift_one = first_back(d_first)
        d_branch_one = d_first_sum.astype(jnp.bfloat16)
        grad_self_out = weight_grad(mixed_flat, d_branch_one)
        d_self = (
            back_prod(d_branch_one, out_full).astype(jnp.bfloat16).reshape(MB_ROWS, tokens_here, D)
        )
        d_self_queries, d_key_all = plain_attention_backward(
            self_queries,
            key_pairs[:, :, :D],
            key_pairs[:, :, D:],
            self_allowed,
            self_peak,
            self_total,
            d_self,
        )
        d_self_pairs = lax.psum_scatter(
            d_key_all.astype(jnp.bfloat16), "blk", scatter_dimension=1, tiled=True
        )
        d_projected = jnp.concatenate(
            [d_self_queries.astype(jnp.bfloat16), d_self_pairs], axis=2
        ).reshape(token_count, 3 * D)
        grad_self_qkv = weight_grad(x_flat, d_projected)
        input_grads.append(
            (ALPHA * d_first_sum + back_prod(d_projected, qkv_full)).reshape(
                MB_ROWS, tokens_here, D
            )
        )
        grad_gains = jnp.stack([d_gain_one, d_gain_two, d_gain_three])
        grad_shifts = jnp.stack([d_shift_one, d_shift_two, d_shift_three, grad_bias_down])
        attn_terms = (
            grad_self_qkv,
            grad_self_out,
            grad_cross_q,
            grad_cross_kv,
            grad_cross_out,
            grad_gains,
            grad_shifts,
        )
        attn_share = (
            lax.psum_scatter(
                attn_terms[0].astype(jnp.bfloat16), "batch", scatter_dimension=0, tiled=True
            ).astype(jnp.float32),
            lax.psum_scatter(
                attn_terms[1].astype(jnp.bfloat16), "batch", scatter_dimension=0, tiled=True
            ).astype(jnp.float32),
            lax.psum_scatter(
                attn_terms[2].astype(jnp.bfloat16), "batch", scatter_dimension=0, tiled=True
            ).astype(jnp.float32),
            lax.psum_scatter(
                attn_terms[3].astype(jnp.bfloat16), "batch", scatter_dimension=0, tiled=True
            ).astype(jnp.float32),
            lax.psum_scatter(
                attn_terms[4].astype(jnp.bfloat16), "batch", scatter_dimension=0, tiled=True
            ).astype(jnp.float32),
            lax.psum_scatter(
                attn_terms[5].astype(jnp.bfloat16), "batch", scatter_dimension=1, tiled=True
            ).astype(jnp.float32),
            lax.psum_scatter(
                attn_terms[6].astype(jnp.bfloat16), "batch", scatter_dimension=1, tiled=True
            ).astype(jnp.float32),
        )
        attn_total = add_terms(attn_total, attn_share)
    grad_parts = tuple(attn_total) + tuple(ffn_total)
    totals = jax.tree.map(
        lambda part: part.astype(jnp.float32), lax.psum(shortened(grad_parts), "blk")
    )
    output = jnp.concatenate(outputs, axis=0)
    d_input = jnp.concatenate(input_grads, axis=0)
    d_memory = jnp.concatenate(memory_grads, axis=0)
    return (
        output,
        d_input,
        d_memory,
        totals[0],
        totals[1],
        totals[2],
        totals[3],
        totals[4],
        totals[7],
        totals[8],
        totals[9],
        totals[5],
        totals[6],
    )


def swap_pair(array):
    return lax.ppermute(array, "blk", [(0, 1), (1, 0)])


def rows_in(array):
    count = lax.axis_size("blk")
    here = array.shape[0] // count
    parts = array.reshape((count, here) + array.shape[1:])
    if count == 1:
        return parts[0]
    if count == 2:
        me = lax.axis_index("blk")
        kept = lax.dynamic_index_in_dim(parts, me, 0, keepdims=False)
        got = swap_pair(lax.dynamic_index_in_dim(parts, 1 - me, 0, keepdims=False))
        first = jnp.where(me == 0, kept, got)
        second = jnp.where(me == 0, got, kept)
        return jnp.concatenate([first, second], axis=1)
    moved = lax.all_to_all(parts, "blk", 0, 0)
    moved = jnp.moveaxis(moved, 0, 1)
    return moved.reshape((here, count * array.shape[1]) + array.shape[2:])


def rows_out(array, kind):
    count = lax.axis_size("blk")
    here, length = array.shape[:2]
    tokens = length // count
    parts = array.reshape((here, count, tokens) + array.shape[2:])
    if count == 1:
        return parts[:, 0].astype(kind)
    if count == 2:
        me = lax.axis_index("blk")
        kept = lax.dynamic_index_in_dim(parts, me, 1, keepdims=False).astype(kind)
        sent = lax.dynamic_index_in_dim(parts, 1 - me, 1, keepdims=False).astype(jnp.bfloat16)
        got = swap_pair(sent).astype(kind)
        first = jnp.where(me == 0, kept, got)
        second = jnp.where(me == 0, got, kept)
        return jnp.concatenate([first, second], axis=0)
    moved = lax.all_to_all(jnp.moveaxis(parts, 1, 0).astype(jnp.bfloat16), "blk", 0, 0)
    return moved.reshape((count * here, tokens) + array.shape[2:]).astype(kind)


def gathered(shard, axis=0):
    return lax.all_gather(shard, "batch", axis=axis, tiled=True)


def shared_out(grad, axis=0):
    part = lax.psum_scatter(
        grad.astype(jnp.bfloat16), "batch", scatter_dimension=axis, tiled=True
    )
    return lax.psum(part, "blk").astype(jnp.float32)


class Flight:
    def __init__(self, steps):
        self.steps = steps
        self.result = None
        self.wanted = next(steps)
        self.pending = None

    def launch(self):
        self.pending = [send(array) for send, array in self.wanted]

    def advance(self, arrived):
        try:
            self.wanted = self.steps.send(arrived)
        except StopIteration as stop:
            self.wanted, self.result = [], stop.value

    def finish(self):
        while self.result is None:
            if self.pending is None:
                self.launch()
            self.advance(self.pending)
            self.pending = None
        return self.result


def tick(value, *flights):
    flying = [f for f in flights if f.result is None]
    value, arrived = lax.optimization_barrier((value, [f.pending or [] for f in flying]))
    for flight, got in zip(flying, arrived):
        if flight.pending is not None:
            flight.advance(got)
    flying = [f for f in flying if f.result is None]
    value, ready = lax.optimization_barrier((value, [[a for _, a in f.wanted] for f in flying]))
    for flight, arrays in zip(flying, ready):
        flight.wanted = [(send, a) for (send, _), a in zip(flight.wanted, arrays)]
        flight.launch()
    return value


def grid_place():
    batch = lax.axis_index("batch")
    return batch // 4, batch // 2 % 2, batch % 2, lax.axis_index("blk")


def z_sender(step):
    return lambda array: to_z(array, step)


def to_core(array):
    return lax.ppermute(array, "batch", [(n, n ^ 1) for n in range(16)])


def to_x(array):
    return lax.ppermute(array, "batch", [(n, n ^ 2) for n in range(16)])


def to_z(array, step):
    return lax.ppermute(array, "batch", [(n, (n + 4 * step) % 16) for n in range(16)])


def to_core_blk(array):
    pairs = [(2 * n + m, 2 * (n ^ 1) + (1 - m)) for n in range(16) for m in range(2)]
    return lax.ppermute(array, ("batch", "blk"), pairs)


def piece(array, axis, at, size):
    return lax.dynamic_slice_in_dim(array, at * size, size, axis)


def summed_low(terms):
    total = terms[0].astype(jnp.float32)
    for term in terms[1:]:
        total = total + term.astype(jnp.float32)
    return total.astype(jnp.bfloat16)


def in_order(at, own, other, axis):
    first = jnp.where(at == 0, own, other)
    second = jnp.where(at == 0, other, own)
    return jnp.concatenate([first, second], axis=axis)


FLIP = {"x": (0, 1, 0, 0), "c": (0, 0, 1, 0), "y": (0, 0, 0, 1)}
SEND = {"x": to_x, "c": to_core, "y": swap_pair}


def weight_gather(shards, path):
    blk = lax.axis_index("blk")
    if "y" in path:
        shards = [piece(s, 1, blk, s.shape[1] // 2) for s in shards]
    held = [(jnp.concatenate(shards, axis=1)[None], [(0, 0, 0, 0)])]
    return (yield from gather_steps(held, [s.shape for s in shards], path, "y" in path))


def gather_steps(held, shapes, path, split):
    for axis in path:
        if axis == "/":
            (block, labels), count = held[0], (len(shapes) + 1) // 2
            wide = sum(shape[1] for shape in shapes[:count])
            ways = [
                gather_steps([(block[:, :, :wide], labels)], shapes[:count], "yxc", split),
                gather_steps([(block[:, :, wide:], labels)], shapes[count:], "xyc", split),
            ]
            return (yield from together(ways))
        if axis == "z":
            block = jnp.concatenate([a for a, _ in held], axis=0) if len(held) > 1 else held[0][0]
            labels = sum((near for _, near in held), [])
            got = yield [(z_sender(step), block) for step in (1, 2, 3)]
            block = jnp.concatenate([block] + list(got), axis=0)
            held = [(block, [(d, b, c, e) for d in range(4) for _, b, c, e in labels])]
        else:
            got = yield [(SEND[axis], a) for a, _ in held]
            flip = FLIP[axis]
            held = held + [
                (g, [tuple(p + f for p, f in zip(label, flip)) for label in near])
                for g, (_, near) in zip(got, held)
            ]
    return placed_blocks(held, shapes, split)


def together(ways):
    wanted = [next(way) for way in ways]
    results = []
    while not results:
        got = yield sum(wanted, [])
        for n, way in enumerate(ways):
            mine, got = got[: len(wanted[n])], got[len(wanted[n]) :]
            try:
                wanted[n] = way.send(mine)
            except StopIteration as stop:
                results += stop.value
    return results


def place_kernel(near_lists, shapes, split, place, *refs):
    sources, targets = refs[: len(near_lists)], refs[len(near_lists) :]
    for source, near in zip(sources, near_lists):
        for n, (dx, dc, dy) in enumerate(near):
            row = (place[1] + dx) % 2 * 2 + (place[2] + dc) % 2
            first = 0
            for target, (tall, wide) in zip(targets, shapes):
                at = pl.ds(pl.multiple_of(row * tall, tall), tall)
                block = source[n, :, first : first + wide]
                if split:
                    side = (place[3] + dy) % 2
                    target[at, pl.ds(pl.multiple_of(side * wide, wide), wide)] = block
                else:
                    target[at, :] = block
                first += wide


def placed_blocks(held, shapes, split):
    place = jnp.stack(grid_place()).astype(jnp.int32)
    counts = [len(near) // 4 for _, near in held]
    near_lists = [[label[1:] for label in near[:n]] for n, (_, near) in zip(counts, held)]
    outs = [(tall, wide * (2 if split else 1)) for tall, wide in shapes]
    return pl.pallas_call(
        functools.partial(place_kernel, near_lists, shapes, split),
        grid_spec=pltpu.PrefetchScalarGridSpec(
            num_scalar_prefetch=1,
            grid=(4,),
            in_specs=[
                pl.BlockSpec((n,) + a.shape[1:], lambda d, p: (d, 0, 0))
                for n, (a, _) in zip(counts, held)
            ],
            out_specs=[
                pl.BlockSpec((4 * tall, wide), lambda d, p: ((p[0] + 4 - d) % 4, 0))
                for tall, wide in outs
            ],
        ),
        out_shape=[jax.ShapeDtypeStruct((tall * 16, wide), jnp.bfloat16) for tall, wide in outs],
        compiler_params=pltpu.CompilerParams(vmem_limit_bytes=40 * 2**20),
        cost_estimate=SHORT,
        name="place_weights",
    )(place, *[a for a, _ in held])


def halves(terms, axis, at):
    size = terms[0].shape[axis] // 2
    return (
        summed_low([piece(t, axis, 1 - at, size) for t in terms]),
        [piece(t, axis, at, size) for t in terms],
    )


def joined_grads(products, at):
    blocks = []
    for left, rights in products:
        halves_of = [piece(r, 1, at, r.shape[1] // 2) for r in rights]
        right = halves_of[0] if len(rights) == 1 else jnp.concatenate(halves_of, axis=1)
        blocks.append(weight_grad(left, right).astype(jnp.bfloat16))
    return blocks[0] if len(blocks) == 1 else jnp.concatenate(blocks, axis=1)


def gradient_reduce(products, path):
    z, x, core, blk = grid_place()
    given = joined_grads(products, 1 - core)
    kept = joined_grads(products, core)
    (got,) = yield [(to_core, given)]
    rows, columns = kept.shape
    terms = [t.reshape(4, 2, rows // 8, columns) for t in (kept, got)]
    for axis in path:
        if axis == "z":
            out = []
            for step in (1, 2, 3):
                parts = [piece(t, 0, (z + step) % 4, 1) for t in terms]
                out.append((z_sender(step), summed_low(parts)))
            out = yield out
            terms = [piece(t, 0, z, 1) for t in terms] + list(out)
        else:
            out, terms = halves(terms, 1, x) if axis == "x" else halves(terms, 3, blk)
            out = yield [(to_x if axis == "x" else swap_pair, out)]
            terms = terms + list(out)
    total = summed_low(terms).reshape(rows // 8, columns // 2)
    mine = piece(total, 0, core, rows // 16)
    theirs = piece(total, 0, 1 - core, rows // 16)
    from_blk, from_core, from_both = yield [
        (swap_pair, mine),
        (to_core, theirs),
        (to_core_blk, theirs),
    ]
    near = in_order(blk, mine, from_blk, 1).astype(jnp.float32)
    far = in_order(blk, from_core, from_both, 1).astype(jnp.float32)
    left, right = jnp.where(core == 0, near, far), jnp.where(core == 0, far, near)
    results, first = [], 0
    for _, rights in products:
        for wide in [r.shape[1] // 2 for r in rights]:
            part = slice(first, first + wide)
            results.append(jnp.concatenate([left[:, part], right[:, part]], axis=1))
            first += wide
    return results


def over_batch(array):
    return lax.psum_scatter(array, "batch", scatter_dimension=0, tiled=True)


def whole_reduce(products):
    grads = [weight_grad(left, right).astype(jnp.bfloat16) for left, right in products]
    grad = grads[0] if len(grads) == 1 else jnp.concatenate(grads, axis=1)
    if not on_small_slice():
        yield []
        return shared_out(grad)
    (part,) = yield [(over_batch, grad)]
    (got,) = yield [(swap_pair, part)]
    return part.astype(jnp.float32) + got.astype(jnp.float32)


def batch_sender(bit):
    return lambda array: lax.ppermute(array, "batch", [(n, n ^ bit) for n in range(16)])


def total_of_all(array):
    for send in (to_core, to_x, swap_pair, batch_sender(4), batch_sender(8)):
        (got,) = yield [(send, array)]
        array = array + got
    return array


def small_gather(gains, shifts, bias):
    packed = jnp.concatenate([gains, shifts, bias.reshape(-1, gains.shape[1])], axis=0)
    place = jnp.arange(16)[:, None, None] == lax.axis_index("batch")
    held = jnp.where(place, packed[None], jnp.zeros_like(packed)[None])
    for bit in (1, 2, 4, 8):
        (got,) = yield [(batch_sender(bit), held)]
        held = held + got
    rows = jnp.moveaxis(held[:, :7], 0, 1).reshape(7, -1)
    return rows[:3], rows[3:], held[:, 7:].reshape(-1)


def rows_in_steps(array):
    if lax.axis_size("blk") != 2:
        yield []
        return rows_in(array)
    here = array.shape[0] // 2
    parts = array.reshape((2, here) + array.shape[1:])
    me = lax.axis_index("blk")
    (got,) = yield [(swap_pair, lax.dynamic_index_in_dim(parts, 1 - me, 0, keepdims=False))]
    return in_order(me, lax.dynamic_index_in_dim(parts, me, 0, keepdims=False), got, 1)


def rows_out_steps(array, kind):
    if lax.axis_size("blk") != 2:
        yield []
        return rows_out(array, kind)
    here, length = array.shape[:2]
    parts = array.reshape((here, 2, length // 2) + array.shape[2:])
    me = lax.axis_index("blk")
    sent = lax.dynamic_index_in_dim(parts, 1 - me, 1, keepdims=False).astype(jnp.bfloat16)
    (got,) = yield [(swap_pair, sent)]
    kept = lax.dynamic_index_in_dim(parts, me, 1, keepdims=False).astype(kind)
    return in_order(me, kept, got.astype(kind), 0)


def plain_gather(shards):
    yield []
    return [gathered(s) for s in shards]


def plain_small_gather(gains, shifts, bias):
    yield []
    return gathered(gains, 1), gathered(shifts, 1), gathered(bias)


def plain_reduce(products):
    yield []
    return [
        shared_out(weight_grad(left, right)) for left, rights in products for right in rights
    ]


def on_small_slice():
    return lax.axis_size("batch") == 16 and lax.axis_size("blk") == 2


def start_gather(shards, path):
    return Flight(weight_gather(shards, path) if on_small_slice() else plain_gather(shards))


def whole_gather(shard):
    (full,) = yield [(gathered, shard)]
    return [full]


def start_whole_gather(shard):
    return Flight(whole_gather(shard))


def start_reduce(products, path):
    return Flight(gradient_reduce(products, path) if on_small_slice() else plain_reduce(products))


def start_small(gains, shifts, bias):
    steps = small_gather if on_small_slice() else plain_small_gather
    return Flight(steps(gains, shifts, bias))


def small_reduce(rows, bias):
    if not on_small_slice():
        yield []
        return shared_out(rows, 1), shared_out(bias)
    packed = yield from total_of_all(jnp.concatenate([rows, bias.reshape(-1, D)], axis=0))
    me = lax.axis_index("batch")
    bias = packed[rows.shape[0] :].reshape(-1)
    return (
        piece(packed[: rows.shape[0]], 1, me, D // 16),
        piece(bias, 0, me, bias.shape[0] // 16),
    )


def each_row(function, rows, arrays, into=None):
    if rows == 1:
        return function(*arrays, into=into)

    def cut(array, n):
        size = array.shape[0] // rows
        return array[n * size : (n + 1) * size]

    results = []
    for n in range(rows):
        kept = None if into is None else [cut(a, n) for a in into]
        results.append(function(*(cut(a, n) for a in arrays), into=kept))
    return [jnp.concatenate(group, axis=0) for group in zip(*results)]


def dot32(left, right):
    return jnp.dot(left, right, preferred_element_type=jnp.float32)


def whole_row_device(
    inputs,
    memory,
    target_ids,
    memory_ids,
    cotangent,
    w_self_qkv,
    w_self_out,
    w_cross_q,
    w_cross_kv,
    w_cross_out,
    w_up,
    w_down,
    b_up,
    gains,
    shifts,
):
    low = jnp.bfloat16
    half = NH // 4
    shard_rows = w_self_qkv.shape[0]
    columns = [w_self_qkv, w_self_out, w_cross_q, w_cross_kv, w_cross_out]
    columns += [gains.T, shifts.T, b_up.reshape(shard_rows, -1)]
    spare = -sum(c.shape[1] for c in columns) % PAIR
    columns.append(jnp.zeros((shard_rows, spare), low))
    attn_full = gathered(jnp.concatenate(columns, axis=1))
    at, fulls = 0, []
    for wide in [D] * 8 + [c.shape[1] for c in columns[5:8]]:
        fulls.append(attn_full[:, at : at + wide])
        at += wide
    qkv_full, (out_full, cross_q_full, mk_full, mv_full, cross_out_full) = fulls[:3], fulls[3:8]
    gain_full = fulls[8].T.astype(jnp.float32)
    shift_full = fulls[9].T.astype(jnp.float32)
    bias_full = fulls[10].reshape(-1).astype(jnp.float32)
    up_parts = jnp.moveaxis(w_up.reshape(shard_rows, -1, D), 1, 0)
    ffn_shard = jnp.concatenate([up_parts, w_down.reshape(-1, shard_rows, D)], axis=0)
    ffn_full = lax.all_gather(ffn_shard, "batch", axis=0)
    x_rows = Flight(rows_in_steps(inputs))
    ids = Flight(rows_in_steps(jnp.stack([target_ids, memory_ids], axis=2)))
    memory = tick(memory, x_rows, ids)
    memory_rows = Flight(rows_in_steps(memory))
    cotangent = tick(cotangent, x_rows, ids, memory_rows)
    cot_rows = Flight(rows_in_steps(cotangent))
    x_rows = x_rows.finish()
    rows, length = x_rows.shape[:2]
    x_flat = x_rows.reshape(-1, D)
    ids = ids.finish()
    target_flat = ids[:, :, 0].reshape(-1)
    memory_id_flat = ids[:, :, 1].reshape(-1)
    memory_flat = memory_rows.finish().reshape(-1, D)

    def self_forward(q, k, v, id_row, into, pairs):
        fq, fk = document_features(id_row, id_row)
        return attention_forward(q, k, v, fq, fk, True, pairs, into)

    qkv = [dot32(x_flat, w).astype(low) for w in qkv_full]
    mixed_flat, self_lse = each_row(
        functools.partial(self_forward, pairs=(0, 2 * half)), rows, (*qkv, target_flat)
    )
    first_sum = ALPHA * x_flat.astype(jnp.float32) + dot32(mixed_flat, out_full)
    first = layer_norm(first_sum, gain_full[0], shift_full[0])
    first_low = first.astype(low)
    cross_queries = dot32(first_low, cross_q_full).astype(low)
    cross_queries = tick(cross_queries, cot_rows)
    memory_keys = dot32(memory_flat, mk_full).astype(low)
    memory_values = dot32(memory_flat, mv_full).astype(low)

    def cross_forward(q, k, v, id_row, memory_id_row, into, pairs):
        fq, fk = document_features(id_row, memory_id_row)
        return attention_forward(q, k, v, fq, fk, False, pairs, into)

    arrays = (cross_queries, memory_keys, memory_values, target_flat, memory_id_flat)
    mixed = each_row(functools.partial(cross_forward, pairs=(0, 2 * half)), rows, arrays)
    cross_flat, cross_lse = tick(mixed, cot_rows)
    second_sum = ALPHA * first + dot32(cross_flat, cross_out_full)
    second = layer_norm(second_sum, gain_full[1], shift_full[1])
    second_low = second.astype(low)
    hidden_low, slope = gelu_rows(second_low, ffn_full, bias_full)
    cot_flat = cot_rows.finish().reshape(-1, D)
    third_sum = ALPHA * second + down_rows(hidden_low, ffn_full) + shift_full[3]
    result, third_back = jax.vjp(layer_norm, third_sum, gain_full[2], shift_full[2])

    d_third, d_gain_three, d_shift_three = third_back(cot_flat.astype(jnp.float32))
    d_branch_three = d_third.astype(low)
    output = Flight(rows_out_steps(result.reshape(rows, length, D), low))
    down_grad = Flight(whole_reduce([(hidden_low, d_branch_three)]))
    d_branch_three, d_third = tick((d_branch_three, d_third), output, down_grad)
    grad_bias_down = jnp.sum(d_branch_three.astype(jnp.float32), axis=0)
    d_pre, grad_bias_up = gelu_back_rows(d_branch_three, ffn_full, slope)
    up_grad = Flight(whole_reduce([(second_low, d_pre)]))
    d_pre = tick(d_pre, up_grad)
    d_second = ALPHA * d_third + up_back_rows(d_pre, ffn_full)
    second_back = jax.vjp(layer_norm, second_sum, gain_full[1], shift_full[1])[1]
    d_second_sum, d_gain_two, d_shift_two = second_back(d_second)
    d_branch_two = d_second_sum.astype(low)
    d_cross = back_prod(d_branch_two, cross_out_full).astype(low)

    def cross_backward(id_row, memory_id_row, *arrays, into, pairs):
        fq, fk = document_features(id_row, memory_id_row)
        return attention_backward(fq, fk, *arrays, False, pairs, into)

    arrays = (target_flat, memory_id_flat, cross_queries, memory_keys, memory_values)
    arrays += (cross_flat, cross_lse, d_cross)
    grads = each_row(functools.partial(cross_backward, pairs=(0, 2 * half)), rows, arrays)
    d_cross_low, d_memory_keys, d_memory_values = tick(grads, output)
    cross_grad = Flight(
        whole_reduce(
            [
                (memory_flat, d_memory_keys),
                (memory_flat, d_memory_values),
                (first_low, d_cross_low),
                (cross_flat, d_branch_two),
            ]
        )
    )
    d_cross_low = tick(d_cross_low, cross_grad)
    d_first = ALPHA * d_second_sum + back_prod(d_cross_low, cross_q_full)
    first_back = jax.vjp(layer_norm, first_sum, gain_full[0], shift_full[0])[1]
    d_first_sum, d_gain_one, d_shift_one = first_back(d_first)
    d_branch_one = d_first_sum.astype(low)
    grad_rows = [d_gain_one, d_gain_two, d_gain_three]
    grad_rows += [d_shift_one, d_shift_two, d_shift_three, grad_bias_down]
    grad_small = Flight(small_reduce(jnp.stack(grad_rows), grad_bias_up))
    d_self = back_prod(d_branch_one, out_full).astype(low)
    d_self_halves = jnp.split(d_self, 2, axis=1)
    d_self_halves = tick(d_self_halves, grad_small)

    def self_backward(id_row, *arrays, into, pairs):
        fq, fk = document_features(id_row, id_row)
        return attention_backward(fq, fk, *arrays, True, pairs, into)

    halves_of = [jnp.split(a, 2, axis=1) for a in (*qkv, mixed_flat, self_lse)]
    arrays = (target_flat, *[a[0] for a in halves_of], d_self_halves[0])
    grads_a = each_row(functools.partial(self_backward, pairs=(0, half)), rows, arrays)
    d_memory = back_prod(d_memory_keys, mk_full) + back_prod(d_memory_values, mv_full)
    d_memory = Flight(rows_out_steps(d_memory.reshape(rows, length, D), jnp.float32))
    grads_a, d_self_b = tick((grads_a, d_self_halves[1]), grad_small)
    early_grad = start_reduce([(x_flat, grads_a), (mixed_flat, [d_branch_one])], "xyz")
    d_self_b = tick(d_self_b, grad_small, early_grad, d_memory)
    arrays = (target_flat, *[a[1] for a in halves_of], d_self_b)
    grads_b = each_row(functools.partial(self_backward, pairs=(0, half)), rows, arrays)
    grads_b = tick(grads_b, grad_small, early_grad, d_memory)
    late_grad = start_reduce([(x_flat, grads_b)], "xyz")
    grads_b = tick(grads_b, grad_small, late_grad)
    d_input = ALPHA * d_first_sum
    for grad_a, grad_b, weight in zip(grads_a, grads_b, qkv_full):
        d_input = d_input + back_prod(jnp.concatenate([grad_a, grad_b], axis=1), weight)
    d_input = Flight(rows_out_steps(d_input.reshape(rows, length, D), jnp.float32))
    flights = [late_grad, early_grad, grad_small, d_memory, d_input, down_grad, up_grad]
    token = grad_bias_up
    for _ in range(3):
        token = tick(token, *flights)
    flights.append(cross_grad)
    while any(f.result is None for f in flights):
        token = tick(token, *flights)
    grad_rows, grad_bias_up = grad_small.finish()
    grad_kv, grad_cross_q, grad_cross_out = jnp.split(cross_grad.finish(), [2 * D, 3 * D], axis=1)
    grad_qa, grad_ka, grad_va, grad_self_out = early_grad.finish()
    grad_qb, grad_kb, grad_vb = late_grad.finish()
    return (
        output.finish(),
        d_input.finish(),
        d_memory.finish(),
        jnp.concatenate([grad_qa, grad_qb, grad_ka, grad_kb, grad_va, grad_vb], axis=1),
        grad_self_out,
        grad_cross_q,
        grad_kv,
        grad_cross_out,
        up_grad.finish(),
        down_grad.finish(),
        grad_bias_up,
        grad_rows[:3],
        grad_rows[3:],
    )


def per_device(inputs, *others):
    if inputs.shape[0] % lax.axis_size("blk") == 0:
        return whole_row_device(inputs, *others)
    return split_row_device(inputs, *others)


def solution(mesh):
    return jax.shard_map(
        per_device,
        mesh=mesh,
        in_specs=(
            P("batch", "blk", None),
            P("batch", "blk", None),
            P("batch", "blk"),
            P("batch", "blk"),
            P("batch", "blk", None),
            P("batch", None),
            P("batch", None),
            P("batch", None),
            P("batch", None),
            P("batch", None),
            P("batch", None),
            P("batch", None),
            P("batch"),
            P(None, "batch"),
            P(None, "batch"),
        ),
        out_specs=(
            P("batch", "blk", None),
            P("batch", "blk", None),
            P("batch", "blk", None),
            P("batch", None),
            P("batch", None),
            P("batch", None),
            P("batch", None),
            P("batch", None),
            P("batch", None),
            P("batch", None),
            P("batch"),
            P(None, "batch"),
            P(None, "batch"),
        ),
        check_vma=False,
    )
```

```python
import functools

import jax
import jax.numpy as jnp
from jax import lax
from jax.experimental import pallas as pl
from jax.experimental.pallas import tpu as pltpu
from jax.sharding import PartitionSpec as P

D = 1024
NH = 16
HD = 64
MB_ROWS = 1
MICRO = 2
ALPHA = 300.0**0.25
MASKED = -1e30
EPSILON = 1e-05
PAIR = 2 * HD
MASK_STEP = -(2.0**100)


def nt(left, right):
    return lax.dot_general(left, right, (((1,), (1,)), ((), ())), preferred_element_type=jnp.float32)


def nn(left, right):
    return lax.dot_general(left, right, (((1,), (0,)), ((), ())), preferred_element_type=jnp.float32)


def lane_of(rows):
    return lax.broadcasted_iota(jnp.int32, (rows, PAIR), 1)


def attention_fwd_kernel(causal, q_ref, k_ref, v_ref, fq_ref, fk_ref, out_ref, lse_ref):
    block = 256
    length = q_ref.shape[0]
    mem = k_ref.shape[0]
    low_q = lane_of(length) < HD
    low_k = lane_of(mem) < HD
    q = q_ref[...] * jnp.bfloat16(HD**-0.5)
    k = k_ref[...]
    v = v_ref[...]
    fq = fq_ref[...]
    fk = fk_ref[...]
    ones = jnp.ones_like(v)
    queries = (jnp.where(low_q, q, fq), jnp.where(low_q, fq, q))
    keys = (jnp.where(low_k, k, fk), jnp.where(low_k, fk, k))
    values = (jnp.where(low_k, v, ones), jnp.where(low_k, ones, v))
    low_blk = lane_of(block) < HD
    units = [(i, h) for i in range(length // block) for h in range(2)]

    def score(unit):
        i, h = unit
        seen = (i + 1) * block if causal else mem
        scores = nt(queries[h][i * block : (i + 1) * block], keys[h][:seen])
        if causal:
            tri = lax.broadcasted_iota(jnp.int32, (block, block), 0) >= lax.broadcasted_iota(
                jnp.int32, (block, block), 1
            )
            diag = jnp.where(tri, scores[:, seen - block :], MASK_STEP)
            scores = diag if i == 0 else jnp.concatenate([scores[:, : seen - block], diag], axis=1)
        return scores

    ahead = score(units[0])
    accs, peaks = [], []
    for n, (i, h) in enumerate(units):
        rows = slice(i * block, (i + 1) * block)
        scores = ahead
        if n + 1 < len(units):
            ahead = score(units[n + 1])
        peak = jnp.max(scores, axis=1, keepdims=True)
        raised = jnp.exp(scores - peak).astype(jnp.bfloat16)
        accs.append(nn(raised, values[h][: scores.shape[1]]))
        peaks.append(peak)
        if h == 1:
            total = pltpu.roll(jnp.where(low_blk, accs[1], accs[0]), HD, 1)
            out_ref[rows, :] = (jnp.where(low_blk, accs[0], accs[1]) / total).astype(out_ref.dtype)
            lse_ref[rows, :] = jnp.where(low_blk, peaks[0], peaks[1]) + jnp.log(total)
            accs, peaks = [], []


def split3(value):
    hi = value.astype(jnp.bfloat16)
    rest = value - hi.astype(jnp.float32)
    mid = rest.astype(jnp.bfloat16)
    lo = (rest - mid.astype(jnp.float32)).astype(jnp.bfloat16)
    return hi, mid, lo


def placed(lane, start, pieces, other):
    for n, piece in enumerate(pieces):
        other = jnp.where(lane == start + n, piece, other)
    return other


def attention_bwd_kernel(causal, q_ref, k_ref, v_ref, fq_ref, fk_ref, out_ref, lse_ref, do_ref, dq_ref, dk_ref, dv_ref, dk_acc, dv_acc, dq_acc):
    block = 256 if causal else 512
    length = q_ref.shape[0]
    mem = k_ref.shape[0]
    lane_q = lane_of(length)
    lane_k = lane_of(mem)
    low_q = lane_q < HD
    low_k = lane_k < HD
    scale = jnp.bfloat16(HD**-0.5)
    q = q_ref[...] * scale
    k = k_ref[...]
    v = v_ref[...]
    do = do_ref[...]
    fq = fq_ref[...]
    fk = fk_ref[...]
    zero_q = jnp.zeros_like(q)
    zero_k = jnp.zeros_like(k)
    one_k = jnp.ones_like(k)
    prod = do.astype(jnp.float32) * out_ref[...].astype(jnp.float32)
    sum_a = jnp.sum(jnp.where(low_q, prod, 0.0), axis=1, keepdims=True)
    sum_b = jnp.sum(jnp.where(low_q, 0.0, prod), axis=1, keepdims=True)
    inner = jnp.where(low_q, sum_b, sum_a)
    lse = pltpu.roll(lse_ref[...], HD, 1)
    half_q = lane_q & (HD - 1)
    half_k = lane_k & (HD - 1)
    fq = placed(half_q, 2, split3(-lse), fq)
    fk = jnp.where((half_k >= 2) & (half_k < 5), one_k, fk)
    fd = placed(half_q, 0, split3(-inner), zero_q)
    fv = jnp.where(half_k < 3, one_k, zero_k)
    queries = (jnp.where(low_q, q, fq), jnp.where(low_q, fq, q))
    keys = (jnp.where(low_k, k, fk), jnp.where(low_k, fk, k))
    grads = (jnp.where(low_q, do, fd), jnp.where(low_q, fd, do))
    values = (jnp.where(low_k, v, fv), jnp.where(low_k, fv, v))
    plain_q = (jnp.where(low_q, q, zero_q), jnp.where(low_q, zero_q, q))
    plain_do = (jnp.where(low_q, do, zero_q), jnp.where(low_q, zero_q, do))
    k_t = k.T
    units = [(i, h) for i in range(length // block) for h in range(2)]

    def scores_of(unit):
        i, h = unit
        rows = slice(i * block, (i + 1) * block)
        seen = (i + 1) * block if causal else mem
        return nt(keys[h][:seen], queries[h][rows]), nt(values[h][:seen], grads[h][rows])

    ahead = scores_of(units[0])
    dv = dk = None
    for n, (i, h) in enumerate(units):
        rows = slice(i * block, (i + 1) * block)
        seen = (i + 1) * block if causal else mem
        s, dp = ahead
        if n + 1 < len(units):
            ahead = scores_of(units[n + 1])
        p = jnp.exp(s)
        if causal:
            tri = lax.broadcasted_iota(jnp.int32, (block, block), 0) <= lax.broadcasted_iota(
                jnp.int32, (block, block), 1
            )
            diag = jnp.where(tri, p[seen - block :], 0.0)
            p = diag if i == 0 else jnp.concatenate([p[: seen - block], diag], axis=0)
        ds = (p * dp).astype(jnp.bfloat16)
        dq_acc[h * HD : (h + 1) * HD, rows] = nn(k_t[h * HD : (h + 1) * HD, :seen], ds)
        dv_part = nn(p.astype(jnp.bfloat16), plain_do[h][rows])
        dk_part = nn(ds, plain_q[h][rows])
        if n == 0:
            dv_acc[:seen] = dv_part
            dk_acc[:seen] = dk_part
            if seen < mem:
                dv_acc[seen:] = jnp.zeros((mem - seen, PAIR), jnp.float32)
                dk_acc[seen:] = jnp.zeros((mem - seen, PAIR), jnp.float32)
        else:
            dv_acc[:seen] += dv_part
            dk_acc[:seen] += dk_part
    dq_ref[...] = (dq_acc[...].T * (HD**-0.5)).astype(dq_ref.dtype)
    dk_ref[...] = dk_acc[...].astype(dk_ref.dtype)
    dv_ref[...] = dv_acc[...].astype(dv_ref.dtype)


def cols(length, first):
    return pl.BlockSpec((length, PAIR), lambda j: (0, first + j))


def whole(length):
    return pl.BlockSpec((length, PAIR), lambda j: (0, 0))


SHORT = pl.CostEstimate(flops=1024, bytes_accessed=1024, transcendentals=0)


def attention_call(kernel, name, pairs, causal, arrays, shared, lengths, kinds, scratch):
    first, count = pairs

    return pl.pallas_call(
        functools.partial(kernel, causal),
        grid=(count,),
        in_specs=[cols(a.shape[0], first) for a in arrays[:3]]
        + [whole(a.shape[0]) for a in shared]
        + [cols(a.shape[0], first) for a in arrays[3:]],
        out_specs=[cols(n, 0) for n in lengths],
        out_shape=[
            jax.ShapeDtypeStruct((n, count * PAIR), kind) for n, kind in zip(lengths, kinds)
        ],
        scratch_shapes=scratch,
        compiler_params=pltpu.CompilerParams(vmem_limit_bytes=48 * 2**20),
        cost_estimate=SHORT,
        name=name,
    )(*arrays[:3], *shared, *arrays[3:])


def attention_forward(queries, keys, values, fq, fk, causal, pairs):
    lengths = (queries.shape[0],) * 2
    kinds = (jnp.bfloat16, jnp.float32)
    arrays, shared = (queries, keys, values), (fq, fk)
    return attention_call(
        attention_fwd_kernel, "attention_forward", pairs, causal, arrays, shared, lengths, kinds, []
    )


def attention_backward(fq, fk, queries, keys, values, mixed, lse, d_mixed, causal, pairs):
    length, mem = queries.shape[0], keys.shape[0]
    scratch = [
        pltpu.VMEM((mem, PAIR), jnp.float32),
        pltpu.VMEM((mem, PAIR), jnp.float32),
        pltpu.VMEM((PAIR, length), jnp.float32),
    ]
    return attention_call(
        attention_bwd_kernel,
        "attention_backward",
        pairs,
        causal,
        (queries, keys, values, mixed, lse, d_mixed),
        (fq, fk),
        (length, mem, mem),
        (jnp.bfloat16,) * 3,
        scratch,
    )


def gelu_kernel(left_ref, right_ref, bias_ref, hidden_ref, slope_ref):
    slope_in = 0.7978845608028654
    right = right_ref[...].reshape(-1, right_ref.shape[-1])
    bias = bias_ref[...]
    step = min(256, left_ref.shape[0])
    for first in range(0, left_ref.shape[0], step):
        rows = slice(first, first + step)
        pre = nn(left_ref[rows, :], right) + bias
        square = pre * pre
        bent = jnp.tanh(slope_in * (pre + 0.044715 * (square * pre)))
        gate = 0.5 * (1.0 + bent)
        hidden_ref[rows, :] = (pre * gate).astype(hidden_ref.dtype)
        bend = (1.0 - bent * bent) * (slope_in + (slope_in * 0.134145) * square)
        slope_ref[rows, :] = gate + (0.5 * pre) * bend


def gelu_rows(left, ffn, bias):
    rows, inner = left.shape
    count, wide = ffn.shape[0], ffn.shape[2]
    tall_shard = inner // count
    columns = bias.shape[0]
    tall = min(rows, 1024)
    return pl.pallas_call(
        gelu_kernel,
        grid=(rows // tall, columns // wide),
        in_specs=[
            pl.BlockSpec((tall, inner), lambda i, j: (i, 0)),
            pl.BlockSpec((count, tall_shard, wide), lambda i, j: (0, j, 0)),
            pl.BlockSpec((1, wide), lambda i, j: (0, j)),
        ],
        out_specs=[pl.BlockSpec((tall, wide), lambda i, j: (i, j))] * 2,
        out_shape=[
            jax.ShapeDtypeStruct((rows, columns), jnp.bfloat16),
            jax.ShapeDtypeStruct((rows, columns), jnp.float32),
        ],
        compiler_params=pltpu.CompilerParams(vmem_limit_bytes=56 * 2**20),
        cost_estimate=SHORT,
        name="gelu_rows",
    )(left, ffn, bias.reshape(1, columns))


def down_kernel(left_ref, right_ref, out_ref):
    right = right_ref[...].reshape(-1, right_ref.shape[-1])
    out_ref[...] = nn(left_ref[...], right)


def down_rows(left, ffn):
    rows, inner = left.shape
    count, columns = ffn.shape[0], ffn.shape[2]
    tall, wide = min(rows, 1024), 256
    return pl.pallas_call(
        down_kernel,
        grid=(rows // tall, columns // wide),
        in_specs=[
            pl.BlockSpec((tall, inner), lambda i, j: (i, 0)),
            pl.BlockSpec((count, inner // count, wide), lambda i, j: (0, 1, j)),
        ],
        out_specs=pl.BlockSpec((tall, wide), lambda i, j: (i, j)),
        out_shape=jax.ShapeDtypeStruct((rows, columns), jnp.float32),
        compiler_params=pltpu.CompilerParams(vmem_limit_bytes=48 * 2**20),
        cost_estimate=SHORT,
        name="down_rows",
    )(left, ffn)


def up_back_kernel(left_ref, right_ref, out_ref):
    wide = right_ref.shape[2]
    tall_shard = out_ref.shape[1] // right_ref.shape[0]
    total = None
    for n in range(right_ref.shape[1] // tall_shard):
        right = right_ref[:, n * tall_shard : (n + 1) * tall_shard].reshape(-1, wide)
        part = nt(left_ref[:, n * wide : (n + 1) * wide], right)
        total = part if total is None else total + part
    out_ref[...] = total


def up_back_rows(left, ffn):
    rows, inner = left.shape
    count, wide = ffn.shape[0], ffn.shape[2]
    tall_shard = D // count
    tall, group = min(rows, 1024), 4
    return pl.pallas_call(
        up_back_kernel,
        grid=(rows // tall, count // group),
        in_specs=[
            pl.BlockSpec((tall, inner), lambda i, j: (i, 0)),
            pl.BlockSpec((group, inner // wide * tall_shard, wide), lambda i, j: (j, 0, 0)),
        ],
        out_specs=pl.BlockSpec((tall, group * tall_shard), lambda i, j: (i, j)),
        out_shape=jax.ShapeDtypeStruct((rows, count * tall_shard), jnp.float32),
        compiler_params=pltpu.CompilerParams(vmem_limit_bytes=48 * 2**20),
        cost_estimate=SHORT,
        name="up_back_rows",
    )(left, ffn)


def gelu_back_kernel(left_ref, right_ref, slope_ref, out_ref, sum_ref):
    right = right_ref[...].reshape(-1, right_ref.shape[-1])
    step = min(512, left_ref.shape[0])
    total = None
    for first in range(0, left_ref.shape[0], step):
        rows = slice(first, first + step)
        d_hidden = nt(left_ref[rows, :], right).astype(jnp.bfloat16).astype(jnp.float32)
        d_pre = (d_hidden * slope_ref[rows, :]).astype(jnp.bfloat16)
        out_ref[rows, :] = d_pre
        part = jnp.sum(d_pre.astype(jnp.float32), axis=0, keepdims=True)
        total = part if total is None else total + part
    sum_ref[...] = total[None]


def gelu_back_rows(left, ffn, slope):
    rows, inner = left.shape
    count, columns = ffn.shape[0], slope.shape[1]
    tall, group = min(rows, 1024), 4
    wide = columns // count * group
    out, sums = pl.pallas_call(
        gelu_back_kernel,
        grid=(rows // tall, columns // wide),
        in_specs=[
            pl.BlockSpec((tall, inner), lambda i, j: (i, 0)),
            pl.BlockSpec((group, columns // count, inner), lambda i, j: (j, 1, 0)),
            pl.BlockSpec((tall, wide), lambda i, j: (i, j)),
        ],
        out_specs=[
            pl.BlockSpec((tall, wide), lambda i, j: (i, j)),
            pl.BlockSpec((1, 1, wide), lambda i, j: (i, 0, j)),
        ],
        out_shape=[
            jax.ShapeDtypeStruct((rows, columns), jnp.bfloat16),
            jax.ShapeDtypeStruct((rows // tall, 1, columns), jnp.float32),
        ],
        compiler_params=pltpu.CompilerParams(vmem_limit_bytes=48 * 2**20),
        cost_estimate=SHORT,
        name="gelu_back_rows",
    )(left, ffn, slope)
    return out, jnp.sum(sums, axis=(0, 1))


def document_features(query_ids, key_ids):
    half = jnp.arange(PAIR, dtype=jnp.int32)[None, :] % HD
    fq = (half == query_ids[:, None]).astype(jnp.bfloat16)
    fk = jnp.where((half < 2) & (half != key_ids[:, None]), MASK_STEP, 0.0).astype(jnp.bfloat16)
    return fq, fk


def shortened(array):
    return jax.tree.map(lambda a: a.astype(jnp.bfloat16) if a.dtype == jnp.float32 else a, array)


def layer_norm(summed, gain_row, shift_row):
    average = jnp.mean(summed, axis=-1, keepdims=True)
    centred = summed - average
    spread = jnp.mean(centred * centred, axis=-1, keepdims=True)
    return centred * lax.rsqrt(spread + EPSILON) * gain_row + shift_row


def split_heads(array_in):
    return array_in.reshape(array_in.shape[0], array_in.shape[1], NH, HD)


def weight_grad(left_rows, right_rows):
    return jnp.einsum("tk,tn->kn", left_rows, right_rows, preferred_element_type=jnp.float32)


def back_prod(grad_rows, matrix):
    return jnp.einsum("tn,kn->tk", grad_rows, matrix, preferred_element_type=jnp.float32)


def attention_scores(queries, key_rows, allowed):
    scores = jnp.einsum(
        "rqhd,rkhd->rhqk",
        split_heads(queries),
        split_heads(key_rows),
        preferred_element_type=jnp.float32,
    ) * HD ** (-0.5)
    return jnp.where(allowed[:, None], scores, MASKED)


def plain_attention_forward(queries, key_rows, value_rows, allowed):
    scores = attention_scores(queries, key_rows, allowed)
    row_peak = jnp.max(scores, axis=-1, keepdims=True)
    raised = jnp.exp(scores - row_peak)
    row_total = jnp.sum(raised, axis=-1, keepdims=True)
    probabilities = (raised / row_total).astype(jnp.bfloat16)
    attended = jnp.einsum(
        "rhqk,rkhd->rqhd",
        probabilities,
        split_heads(value_rows),
        preferred_element_type=jnp.float32,
    )
    return (attended.reshape(queries.shape).astype(jnp.bfloat16), row_peak, row_total)


def plain_attention_backward(queries, key_rows, value_rows, allowed, row_peak, row_total, d_attended):
    scores = attention_scores(queries, key_rows, allowed)
    probabilities = jnp.exp(scores - row_peak) / row_total
    d_heads = split_heads(d_attended)
    d_values = jnp.einsum(
        "rhqk,rqhd->rkhd",
        probabilities.astype(jnp.bfloat16),
        d_heads,
        preferred_element_type=jnp.float32,
    )
    d_probs = jnp.einsum(
        "rqhd,rkhd->rhqk", d_heads, split_heads(value_rows), preferred_element_type=jnp.float32
    )
    inner_sum = jnp.sum(probabilities * d_probs, axis=-1, keepdims=True)
    d_scores = (probabilities * (d_probs - inner_sum)).astype(jnp.bfloat16)
    d_queries = jnp.einsum(
        "rhqk,rkhd->rqhd", d_scores, split_heads(key_rows), preferred_element_type=jnp.float32
    ) * HD ** (-0.5)
    d_keys = jnp.einsum(
        "rhqk,rqhd->rkhd", d_scores, split_heads(queries), preferred_element_type=jnp.float32
    ) * HD ** (-0.5)
    d_pairs = jnp.concatenate(
        [d_keys.reshape(key_rows.shape), d_values.reshape(value_rows.shape)], axis=2
    )
    return (d_queries.reshape(queries.shape), d_pairs)


def add_terms(running, fresh):
    if running is None:
        return fresh
    return tuple((first_term + second_term for first_term, second_term in zip(running, fresh)))


def split_row_device(
    inputs,
    memory,
    target_ids,
    memory_ids,
    cotangent,
    w_self_qkv,
    w_self_out,
    w_cross_q,
    w_cross_kv,
    w_cross_out,
    w_up,
    w_down,
    b_up,
    gains,
    shifts,
):
    tokens_here = inputs.shape[1]
    length = tokens_here * lax.axis_size("blk")
    token_count = MB_ROWS * tokens_here
    query_places = lax.axis_index("blk") * tokens_here + jnp.arange(tokens_here, dtype=jnp.int32)
    key_places = jnp.arange(length, dtype=jnp.int32)
    causal = key_places[None, :] <= query_places[:, None]
    outputs, input_grads, memory_grads = ([], [], [])
    attn_total = None
    ffn_total = None
    for micro_step in range(MICRO):
        row_range = slice(micro_step * MB_ROWS, (micro_step + 1) * MB_ROWS)
        qkv_full, out_full, cross_q_full, cross_kv_full, cross_out_full, gain_low, shift_low = (
            lax.all_gather(w_self_qkv, "batch", axis=0, tiled=True),
            lax.all_gather(w_self_out, "batch", axis=0, tiled=True),
            lax.all_gather(w_cross_q, "batch", axis=0, tiled=True),
            lax.all_gather(w_cross_kv, "batch", axis=0, tiled=True),
            lax.all_gather(w_cross_out, "batch", axis=0, tiled=True),
            lax.all_gather(gains, "batch", axis=1, tiled=True),
            lax.all_gather(shifts, "batch", axis=1, tiled=True),
        )
        gain_full = gain_low.astype(jnp.float32)
        shift_full = shift_low.astype(jnp.float32)
        x_flat = inputs[row_range].reshape(token_count, D)
        memory_flat = memory[row_range].reshape(token_count, D)
        seg_rows = target_ids[row_range]
        memory_seg_rows = memory_ids[row_range]
        projected = (
            jnp.dot(x_flat, qkv_full, preferred_element_type=jnp.float32)
            .astype(jnp.bfloat16)
            .reshape(MB_ROWS, tokens_here, 3 * D)
        )
        self_queries = projected[:, :, :D]
        key_pairs, key_segs = (
            lax.all_gather(projected[:, :, D:], "blk", axis=1, tiled=True),
            lax.all_gather(seg_rows, "blk", axis=1, tiled=True),
        )
        self_allowed = (seg_rows[:, :, None] == key_segs[:, None, :]) & causal[None]
        self_mixed, self_peak, self_total = plain_attention_forward(
            self_queries, key_pairs[:, :, :D], key_pairs[:, :, D:], self_allowed
        )
        mixed_flat = self_mixed.reshape(token_count, D)
        first_sum = ALPHA * x_flat.astype(jnp.float32) + jnp.dot(
            mixed_flat, out_full, preferred_element_type=jnp.float32
        )
        first = layer_norm(first_sum, gain_full[0], shift_full[0])
        first_low = first.astype(jnp.bfloat16)
        cross_queries = (
            jnp.dot(first_low, cross_q_full, preferred_element_type=jnp.float32)
            .astype(jnp.bfloat16)
            .reshape(MB_ROWS, tokens_here, D)
        )
        memory_local = (
            jnp.dot(memory_flat, cross_kv_full, preferred_element_type=jnp.float32)
            .astype(jnp.bfloat16)
            .reshape(MB_ROWS, tokens_here, 2 * D)
        )
        memory_pairs, memory_segs = (
            lax.all_gather(memory_local, "blk", axis=1, tiled=True),
            lax.all_gather(memory_seg_rows, "blk", axis=1, tiled=True),
        )
        cross_allowed = seg_rows[:, :, None] == memory_segs[:, None, :]
        cross_mixed, cross_peak, cross_total = plain_attention_forward(
            cross_queries, memory_pairs[:, :, :D], memory_pairs[:, :, D:], cross_allowed
        )
        cross_flat = cross_mixed.reshape(token_count, D)
        second_sum = ALPHA * first + jnp.dot(
            cross_flat, cross_out_full, preferred_element_type=jnp.float32
        )
        second = layer_norm(second_sum, gain_full[1], shift_full[1])
        second_low = second.astype(jnp.bfloat16)
        up_full, down_full, bias_full = (
            lax.all_gather(w_up, "batch", axis=0, tiled=True),
            lax.all_gather(w_down, "batch", axis=0, tiled=True),
            lax.all_gather(b_up, "batch", axis=0, tiled=True),
        )
        hidden_pre = jnp.dot(
            second_low, up_full, preferred_element_type=jnp.float32
        ) + bias_full.astype(jnp.float32)
        hidden_low = jax.nn.gelu(hidden_pre).astype(jnp.bfloat16)
        third_sum = (
            ALPHA * second
            + jnp.dot(hidden_low, down_full, preferred_element_type=jnp.float32)
            + shift_full[3]
        )
        result, third_back = jax.vjp(layer_norm, third_sum, gain_full[2], shift_full[2])
        outputs.append(result.astype(jnp.bfloat16).reshape(MB_ROWS, tokens_here, D))
        cot_flat = cotangent[row_range].reshape(token_count, D).astype(jnp.float32)
        d_third, d_gain_three, d_shift_three = third_back(cot_flat)
        d_branch_three = d_third.astype(jnp.bfloat16)
        grad_down = weight_grad(hidden_low, d_branch_three)
        grad_bias_down = jnp.sum(d_branch_three.astype(jnp.float32), axis=0)
        d_hidden = back_prod(d_branch_three, down_full).astype(jnp.bfloat16)
        gelu_back = jax.vjp(jax.nn.gelu, hidden_pre)[1]
        d_pre = gelu_back(d_hidden.astype(jnp.float32))[0].astype(jnp.bfloat16)
        grad_up = weight_grad(second_low, d_pre)
        grad_bias_up = jnp.sum(d_pre.astype(jnp.float32), axis=0)
        d_second = ALPHA * d_third + back_prod(d_pre, up_full)
        ffn_terms = (grad_up, grad_down, grad_bias_up)
        ffn_share = (
            lax.psum_scatter(
                ffn_terms[0].astype(jnp.bfloat16), "batch", scatter_dimension=0, tiled=True
            ).astype(jnp.float32),
            lax.psum_scatter(
                ffn_terms[1].astype(jnp.bfloat16), "batch", scatter_dimension=0, tiled=True
            ).astype(jnp.float32),
            lax.psum_scatter(
                ffn_terms[2].astype(jnp.bfloat16), "batch", scatter_dimension=0, tiled=True
            ).astype(jnp.float32),
        )
        ffn_total = add_terms(ffn_total, ffn_share)
        second_back = jax.vjp(layer_norm, second_sum, gain_full[1], shift_full[1])[1]
        d_second_sum, d_gain_two, d_shift_two = second_back(d_second)
        d_branch_two = d_second_sum.astype(jnp.bfloat16)
        grad_cross_out = weight_grad(cross_flat, d_branch_two)
        d_cross = (
            back_prod(d_branch_two, cross_out_full)
            .astype(jnp.bfloat16)
            .reshape(MB_ROWS, tokens_here, D)
        )
        d_cross_queries, d_memory_all = plain_attention_backward(
            cross_queries,
            memory_pairs[:, :, :D],
            memory_pairs[:, :, D:],
            cross_allowed,
            cross_peak,
            cross_total,
            d_cross,
        )
        d_memory_pairs = lax.psum_scatter(
            d_memory_all.astype(jnp.bfloat16), "blk", scatter_dimension=1, tiled=True
        ).reshape(token_count, 2 * D)
        grad_cross_kv = weight_grad(memory_flat, d_memory_pairs)
        memory_grads.append(
            back_prod(d_memory_pairs, cross_kv_full).reshape(MB_ROWS, tokens_here, D)
        )
        d_cross_low = d_cross_queries.astype(jnp.bfloat16).reshape(token_count, D)
        grad_cross_q = weight_grad(first_low, d_cross_low)
        d_first = ALPHA * d_second_sum + back_prod(d_cross_low, cross_q_full)
        first_back = jax.vjp(layer_norm, first_sum, gain_full[0], shift_full[0])[1]
        d_first_sum, d_gain_one, d_shift_one = first_back(d_first)
        d_branch_one = d_first_sum.astype(jnp.bfloat16)
        grad_self_out = weight_grad(mixed_flat, d_branch_one)
        d_self = (
            back_prod(d_branch_one, out_full).astype(jnp.bfloat16).reshape(MB_ROWS, tokens_here, D)
        )
        d_self_queries, d_key_all = plain_attention_backward(
            self_queries,
            key_pairs[:, :, :D],
            key_pairs[:, :, D:],
            self_allowed,
            self_peak,
            self_total,
            d_self,
        )
        d_self_pairs = lax.psum_scatter(
            d_key_all.astype(jnp.bfloat16), "blk", scatter_dimension=1, tiled=True
        )
        d_projected = jnp.concatenate(
            [d_self_queries.astype(jnp.bfloat16), d_self_pairs], axis=2
        ).reshape(token_count, 3 * D)
        grad_self_qkv = weight_grad(x_flat, d_projected)
        input_grads.append(
            (ALPHA * d_first_sum + back_prod(d_projected, qkv_full)).reshape(
                MB_ROWS, tokens_here, D
            )
        )
        grad_gains = jnp.stack([d_gain_one, d_gain_two, d_gain_three])
        grad_shifts = jnp.stack([d_shift_one, d_shift_two, d_shift_three, grad_bias_down])
        attn_terms = (
            grad_self_qkv,
            grad_self_out,
            grad_cross_q,
            grad_cross_kv,
            grad_cross_out,
            grad_gains,
            grad_shifts,
        )
        attn_share = (
            lax.psum_scatter(
                attn_terms[0].astype(jnp.bfloat16), "batch", scatter_dimension=0, tiled=True
            ).astype(jnp.float32),
            lax.psum_scatter(
                attn_terms[1].astype(jnp.bfloat16), "batch", scatter_dimension=0, tiled=True
            ).astype(jnp.float32),
            lax.psum_scatter(
                attn_terms[2].astype(jnp.bfloat16), "batch", scatter_dimension=0, tiled=True
            ).astype(jnp.float32),
            lax.psum_scatter(
                attn_terms[3].astype(jnp.bfloat16), "batch", scatter_dimension=0, tiled=True
            ).astype(jnp.float32),
            lax.psum_scatter(
                attn_terms[4].astype(jnp.bfloat16), "batch", scatter_dimension=0, tiled=True
            ).astype(jnp.float32),
            lax.psum_scatter(
                attn_terms[5].astype(jnp.bfloat16), "batch", scatter_dimension=1, tiled=True
            ).astype(jnp.float32),
            lax.psum_scatter(
                attn_terms[6].astype(jnp.bfloat16), "batch", scatter_dimension=1, tiled=True
            ).astype(jnp.float32),
        )
        attn_total = add_terms(attn_total, attn_share)
    grad_parts = tuple(attn_total) + tuple(ffn_total)
    totals = jax.tree.map(
        lambda part: part.astype(jnp.float32), lax.psum(shortened(grad_parts), "blk")
    )
    output = jnp.concatenate(outputs, axis=0)
    d_input = jnp.concatenate(input_grads, axis=0)
    d_memory = jnp.concatenate(memory_grads, axis=0)
    return (
        output,
        d_input,
        d_memory,
        totals[0],
        totals[1],
        totals[2],
        totals[3],
        totals[4],
        totals[7],
        totals[8],
        totals[9],
        totals[5],
        totals[6],
    )


def swap_pair(array):
    return lax.ppermute(array, "blk", [(0, 1), (1, 0)])


def rows_in(array):
    count = lax.axis_size("blk")
    here = array.shape[0] // count
    parts = array.reshape((count, here) + array.shape[1:])
    if count == 1:
        return parts[0]
    if count == 2:
        me = lax.axis_index("blk")
        kept = lax.dynamic_index_in_dim(parts, me, 0, keepdims=False)
        got = swap_pair(lax.dynamic_index_in_dim(parts, 1 - me, 0, keepdims=False))
        first = jnp.where(me == 0, kept, got)
        second = jnp.where(me == 0, got, kept)
        return jnp.concatenate([first, second], axis=1)
    moved = lax.all_to_all(parts, "blk", 0, 0)
    moved = jnp.moveaxis(moved, 0, 1)
    return moved.reshape((here, count * array.shape[1]) + array.shape[2:])


def rows_out(array, kind):
    count = lax.axis_size("blk")
    here, length = array.shape[:2]
    tokens = length // count
    parts = array.reshape((here, count, tokens) + array.shape[2:])
    if count == 1:
        return parts[:, 0].astype(kind)
    if count == 2:
        me = lax.axis_index("blk")
        kept = lax.dynamic_index_in_dim(parts, me, 1, keepdims=False).astype(kind)
        sent = lax.dynamic_index_in_dim(parts, 1 - me, 1, keepdims=False).astype(jnp.bfloat16)
        got = swap_pair(sent).astype(kind)
        first = jnp.where(me == 0, kept, got)
        second = jnp.where(me == 0, got, kept)
        return jnp.concatenate([first, second], axis=0)
    moved = lax.all_to_all(jnp.moveaxis(parts, 1, 0).astype(jnp.bfloat16), "blk", 0, 0)
    return moved.reshape((count * here, tokens) + array.shape[2:]).astype(kind)


def gathered(shard, axis=0):
    return lax.all_gather(shard, "batch", axis=axis, tiled=True)


def shared_out(grad, axis=0):
    part = lax.psum_scatter(
        grad.astype(jnp.bfloat16), "batch", scatter_dimension=axis, tiled=True
    )
    return lax.psum(part, "blk").astype(jnp.float32)


class Flight:
    def __init__(self, steps):
        self.steps = steps
        self.result = None
        self.wanted = next(steps)
        self.pending = None

    def launch(self):
        self.pending = [send(array) for send, array in self.wanted]

    def advance(self, arrived):
        try:
            self.wanted = self.steps.send(arrived)
        except StopIteration as stop:
            self.wanted, self.result = [], stop.value

    def finish(self):
        while self.result is None:
            if self.pending is None:
                self.launch()
            self.advance(self.pending)
            self.pending = None
        return self.result


def tick(value, *flights):
    flying = [f for f in flights if f.result is None]
    value, arrived = lax.optimization_barrier((value, [f.pending or [] for f in flying]))
    for flight, got in zip(flying, arrived):
        if flight.pending is not None:
            flight.advance(got)
    flying = [f for f in flying if f.result is None]
    value, ready = lax.optimization_barrier((value, [[a for _, a in f.wanted] for f in flying]))
    for flight, arrays in zip(flying, ready):
        flight.wanted = [(send, a) for (send, _), a in zip(flight.wanted, arrays)]
        flight.launch()
    return value


def grid_place():
    batch = lax.axis_index("batch")
    return batch // 4, batch // 2 % 2, batch % 2, lax.axis_index("blk")


def z_sender(step):
    return lambda array: to_z(array, step)


def to_core(array):
    return lax.ppermute(array, "batch", [(n, n ^ 1) for n in range(16)])


def to_x(array):
    return lax.ppermute(array, "batch", [(n, n ^ 2) for n in range(16)])


def to_z(array, step):
    return lax.ppermute(array, "batch", [(n, (n + 4 * step) % 16) for n in range(16)])


def to_core_blk(array):
    pairs = [(2 * n + m, 2 * (n ^ 1) + (1 - m)) for n in range(16) for m in range(2)]
    return lax.ppermute(array, ("batch", "blk"), pairs)


def piece(array, axis, at, size):
    return lax.dynamic_slice_in_dim(array, at * size, size, axis)


def summed_low(terms):
    total = terms[0].astype(jnp.float32)
    for term in terms[1:]:
        total = total + term.astype(jnp.float32)
    return total.astype(jnp.bfloat16)


def in_order(at, own, other, axis):
    first = jnp.where(at == 0, own, other)
    second = jnp.where(at == 0, other, own)
    return jnp.concatenate([first, second], axis=axis)


FLIP = {"x": (0, 1, 0, 0), "c": (0, 0, 1, 0), "y": (0, 0, 0, 1)}
SEND = {"x": to_x, "c": to_core, "y": swap_pair}


def weight_gather(shards, path):
    blk = lax.axis_index("blk")
    if "y" in path:
        shards = [piece(s, 1, blk, s.shape[1] // 2) for s in shards]
    held = [(jnp.concatenate(shards, axis=1)[None], [(0, 0, 0, 0)])]
    return (yield from gather_steps(held, [s.shape for s in shards], path, "y" in path))


def gather_steps(held, shapes, path, split):
    for axis in path:
        if axis == "/":
            (block, labels), count = held[0], (len(shapes) + 1) // 2
            wide = sum(shape[1] for shape in shapes[:count])
            ways = [
                gather_steps([(block[:, :, :wide], labels)], shapes[:count], "yxc", split),
                gather_steps([(block[:, :, wide:], labels)], shapes[count:], "xyc", split),
            ]
            return (yield from together(ways))
        if axis == "z":
            block = jnp.concatenate([a for a, _ in held], axis=0) if len(held) > 1 else held[0][0]
            labels = sum((near for _, near in held), [])
            got = yield [(z_sender(step), block) for step in (1, 2, 3)]
            block = jnp.concatenate([block] + list(got), axis=0)
            held = [(block, [(d, b, c, e) for d in range(4) for _, b, c, e in labels])]
        else:
            got = yield [(SEND[axis], a) for a, _ in held]
            flip = FLIP[axis]
            held = held + [
                (g, [tuple(p + f for p, f in zip(label, flip)) for label in near])
                for g, (_, near) in zip(got, held)
            ]
    return placed_blocks(held, shapes, split)


def together(ways):
    wanted = [next(way) for way in ways]
    results = []
    while not results:
        got = yield sum(wanted, [])
        for n, way in enumerate(ways):
            mine, got = got[: len(wanted[n])], got[len(wanted[n]) :]
            try:
                wanted[n] = way.send(mine)
            except StopIteration as stop:
                results += stop.value
    return results


def place_kernel(near_lists, shapes, split, place, *refs):
    sources, targets = refs[: len(near_lists)], refs[len(near_lists) :]
    for source, near in zip(sources, near_lists):
        for n, (dx, dc, dy) in enumerate(near):
            row = (place[1] + dx) % 2 * 2 + (place[2] + dc) % 2
            first = 0
            for target, (tall, wide) in zip(targets, shapes):
                at = pl.ds(pl.multiple_of(row * tall, tall), tall)
                block = source[n, :, first : first + wide]
                if split:
                    side = (place[3] + dy) % 2
                    target[at, pl.ds(pl.multiple_of(side * wide, wide), wide)] = block
                else:
                    target[at, :] = block
                first += wide


def placed_blocks(held, shapes, split):
    place = jnp.stack(grid_place()).astype(jnp.int32)
    counts = [len(near) // 4 for _, near in held]
    near_lists = [[label[1:] for label in near[:n]] for n, (_, near) in zip(counts, held)]
    outs = [(tall, wide * (2 if split else 1)) for tall, wide in shapes]
    return pl.pallas_call(
        functools.partial(place_kernel, near_lists, shapes, split),
        grid_spec=pltpu.PrefetchScalarGridSpec(
            num_scalar_prefetch=1,
            grid=(4,),
            in_specs=[
                pl.BlockSpec((n,) + a.shape[1:], lambda d, p: (d, 0, 0))
                for n, (a, _) in zip(counts, held)
            ],
            out_specs=[
                pl.BlockSpec((4 * tall, wide), lambda d, p: ((p[0] + 4 - d) % 4, 0))
                for tall, wide in outs
            ],
        ),
        out_shape=[jax.ShapeDtypeStruct((tall * 16, wide), jnp.bfloat16) for tall, wide in outs],
        compiler_params=pltpu.CompilerParams(vmem_limit_bytes=40 * 2**20),
        cost_estimate=SHORT,
        name="place_weights",
    )(place, *[a for a, _ in held])


def halves(terms, axis, at):
    size = terms[0].shape[axis] // 2
    return (
        summed_low([piece(t, axis, 1 - at, size) for t in terms]),
        [piece(t, axis, at, size) for t in terms],
    )


def grads_kernel(plan, halved, *refs):
    lefts = 1 + max(p[0] for p in plan)
    rights = 1 + max(p[1] for p in plan)
    outs = refs[-4 - (2 if halved else 1) : -4]
    extra = refs[lefts + rights : -4 - len(outs)]
    left_buf, right_buf, out_buf, sems = refs[-4:]
    core = lax.axis_index("batch") % 2

    def loads(n):
        left, right, first, wide = plan[n]
        copies = []
        if n == 0 or plan[n - 1][0] != left:
            slot = left % 2
            copies.append(pltpu.make_async_copy(refs[left], left_buf.at[slot], sems.at[0, slot]))
        source = refs[lefts + right].at[:, pl.ds(first, wide)]
        target = right_buf.at[n % 2, :, pl.ds(0, wide)]
        copies.append(pltpu.make_async_copy(source, target, sems.at[1, n % 2]))
        return copies

    def stores(n):
        wide = plan[n][3]
        at = sum(p[3] for p in plan[:n])
        held = out_buf.at[n % 2]
        if not halved:
            place = outs[0].at[:, pl.ds(at, wide)]
            return [pltpu.make_async_copy(held.at[:, pl.ds(0, wide)], place, sems.at[2, n % 2])]
        copies = []
        for side, out in enumerate(outs):
            first = pl.multiple_of((core + 1 - side) % 2 * (wide // 2), wide // 2)
            place = out.at[:, pl.ds(at // 2, wide // 2)]
            source = held.at[:, pl.ds(first, wide // 2)]
            copies.append(pltpu.make_async_copy(source, place, sems.at[2 + side, n % 2]))
        return copies

    for copy in loads(0):
        copy.start()
    if extra:
        wide = extra[0].shape[1]
        held = out_buf.at[0, :, pl.ds(0, wide)]
        place = outs[0].at[:, pl.ds(sum(p[3] for p in plan), wide)]
        for source, target in ((extra[0], held), (held, place)):
            copy = pltpu.make_async_copy(source, target, sems.at[3, 0])
            copy.start()
            copy.wait()
    for n, (left, _, _, wide) in enumerate(plan):
        if n + 1 < len(plan):
            for copy in loads(n + 1):
                copy.start()
        for copy in loads(n):
            copy.wait()
        if n >= 2:
            for copy in stores(n - 2):
                copy.wait()
        grad = lax.dot_general(
            left_buf[left % 2],
            right_buf[n % 2, :, :wide],
            (((0,), (0,)), ((), ())),
            preferred_element_type=jnp.float32,
        )
        out_buf[n % 2, :, :wide] = grad.astype(out_buf.dtype)
        for copy in stores(n):
            copy.start()
    for n in range(max(0, len(plan) - 2), len(plan)):
        for copy in stores(n):
            copy.wait()


def joined_grads(products, halved, extra=()):
    lefts, rights, plan = [], [], []
    for left, group in products:
        lefts.append(left)
        for right in group:
            rights.append(right)
            wide = min(right.shape[1], D)
            for first in range(0, right.shape[1], wide):
                plan.append((len(lefts) - 1, len(rights) - 1, first, wide))
    tokens, rows = lefts[0].shape
    total = sum(p[3] for p in plan) + sum(e.shape[1] for e in extra)
    shape = jax.ShapeDtypeStruct((rows, total // 2 if halved else total), jnp.bfloat16)
    anywhere = pl.BlockSpec(memory_space=pl.ANY)
    widest = max(p[3] for p in plan)
    return pl.pallas_call(
        functools.partial(grads_kernel, plan, halved),
        in_specs=[anywhere] * (len(lefts) + len(rights) + len(extra)),
        out_specs=[anywhere] * (2 if halved else 1),
        out_shape=[shape] * (2 if halved else 1),
        scratch_shapes=[
            pltpu.VMEM((2, tokens, rows), jnp.bfloat16),
            pltpu.VMEM((2, tokens, widest), jnp.bfloat16),
            pltpu.VMEM((2, rows, widest), jnp.bfloat16),
            pltpu.SemaphoreType.DMA((4, 2)),
        ],
        compiler_params=pltpu.CompilerParams(vmem_limit_bytes=48 * 2**20),
        cost_estimate=SHORT,
        name="joined_grads",
    )(*lefts, *rights, *extra)


def gradient_reduce(products, path):
    z, x, core, blk = grid_place()
    given, kept = joined_grads(products, True)
    (got,) = yield [(to_core, given)]
    rows, columns = kept.shape
    terms = [t.reshape(4, 2, rows // 8, columns) for t in (kept, got)]
    for axis in path:
        if axis == "z":
            out = []
            for step in (1, 2, 3):
                parts = [piece(t, 0, (z + step) % 4, 1) for t in terms]
                out.append((z_sender(step), summed_low(parts)))
            out = yield out
            terms = [piece(t, 0, z, 1) for t in terms] + list(out)
        else:
            out, terms = halves(terms, 1, x) if axis == "x" else halves(terms, 3, blk)
            out = yield [(to_x if axis == "x" else swap_pair, out)]
            terms = terms + list(out)
    total = summed_low(terms).reshape(rows // 8, columns // 2)
    mine = piece(total, 0, core, rows // 16)
    theirs = piece(total, 0, 1 - core, rows // 16)
    from_blk, from_core, from_both = yield [
        (swap_pair, mine),
        (to_core, theirs),
        (to_core_blk, theirs),
    ]
    near = in_order(blk, mine, from_blk, 1).astype(jnp.float32)
    far = in_order(blk, from_core, from_both, 1).astype(jnp.float32)
    left, right = jnp.where(core == 0, near, far), jnp.where(core == 0, far, near)
    results, first = [], 0
    for _, rights in products:
        for whole_wide in [r.shape[1] for r in rights]:
            blocks = []
            for _ in range(0, whole_wide, min(whole_wide, D)):
                wide = min(whole_wide, D) // 2
                blocks += [left[:, first : first + wide], right[:, first : first + wide]]
                first += wide
            results.append(jnp.concatenate(blocks, axis=1))
    return results


def over_batch(array):
    return lax.psum_scatter(array, "batch", scatter_dimension=0, tiled=True)


def whole_reduce(products, small=None):
    if not on_small_slice():
        yield []
        grads = [shared_out(weight_grad(left, r)) for left, rights in products for r in rights]
        grad = jnp.concatenate(grads, axis=1)
        return grad if small is None else (grad, shared_out(small[0], 1), shared_out(small[1]))
    extra = ()
    if small is not None:
        columns = jnp.concatenate([small[0].T, small[1].reshape(D, -1)], axis=1)
        columns = jnp.pad(columns, ((0, 0), (0, PAIR - columns.shape[1])))
        extra = (columns.astype(jnp.bfloat16),)
    if len(products) == 1:
        grad = weight_grad(products[0][0], products[0][1][0]).astype(jnp.bfloat16)
    else:
        (grad,) = joined_grads(products, False, extra)
    (part,) = yield [(over_batch, grad)]
    (got,) = yield [(swap_pair, part)]
    total = part.astype(jnp.float32) + got.astype(jnp.float32)
    if small is None:
        return total
    total, columns, count = total[:, :-PAIR], total[:, -PAIR:], small[0].shape[0]
    bias = columns[:, count : count + small[1].shape[0] // D]
    return total, columns[:, :count].T, bias.reshape(-1)


def batch_sender(bit):
    return lambda array: lax.ppermute(array, "batch", [(n, n ^ bit) for n in range(16)])


def total_of_all(array):
    for send in (to_core, to_x, swap_pair, batch_sender(4), batch_sender(8)):
        (got,) = yield [(send, array)]
        array = array + got
    return array


def small_gather(gains, shifts, bias):
    packed = jnp.concatenate([gains, shifts, bias.reshape(-1, gains.shape[1])], axis=0)
    place = jnp.arange(16)[:, None, None] == lax.axis_index("batch")
    held = jnp.where(place, packed[None], jnp.zeros_like(packed)[None])
    for bit in (1, 2, 4, 8):
        (got,) = yield [(batch_sender(bit), held)]
        held = held + got
    rows = jnp.moveaxis(held[:, :7], 0, 1).reshape(7, -1)
    return rows[:3], rows[3:], held[:, 7:].reshape(-1)


def rows_in_steps(array):
    if lax.axis_size("blk") != 2:
        yield []
        return rows_in(array)
    here = array.shape[0] // 2
    parts = array.reshape((2, here) + array.shape[1:])
    me = lax.axis_index("blk")
    (got,) = yield [(swap_pair, lax.dynamic_index_in_dim(parts, 1 - me, 0, keepdims=False))]
    return in_order(me, lax.dynamic_index_in_dim(parts, me, 0, keepdims=False), got, 1)


def rows_out_steps(array, kind):
    if lax.axis_size("blk") != 2:
        yield []
        return rows_out(array, kind)
    here, length = array.shape[:2]
    parts = array.reshape((here, 2, length // 2) + array.shape[2:])
    me = lax.axis_index("blk")
    sent = lax.dynamic_index_in_dim(parts, 1 - me, 1, keepdims=False).astype(jnp.bfloat16)
    (got,) = yield [(swap_pair, sent)]
    kept = lax.dynamic_index_in_dim(parts, me, 1, keepdims=False).astype(kind)
    return in_order(me, kept, got.astype(kind), 0)


def plain_gather(shards):
    yield []
    return [gathered(s) for s in shards]


def plain_small_gather(gains, shifts, bias):
    yield []
    return gathered(gains, 1), gathered(shifts, 1), gathered(bias)


def plain_reduce(products):
    yield []
    return [
        shared_out(weight_grad(left, right)) for left, rights in products for right in rights
    ]


def on_small_slice():
    return lax.axis_size("batch") == 16 and lax.axis_size("blk") == 2


def start_gather(shards, path):
    return Flight(weight_gather(shards, path) if on_small_slice() else plain_gather(shards))


def whole_gather(shard):
    (full,) = yield [(gathered, shard)]
    return [full]


def start_whole_gather(shard):
    return Flight(whole_gather(shard))


def start_reduce(products, path):
    return Flight(gradient_reduce(products, path) if on_small_slice() else plain_reduce(products))


def start_small(gains, shifts, bias):
    steps = small_gather if on_small_slice() else plain_small_gather
    return Flight(steps(gains, shifts, bias))


def small_reduce(rows, bias):
    if not on_small_slice():
        yield []
        return shared_out(rows, 1), shared_out(bias)
    packed = yield from total_of_all(jnp.concatenate([rows, bias.reshape(-1, D)], axis=0))
    me = lax.axis_index("batch")
    bias = packed[rows.shape[0] :].reshape(-1)
    return (
        piece(packed[: rows.shape[0]], 1, me, D // 16),
        piece(bias, 0, me, bias.shape[0] // 16),
    )


def each_row(function, rows, arrays):
    if rows == 1:
        return function(*arrays)

    def cut(array, n):
        size = array.shape[0] // rows
        return array[n * size : (n + 1) * size]

    results = [function(*(cut(a, n) for a in arrays)) for n in range(rows)]
    return [jnp.concatenate(group, axis=0) for group in zip(*results)]


def dot32(left, right):
    return jnp.dot(left, right, preferred_element_type=jnp.float32)


def whole_row_device(
    inputs,
    memory,
    target_ids,
    memory_ids,
    cotangent,
    w_self_qkv,
    w_self_out,
    w_cross_q,
    w_cross_kv,
    w_cross_out,
    w_up,
    w_down,
    b_up,
    gains,
    shifts,
):
    low = jnp.bfloat16
    half = NH // 4
    shard_rows = w_self_qkv.shape[0]
    columns = [w_self_qkv, w_self_out, w_cross_q, w_cross_kv, w_cross_out]
    columns += [gains.T, shifts.T, b_up.reshape(shard_rows, -1)]
    spare = -sum(c.shape[1] for c in columns) % PAIR
    columns.append(jnp.zeros((shard_rows, spare), low))
    attn_full = gathered(jnp.concatenate(columns, axis=1))
    at, fulls = 0, []
    for wide in [D] * 8 + [c.shape[1] for c in columns[5:8]]:
        fulls.append(attn_full[:, at : at + wide])
        at += wide
    qkv_full, (out_full, cross_q_full, mk_full, mv_full, cross_out_full) = fulls[:3], fulls[3:8]
    gain_full = fulls[8].T.astype(jnp.float32)
    shift_full = fulls[9].T.astype(jnp.float32)
    bias_full = fulls[10].reshape(-1).astype(jnp.float32)
    up_parts = [w_up[:, n : n + D] for n in range(0, w_up.shape[1], D)]
    ffn_shard = jnp.concatenate(up_parts + [w_down, jnp.zeros((8, D), low)], axis=0)
    ffn_full = lax.all_gather(ffn_shard, "batch", axis=0)
    x_rows = Flight(rows_in_steps(inputs))
    ids = Flight(rows_in_steps(jnp.stack([target_ids, memory_ids], axis=2)))
    memory = tick(memory, x_rows, ids)
    memory_rows = Flight(rows_in_steps(memory))
    cotangent = tick(cotangent, x_rows, ids, memory_rows)
    cot_rows = Flight(rows_in_steps(cotangent))
    x_rows = x_rows.finish()
    rows, length = x_rows.shape[:2]
    x_flat = x_rows.reshape(-1, D)
    ids = ids.finish()
    target_flat = ids[:, :, 0].reshape(-1)
    memory_id_flat = ids[:, :, 1].reshape(-1)
    memory_flat = memory_rows.finish().reshape(-1, D)

    def self_forward(q, k, v, id_row, pairs):
        fq, fk = document_features(id_row, id_row)
        return attention_forward(q, k, v, fq, fk, True, pairs)

    qkv = [dot32(x_flat, w).astype(low) for w in qkv_full]
    mixed_flat, self_lse = each_row(
        functools.partial(self_forward, pairs=(0, 2 * half)), rows, (*qkv, target_flat)
    )
    first_sum = ALPHA * x_flat.astype(jnp.float32) + dot32(mixed_flat, out_full)
    first = layer_norm(first_sum, gain_full[0], shift_full[0])
    first_low = first.astype(low)
    cross_queries = dot32(first_low, cross_q_full).astype(low)
    cross_queries = tick(cross_queries, cot_rows)
    memory_keys = dot32(memory_flat, mk_full).astype(low)
    memory_values = dot32(memory_flat, mv_full).astype(low)

    def cross_forward(q, k, v, id_row, memory_id_row, pairs):
        fq, fk = document_features(id_row, memory_id_row)
        return attention_forward(q, k, v, fq, fk, False, pairs)

    arrays = (cross_queries, memory_keys, memory_values, target_flat, memory_id_flat)
    mixed = each_row(functools.partial(cross_forward, pairs=(0, 2 * half)), rows, arrays)
    cross_flat, cross_lse = tick(mixed, cot_rows)
    second_sum = ALPHA * first + dot32(cross_flat, cross_out_full)
    second = layer_norm(second_sum, gain_full[1], shift_full[1])
    second_low = second.astype(low)
    hidden_low, slope = gelu_rows(second_low, ffn_full, bias_full)
    cot_flat = cot_rows.finish().reshape(-1, D)
    third_sum = ALPHA * second + down_rows(hidden_low, ffn_full) + shift_full[3]
    result, third_back = jax.vjp(layer_norm, third_sum, gain_full[2], shift_full[2])

    d_third, d_gain_three, d_shift_three = third_back(cot_flat.astype(jnp.float32))
    d_branch_three = d_third.astype(low)
    output = Flight(rows_out_steps(result.reshape(rows, length, D), low))
    down_grad = Flight(whole_reduce([(hidden_low, [d_branch_three])]))
    d_branch_three, d_third = tick((d_branch_three, d_third), output, down_grad)
    grad_bias_down = jnp.sum(d_branch_three.astype(jnp.float32), axis=0)
    d_pre, grad_bias_up = gelu_back_rows(d_branch_three, ffn_full, slope)
    up_grad = start_reduce([(second_low, [d_pre])], "xyz")
    d_pre = tick(d_pre, up_grad)
    d_second = ALPHA * d_third + up_back_rows(d_pre, ffn_full)
    second_back = jax.vjp(layer_norm, second_sum, gain_full[1], shift_full[1])[1]
    d_second_sum, d_gain_two, d_shift_two = second_back(d_second)
    d_branch_two = tick(d_second_sum.astype(low), up_grad)
    d_cross = back_prod(d_branch_two, cross_out_full).astype(low)

    def cross_backward(id_row, memory_id_row, *arrays, pairs):
        fq, fk = document_features(id_row, memory_id_row)
        return attention_backward(fq, fk, *arrays, False, pairs)

    arrays = (target_flat, memory_id_flat, cross_queries, memory_keys, memory_values)
    arrays += (cross_flat, cross_lse, d_cross)
    grads = each_row(functools.partial(cross_backward, pairs=(0, 2 * half)), rows, arrays)
    d_cross_low, d_memory_keys, d_memory_values = tick(grads, output, up_grad)
    d_first = ALPHA * d_second_sum + back_prod(d_cross_low, cross_q_full)
    first_back = jax.vjp(layer_norm, first_sum, gain_full[0], shift_full[0])[1]
    d_first_sum, d_gain_one, d_shift_one = first_back(d_first)
    d_branch_one = d_first_sum.astype(low)
    grad_rows = [d_gain_one, d_gain_two, d_gain_three]
    grad_rows += [d_shift_one, d_shift_two, d_shift_three, grad_bias_down]
    cross_grad = Flight(
        whole_reduce(
            [
                (memory_flat, [d_memory_keys, d_memory_values]),
                (first_low, [d_cross_low]),
                (cross_flat, [d_branch_two]),
                (mixed_flat, [d_branch_one]),
            ],
            (jnp.stack(grad_rows), grad_bias_up),
        )
    )
    d_branch_one = tick(d_branch_one, cross_grad, up_grad)
    d_self = back_prod(d_branch_one, out_full).astype(low)
    d_memory = back_prod(d_memory_keys, mk_full) + back_prod(d_memory_values, mv_full)
    d_self, d_memory = lax.optimization_barrier((d_self, d_memory))
    d_memory = Flight(rows_out_steps(d_memory.reshape(rows, length, D), jnp.float32))
    d_self = tick(d_self, down_grad, d_memory)

    def self_backward(id_row, *arrays, pairs):
        fq, fk = document_features(id_row, id_row)
        return attention_backward(fq, fk, *arrays, True, pairs)

    arrays = (target_flat, *qkv, mixed_flat, self_lse, d_self)
    grads_a = each_row(functools.partial(self_backward, pairs=(0, half)), rows, arrays)
    grads_a = tick(grads_a, up_grad, down_grad)
    early_grad = start_reduce([(x_flat, grads_a)], "xzy")
    d_self = tick(d_self, early_grad, d_memory)
    arrays = (target_flat, *qkv, mixed_flat, self_lse, d_self)
    grads_b = each_row(functools.partial(self_backward, pairs=(half, half)), rows, arrays)
    grads_b = tick(grads_b, early_grad, up_grad)
    d_input = ALPHA * d_first_sum
    for grad_a, grad_b, weight in zip(grads_a, grads_b, qkv_full):
        d_input = d_input + back_prod(jnp.concatenate([grad_a, grad_b], axis=1), weight)
    d_input = Flight(rows_out_steps(d_input.reshape(rows, length, D), jnp.float32))
    grads_b = tick(grads_b, d_input)
    late_grad = start_reduce([(x_flat, grads_b)], "xzy")
    token = tick(grads_b[0], late_grad, early_grad)
    token = tick(token, late_grad)
    flights = [late_grad, early_grad, d_input, cross_grad]
    while any(f.result is None for f in flights):
        token = tick(token, *flights)
    grads, grad_rows, grad_bias_up = cross_grad.finish()
    grad_kv, grad_cross_q, grad_cross_out, grad_self_out = jnp.split(
        grads, [2 * D, 3 * D, 4 * D], axis=1
    )
    grad_qa, grad_ka, grad_va = early_grad.finish()
    grad_qb, grad_kb, grad_vb = late_grad.finish()
    return (
        output.finish(),
        d_input.finish(),
        d_memory.finish(),
        jnp.concatenate([grad_qa, grad_qb, grad_ka, grad_kb, grad_va, grad_vb], axis=1),
        grad_self_out,
        grad_cross_q,
        grad_kv,
        grad_cross_out,
        up_grad.finish()[0],
        down_grad.finish(),
        grad_bias_up,
        grad_rows[:3],
        grad_rows[3:],
    )


def per_device(inputs, *others):
    if inputs.shape[0] % lax.axis_size("blk") == 0:
        return whole_row_device(inputs, *others)
    return split_row_device(inputs, *others)


def solution(mesh):
    return jax.shard_map(
        per_device,
        mesh=mesh,
        in_specs=(
            P("batch", "blk", None),
            P("batch", "blk", None),
            P("batch", "blk"),
            P("batch", "blk"),
            P("batch", "blk", None),
            P("batch", None),
            P("batch", None),
            P("batch", None),
            P("batch", None),
            P("batch", None),
            P("batch", None),
            P("batch", None),
            P("batch"),
            P(None, "batch"),
            P(None, "batch"),
        ),
        out_specs=(
            P("batch", "blk", None),
            P("batch", "blk", None),
            P("batch", "blk", None),
            P("batch", None),
            P("batch", None),
            P("batch", None),
            P("batch", None),
            P("batch", None),
            P("batch", None),
            P("batch", None),
            P("batch"),
            P(None, "batch"),
            P(None, "batch"),
        ),
        check_vma=False,
    )
```

```python
import functools

import jax
import jax.numpy as jnp
from jax import lax
from jax.experimental import pallas as pl
from jax.experimental.pallas import tpu as pltpu
from jax.sharding import PartitionSpec as P

D = 1024
NH = 16
HD = 64
MB_ROWS = 1
MICRO = 2
ALPHA = 300.0**0.25
MASKED = -1e30
EPSILON = 1e-05
PAIR = 2 * HD
MASK_STEP = -(2.0**100)


def nt(left, right):
    return lax.dot_general(left, right, (((1,), (1,)), ((), ())), preferred_element_type=jnp.float32)


def nn(left, right):
    return lax.dot_general(left, right, (((1,), (0,)), ((), ())), preferred_element_type=jnp.float32)


def lane_of(rows):
    return lax.broadcasted_iota(jnp.int32, (rows, PAIR), 1)


def attention_fwd_kernel(causal, q_ref, k_ref, v_ref, fq_ref, fk_ref, out_ref, lse_ref):
    block = 256
    length = q_ref.shape[0]
    mem = k_ref.shape[0]
    low_q = lane_of(length) < HD
    low_k = lane_of(mem) < HD
    q = q_ref[...] * jnp.bfloat16(HD**-0.5)
    k = k_ref[...]
    v = v_ref[...]
    fq = fq_ref[...]
    fk = fk_ref[...]
    ones = jnp.ones_like(v)
    queries = (jnp.where(low_q, q, fq), jnp.where(low_q, fq, q))
    keys = (jnp.where(low_k, k, fk), jnp.where(low_k, fk, k))
    values = (jnp.where(low_k, v, ones), jnp.where(low_k, ones, v))
    low_blk = lane_of(block) < HD
    units = [(i, h) for i in range(length // block) for h in range(2)]

    def score(unit):
        i, h = unit
        seen = (i + 1) * block if causal else mem
        scores = nt(queries[h][i * block : (i + 1) * block], keys[h][:seen])
        if causal:
            tri = lax.broadcasted_iota(jnp.int32, (block, block), 0) >= lax.broadcasted_iota(
                jnp.int32, (block, block), 1
            )
            diag = jnp.where(tri, scores[:, seen - block :], MASK_STEP)
            scores = diag if i == 0 else jnp.concatenate([scores[:, : seen - block], diag], axis=1)
        return scores

    ahead = score(units[0])
    accs, peaks = [], []
    for n, (i, h) in enumerate(units):
        rows = slice(i * block, (i + 1) * block)
        scores = ahead
        if n + 1 < len(units):
            ahead = score(units[n + 1])
        peak = jnp.max(scores, axis=1, keepdims=True)
        raised = jnp.exp(scores - peak).astype(jnp.bfloat16)
        accs.append(nn(raised, values[h][: scores.shape[1]]))
        peaks.append(peak)
        if h == 1:
            total = pltpu.roll(jnp.where(low_blk, accs[1], accs[0]), HD, 1)
            out_ref[rows, :] = (jnp.where(low_blk, accs[0], accs[1]) / total).astype(out_ref.dtype)
            lse_ref[rows, :] = jnp.where(low_blk, peaks[0], peaks[1]) + jnp.log(total)
            accs, peaks = [], []


def split3(value):
    hi = value.astype(jnp.bfloat16)
    rest = value - hi.astype(jnp.float32)
    mid = rest.astype(jnp.bfloat16)
    lo = (rest - mid.astype(jnp.float32)).astype(jnp.bfloat16)
    return hi, mid, lo


def placed(lane, start, pieces, other):
    for n, piece in enumerate(pieces):
        other = jnp.where(lane == start + n, piece, other)
    return other


def attention_bwd_kernel(causal, q_ref, k_ref, v_ref, fq_ref, fk_ref, out_ref, lse_ref, do_ref, dq_ref, dk_ref, dv_ref, dk_acc, dv_acc, dq_acc):
    block = 256 if causal else 512
    length = q_ref.shape[0]
    mem = k_ref.shape[0]
    lane_q = lane_of(length)
    lane_k = lane_of(mem)
    low_q = lane_q < HD
    low_k = lane_k < HD
    scale = jnp.bfloat16(HD**-0.5)
    q = q_ref[...] * scale
    k = k_ref[...]
    v = v_ref[...]
    do = do_ref[...]
    fq = fq_ref[...]
    fk = fk_ref[...]
    zero_q = jnp.zeros_like(q)
    zero_k = jnp.zeros_like(k)
    one_k = jnp.ones_like(k)
    prod = do.astype(jnp.float32) * out_ref[...].astype(jnp.float32)
    sum_a = jnp.sum(jnp.where(low_q, prod, 0.0), axis=1, keepdims=True)
    sum_b = jnp.sum(jnp.where(low_q, 0.0, prod), axis=1, keepdims=True)
    inner = jnp.where(low_q, sum_b, sum_a)
    lse = pltpu.roll(lse_ref[...], HD, 1)
    half_q = lane_q & (HD - 1)
    half_k = lane_k & (HD - 1)
    fq = placed(half_q, 2, split3(-lse), fq)
    fk = jnp.where((half_k >= 2) & (half_k < 5), one_k, fk)
    fd = placed(half_q, 0, split3(-inner), zero_q)
    fv = jnp.where(half_k < 3, one_k, zero_k)
    queries = (jnp.where(low_q, q, fq), jnp.where(low_q, fq, q))
    keys = (jnp.where(low_k, k, fk), jnp.where(low_k, fk, k))
    grads = (jnp.where(low_q, do, fd), jnp.where(low_q, fd, do))
    values = (jnp.where(low_k, v, fv), jnp.where(low_k, fv, v))
    plain_q = (jnp.where(low_q, q, zero_q), jnp.where(low_q, zero_q, q))
    plain_do = (jnp.where(low_q, do, zero_q), jnp.where(low_q, zero_q, do))
    k_t = k.T
    units = [(i, h) for i in range(length // block) for h in range(2)]

    def scores_of(unit):
        i, h = unit
        rows = slice(i * block, (i + 1) * block)
        seen = (i + 1) * block if causal else mem
        return nt(keys[h][:seen], queries[h][rows]), nt(values[h][:seen], grads[h][rows])

    ahead = scores_of(units[0])
    dv = dk = None
    for n, (i, h) in enumerate(units):
        rows = slice(i * block, (i + 1) * block)
        seen = (i + 1) * block if causal else mem
        s, dp = ahead
        if n + 1 < len(units):
            ahead = scores_of(units[n + 1])
        p = jnp.exp(s)
        if causal:
            tri = lax.broadcasted_iota(jnp.int32, (block, block), 0) <= lax.broadcasted_iota(
                jnp.int32, (block, block), 1
            )
            diag = jnp.where(tri, p[seen - block :], 0.0)
            p = diag if i == 0 else jnp.concatenate([p[: seen - block], diag], axis=0)
        ds = (p * dp).astype(jnp.bfloat16)
        dq_acc[h * HD : (h + 1) * HD, rows] = nn(k_t[h * HD : (h + 1) * HD, :seen], ds)
        dv_part = nn(p.astype(jnp.bfloat16), plain_do[h][rows])
        dk_part = nn(ds, plain_q[h][rows])
        if n == 0:
            dv_acc[:seen] = dv_part
            dk_acc[:seen] = dk_part
            if seen < mem:
                dv_acc[seen:] = jnp.zeros((mem - seen, PAIR), jnp.float32)
                dk_acc[seen:] = jnp.zeros((mem - seen, PAIR), jnp.float32)
        else:
            dv_acc[:seen] += dv_part
            dk_acc[:seen] += dk_part
    dq_ref[...] = (dq_acc[...].T * (HD**-0.5)).astype(dq_ref.dtype)
    dk_ref[...] = dk_acc[...].astype(dk_ref.dtype)
    dv_ref[...] = dv_acc[...].astype(dv_ref.dtype)


def cols(length, first):
    return pl.BlockSpec((length, PAIR), lambda j: (0, first + j))


def whole(length):
    return pl.BlockSpec((length, PAIR), lambda j: (0, 0))


SHORT = pl.CostEstimate(flops=1024, bytes_accessed=1024, transcendentals=0)


def attention_call(kernel, name, pairs, causal, arrays, shared, lengths, kinds, scratch):
    first, count = pairs

    return pl.pallas_call(
        functools.partial(kernel, causal),
        grid=(count,),
        in_specs=[cols(a.shape[0], first) for a in arrays[:3]]
        + [whole(a.shape[0]) for a in shared]
        + [cols(a.shape[0], first) for a in arrays[3:]],
        out_specs=[cols(n, 0) for n in lengths],
        out_shape=[
            jax.ShapeDtypeStruct((n, count * PAIR), kind) for n, kind in zip(lengths, kinds)
        ],
        scratch_shapes=scratch,
        compiler_params=pltpu.CompilerParams(vmem_limit_bytes=48 * 2**20),
        cost_estimate=SHORT,
        name=name,
    )(*arrays[:3], *shared, *arrays[3:])


def attention_forward(queries, keys, values, fq, fk, causal, pairs):
    lengths = (queries.shape[0],) * 2
    kinds = (jnp.bfloat16, jnp.float32)
    arrays, shared = (queries, keys, values), (fq, fk)
    return attention_call(
        attention_fwd_kernel, "attention_forward", pairs, causal, arrays, shared, lengths, kinds, []
    )


def attention_backward(fq, fk, queries, keys, values, mixed, lse, d_mixed, causal, pairs):
    length, mem = queries.shape[0], keys.shape[0]
    scratch = [
        pltpu.VMEM((mem, PAIR), jnp.float32),
        pltpu.VMEM((mem, PAIR), jnp.float32),
        pltpu.VMEM((PAIR, length), jnp.float32),
    ]
    return attention_call(
        attention_bwd_kernel,
        "attention_backward",
        pairs,
        causal,
        (queries, keys, values, mixed, lse, d_mixed),
        (fq, fk),
        (length, mem, mem),
        (jnp.bfloat16,) * 3,
        scratch,
    )


def gelu_kernel(left_ref, right_ref, bias_ref, hidden_ref, slope_ref):
    slope_in = 0.7978845608028654
    right = right_ref[...].reshape(-1, right_ref.shape[-1])
    bias = bias_ref[...]
    step = min(256, left_ref.shape[0])
    for first in range(0, left_ref.shape[0], step):
        rows = slice(first, first + step)
        pre = nn(left_ref[rows, :], right) + bias
        square = pre * pre
        bent = jnp.tanh(slope_in * (pre + 0.044715 * (square * pre)))
        gate = 0.5 * (1.0 + bent)
        hidden_ref[rows, :] = (pre * gate).astype(hidden_ref.dtype)
        bend = (1.0 - bent * bent) * (slope_in + (slope_in * 0.134145) * square)
        slope_ref[rows, :] = gate + (0.5 * pre) * bend


def gelu_rows(left, ffn, bias):
    rows, inner = left.shape
    count, wide = ffn.shape[0], ffn.shape[2]
    tall_shard = inner // count
    columns = bias.shape[0]
    tall = min(rows, 1024)
    return pl.pallas_call(
        gelu_kernel,
        grid=(rows // tall, columns // wide),
        in_specs=[
            pl.BlockSpec((tall, inner), lambda i, j: (i, 0)),
            pl.BlockSpec((count, tall_shard, wide), lambda i, j: (0, j, 0)),
            pl.BlockSpec((1, wide), lambda i, j: (0, j)),
        ],
        out_specs=[pl.BlockSpec((tall, wide), lambda i, j: (i, j))] * 2,
        out_shape=[
            jax.ShapeDtypeStruct((rows, columns), jnp.bfloat16),
            jax.ShapeDtypeStruct((rows, columns), jnp.float32),
        ],
        compiler_params=pltpu.CompilerParams(vmem_limit_bytes=56 * 2**20),
        cost_estimate=SHORT,
        name="gelu_rows",
    )(left, ffn, bias.reshape(1, columns))


def spread_rows(summed):
    centred = summed - jnp.mean(summed, axis=1, keepdims=True)
    scale = lax.rsqrt(jnp.mean(centred * centred, axis=1, keepdims=True) + EPSILON)
    return centred * scale, scale


def norm_back(unit, scale, gain, grad):
    inner = grad * gain
    lean = jnp.mean(inner, axis=1, keepdims=True)
    tilt = jnp.mean(inner * unit, axis=1, keepdims=True)
    return scale * (inner - lean - unit * tilt)


def add_column_sums(ref, terms):
    rows = [jnp.sum(t, axis=0, keepdims=True) for t in terms]
    rows.append(jnp.zeros((ref.shape[0] - len(rows), ref.shape[1]), jnp.float32))
    part = jnp.concatenate(rows, axis=0)

    @pl.when(pl.program_id(0) == 0)
    def _():
        ref[...] = part

    @pl.when(pl.program_id(0) > 0)
    def _():
        ref[...] += part


def row_tiles(kernel, name, tiled, fixed, outs, sums=False):
    rows = tiled[0].shape[0]
    tall = min(rows, 256)
    in_specs = [pl.BlockSpec((tall, a.shape[1]), lambda i: (i, 0)) for a in tiled]
    for _, block, index in fixed:
        in_specs.append(
            pl.BlockSpec(block, lambda i, at=index: at, pipeline_mode=pl.Buffered(1))
        )
    out_specs = [pl.BlockSpec((tall, D), lambda i: (i, 0)) for _ in outs]
    out_shape = [jax.ShapeDtypeStruct((rows, D), kind) for kind in outs]
    if sums:
        out_specs.append(pl.BlockSpec((8, D), lambda i: (0, 0)))
        out_shape.append(jax.ShapeDtypeStruct((8, D), jnp.float32))
    return pl.pallas_call(
        kernel,
        grid=(rows // tall,),
        in_specs=in_specs,
        out_specs=out_specs,
        out_shape=out_shape,
        compiler_params=pltpu.CompilerParams(vmem_limit_bytes=56 * 2**20),
        cost_estimate=SHORT,
        name=name,
    )(*tiled, *[array for array, _, _ in fixed])


def column_block(attn_full, block):
    return (attn_full, (D, D), (0, block))


def small_block(norms):
    return (norms, norms.shape, (0, 0))


def first_norm_kernel(mixed, x, out_w, cross_w, norms, sum_ref, normed_ref, low_ref, query_ref):
    summed = ALPHA * x[...].astype(jnp.float32) + nn(mixed[...], out_w[...])
    sum_ref[...] = summed
    normed = spread_rows(summed)[0] * norms[0:1, :] + norms[3:4, :]
    normed_ref[...] = normed
    low = normed.astype(jnp.bfloat16)
    low_ref[...] = low
    query_ref[...] = nn(low, cross_w[...]).astype(jnp.bfloat16)


def second_norm_kernel(mixed, first, out_w, norms, sum_ref, normed_ref, low_ref):
    summed = ALPHA * first[...] + nn(mixed[...], out_w[...])
    sum_ref[...] = summed
    normed = spread_rows(summed)[0] * norms[1:2, :] + norms[4:5, :]
    normed_ref[...] = normed
    low_ref[...] = normed.astype(jnp.bfloat16)


def third_norm_kernel(hidden, second, cot, down, norms, out_ref, grad_ref, low_ref, sums_ref):
    right = down[...].reshape(-1, down.shape[-1])
    summed = ALPHA * second[...] + nn(hidden[...], right) + norms[6:7, :]
    unit, scale = spread_rows(summed)
    out_ref[...] = (unit * norms[2:3, :] + norms[5:6, :]).astype(jnp.bfloat16)
    cotangent = cot[...].astype(jnp.float32)
    grad = norm_back(unit, scale, norms[2:3, :], cotangent)
    grad_ref[...] = grad
    low = grad.astype(jnp.bfloat16)
    low_ref[...] = low
    add_column_sums(sums_ref, [cotangent * unit, cotangent, low.astype(jnp.float32)])


def second_back_kernel(
    d_pre, d_third, summed, up, out_w, norms, grad_ref, low_ref, back_ref, sums_ref
):
    wide = up.shape[2]
    tall_shard = D // up.shape[0]
    grad = ALPHA * d_third[...]
    for n in range(up.shape[1] // tall_shard):
        right = up[:, n * tall_shard : (n + 1) * tall_shard].reshape(-1, wide)
        grad += nt(d_pre[:, n * wide : (n + 1) * wide], right)
    unit, scale = spread_rows(summed[...])
    d_sum = norm_back(unit, scale, norms[1:2, :], grad)
    grad_ref[...] = d_sum
    low = d_sum.astype(jnp.bfloat16)
    low_ref[...] = low
    back_ref[...] = nt(low, out_w[...]).astype(jnp.bfloat16)
    add_column_sums(sums_ref, [grad * unit, grad])


def first_back_kernel(
    d_query, d_second, summed, cross_w, out_w, norms, grad_ref, low_ref, back_ref, sums_ref
):
    grad = ALPHA * d_second[...] + nt(d_query[...], cross_w[...])
    unit, scale = spread_rows(summed[...])
    d_sum = norm_back(unit, scale, norms[0:1, :], grad)
    grad_ref[...] = d_sum
    low = d_sum.astype(jnp.bfloat16)
    low_ref[...] = low
    back_ref[...] = nt(low, out_w[...]).astype(jnp.bfloat16)
    add_column_sums(sums_ref, [grad * unit, grad])


def gelu_back_kernel(left_ref, right_ref, slope_ref, out_ref, sum_ref):
    right = right_ref[...].reshape(-1, right_ref.shape[-1])
    step = min(512, left_ref.shape[0])
    total = None
    for first in range(0, left_ref.shape[0], step):
        rows = slice(first, first + step)
        d_hidden = nt(left_ref[rows, :], right).astype(jnp.bfloat16).astype(jnp.float32)
        d_pre = (d_hidden * slope_ref[rows, :]).astype(jnp.bfloat16)
        out_ref[rows, :] = d_pre
        part = jnp.sum(d_pre.astype(jnp.float32), axis=0, keepdims=True)
        total = part if total is None else total + part
    sum_ref[...] = total[None]


def gelu_back_rows(left, ffn, slope):
    rows, inner = left.shape
    count, columns = ffn.shape[0], slope.shape[1]
    tall, group = min(rows, 1024), 4
    wide = columns // count * group
    out, sums = pl.pallas_call(
        gelu_back_kernel,
        grid=(rows // tall, columns // wide),
        in_specs=[
            pl.BlockSpec((tall, inner), lambda i, j: (i, 0)),
            pl.BlockSpec((group, columns // count, inner), lambda i, j: (j, 1, 0)),
            pl.BlockSpec((tall, wide), lambda i, j: (i, j)),
        ],
        out_specs=[
            pl.BlockSpec((tall, wide), lambda i, j: (i, j)),
            pl.BlockSpec((1, 1, wide), lambda i, j: (i, 0, j)),
        ],
        out_shape=[
            jax.ShapeDtypeStruct((rows, columns), jnp.bfloat16),
            jax.ShapeDtypeStruct((rows // tall, 1, columns), jnp.float32),
        ],
        compiler_params=pltpu.CompilerParams(vmem_limit_bytes=48 * 2**20),
        cost_estimate=SHORT,
        name="gelu_back_rows",
    )(left, ffn, slope)
    return out, jnp.sum(sums, axis=(0, 1))


def document_features(query_ids, key_ids):
    half = jnp.arange(PAIR, dtype=jnp.int32)[None, :] % HD
    fq = (half == query_ids[:, None]).astype(jnp.bfloat16)
    fk = jnp.where((half < 2) & (half != key_ids[:, None]), MASK_STEP, 0.0).astype(jnp.bfloat16)
    return fq, fk


def shortened(array):
    return jax.tree.map(lambda a: a.astype(jnp.bfloat16) if a.dtype == jnp.float32 else a, array)


def layer_norm(summed, gain_row, shift_row):
    average = jnp.mean(summed, axis=-1, keepdims=True)
    centred = summed - average
    spread = jnp.mean(centred * centred, axis=-1, keepdims=True)
    return centred * lax.rsqrt(spread + EPSILON) * gain_row + shift_row


def split_heads(array_in):
    return array_in.reshape(array_in.shape[0], array_in.shape[1], NH, HD)


def weight_grad(left_rows, right_rows):
    return jnp.einsum("tk,tn->kn", left_rows, right_rows, preferred_element_type=jnp.float32)


def back_prod(grad_rows, matrix):
    return jnp.einsum("tn,kn->tk", grad_rows, matrix, preferred_element_type=jnp.float32)


def attention_scores(queries, key_rows, allowed):
    scores = jnp.einsum(
        "rqhd,rkhd->rhqk",
        split_heads(queries),
        split_heads(key_rows),
        preferred_element_type=jnp.float32,
    ) * HD ** (-0.5)
    return jnp.where(allowed[:, None], scores, MASKED)


def plain_attention_forward(queries, key_rows, value_rows, allowed):
    scores = attention_scores(queries, key_rows, allowed)
    row_peak = jnp.max(scores, axis=-1, keepdims=True)
    raised = jnp.exp(scores - row_peak)
    row_total = jnp.sum(raised, axis=-1, keepdims=True)
    probabilities = (raised / row_total).astype(jnp.bfloat16)
    attended = jnp.einsum(
        "rhqk,rkhd->rqhd",
        probabilities,
        split_heads(value_rows),
        preferred_element_type=jnp.float32,
    )
    return (attended.reshape(queries.shape).astype(jnp.bfloat16), row_peak, row_total)


def plain_attention_backward(queries, key_rows, value_rows, allowed, row_peak, row_total, d_attended):
    scores = attention_scores(queries, key_rows, allowed)
    probabilities = jnp.exp(scores - row_peak) / row_total
    d_heads = split_heads(d_attended)
    d_values = jnp.einsum(
        "rhqk,rqhd->rkhd",
        probabilities.astype(jnp.bfloat16),
        d_heads,
        preferred_element_type=jnp.float32,
    )
    d_probs = jnp.einsum(
        "rqhd,rkhd->rhqk", d_heads, split_heads(value_rows), preferred_element_type=jnp.float32
    )
    inner_sum = jnp.sum(probabilities * d_probs, axis=-1, keepdims=True)
    d_scores = (probabilities * (d_probs - inner_sum)).astype(jnp.bfloat16)
    d_queries = jnp.einsum(
        "rhqk,rkhd->rqhd", d_scores, split_heads(key_rows), preferred_element_type=jnp.float32
    ) * HD ** (-0.5)
    d_keys = jnp.einsum(
        "rhqk,rqhd->rkhd", d_scores, split_heads(queries), preferred_element_type=jnp.float32
    ) * HD ** (-0.5)
    d_pairs = jnp.concatenate(
        [d_keys.reshape(key_rows.shape), d_values.reshape(value_rows.shape)], axis=2
    )
    return (d_queries.reshape(queries.shape), d_pairs)


def add_terms(running, fresh):
    if running is None:
        return fresh
    return tuple((first_term + second_term for first_term, second_term in zip(running, fresh)))


def split_row_device(
    inputs,
    memory,
    target_ids,
    memory_ids,
    cotangent,
    w_self_qkv,
    w_self_out,
    w_cross_q,
    w_cross_kv,
    w_cross_out,
    w_up,
    w_down,
    b_up,
    gains,
    shifts,
):
    tokens_here = inputs.shape[1]
    length = tokens_here * lax.axis_size("blk")
    token_count = MB_ROWS * tokens_here
    query_places = lax.axis_index("blk") * tokens_here + jnp.arange(tokens_here, dtype=jnp.int32)
    key_places = jnp.arange(length, dtype=jnp.int32)
    causal = key_places[None, :] <= query_places[:, None]
    outputs, input_grads, memory_grads = ([], [], [])
    attn_total = None
    ffn_total = None
    for micro_step in range(MICRO):
        row_range = slice(micro_step * MB_ROWS, (micro_step + 1) * MB_ROWS)
        qkv_full, out_full, cross_q_full, cross_kv_full, cross_out_full, gain_low, shift_low = (
            lax.all_gather(w_self_qkv, "batch", axis=0, tiled=True),
            lax.all_gather(w_self_out, "batch", axis=0, tiled=True),
            lax.all_gather(w_cross_q, "batch", axis=0, tiled=True),
            lax.all_gather(w_cross_kv, "batch", axis=0, tiled=True),
            lax.all_gather(w_cross_out, "batch", axis=0, tiled=True),
            lax.all_gather(gains, "batch", axis=1, tiled=True),
            lax.all_gather(shifts, "batch", axis=1, tiled=True),
        )
        gain_full = gain_low.astype(jnp.float32)
        shift_full = shift_low.astype(jnp.float32)
        x_flat = inputs[row_range].reshape(token_count, D)
        memory_flat = memory[row_range].reshape(token_count, D)
        seg_rows = target_ids[row_range]
        memory_seg_rows = memory_ids[row_range]
        projected = (
            jnp.dot(x_flat, qkv_full, preferred_element_type=jnp.float32)
            .astype(jnp.bfloat16)
            .reshape(MB_ROWS, tokens_here, 3 * D)
        )
        self_queries = projected[:, :, :D]
        key_pairs, key_segs = (
            lax.all_gather(projected[:, :, D:], "blk", axis=1, tiled=True),
            lax.all_gather(seg_rows, "blk", axis=1, tiled=True),
        )
        self_allowed = (seg_rows[:, :, None] == key_segs[:, None, :]) & causal[None]
        self_mixed, self_peak, self_total = plain_attention_forward(
            self_queries, key_pairs[:, :, :D], key_pairs[:, :, D:], self_allowed
        )
        mixed_flat = self_mixed.reshape(token_count, D)
        first_sum = ALPHA * x_flat.astype(jnp.float32) + jnp.dot(
            mixed_flat, out_full, preferred_element_type=jnp.float32
        )
        first = layer_norm(first_sum, gain_full[0], shift_full[0])
        first_low = first.astype(jnp.bfloat16)
        cross_queries = (
            jnp.dot(first_low, cross_q_full, preferred_element_type=jnp.float32)
            .astype(jnp.bfloat16)
            .reshape(MB_ROWS, tokens_here, D)
        )
        memory_local = (
            jnp.dot(memory_flat, cross_kv_full, preferred_element_type=jnp.float32)
            .astype(jnp.bfloat16)
            .reshape(MB_ROWS, tokens_here, 2 * D)
        )
        memory_pairs, memory_segs = (
            lax.all_gather(memory_local, "blk", axis=1, tiled=True),
            lax.all_gather(memory_seg_rows, "blk", axis=1, tiled=True),
        )
        cross_allowed = seg_rows[:, :, None] == memory_segs[:, None, :]
        cross_mixed, cross_peak, cross_total = plain_attention_forward(
            cross_queries, memory_pairs[:, :, :D], memory_pairs[:, :, D:], cross_allowed
        )
        cross_flat = cross_mixed.reshape(token_count, D)
        second_sum = ALPHA * first + jnp.dot(
            cross_flat, cross_out_full, preferred_element_type=jnp.float32
        )
        second = layer_norm(second_sum, gain_full[1], shift_full[1])
        second_low = second.astype(jnp.bfloat16)
        up_full, down_full, bias_full = (
            lax.all_gather(w_up, "batch", axis=0, tiled=True),
            lax.all_gather(w_down, "batch", axis=0, tiled=True),
            lax.all_gather(b_up, "batch", axis=0, tiled=True),
        )
        hidden_pre = jnp.dot(
            second_low, up_full, preferred_element_type=jnp.float32
        ) + bias_full.astype(jnp.float32)
        hidden_low = jax.nn.gelu(hidden_pre).astype(jnp.bfloat16)
        third_sum = (
            ALPHA * second
            + jnp.dot(hidden_low, down_full, preferred_element_type=jnp.float32)
            + shift_full[3]
        )
        result, third_back = jax.vjp(layer_norm, third_sum, gain_full[2], shift_full[2])
        outputs.append(result.astype(jnp.bfloat16).reshape(MB_ROWS, tokens_here, D))
        cot_flat = cotangent[row_range].reshape(token_count, D).astype(jnp.float32)
        d_third, d_gain_three, d_shift_three = third_back(cot_flat)
        d_branch_three = d_third.astype(jnp.bfloat16)
        grad_down = weight_grad(hidden_low, d_branch_three)
        grad_bias_down = jnp.sum(d_branch_three.astype(jnp.float32), axis=0)
        d_hidden = back_prod(d_branch_three, down_full).astype(jnp.bfloat16)
        gelu_back = jax.vjp(jax.nn.gelu, hidden_pre)[1]
        d_pre = gelu_back(d_hidden.astype(jnp.float32))[0].astype(jnp.bfloat16)
        grad_up = weight_grad(second_low, d_pre)
        grad_bias_up = jnp.sum(d_pre.astype(jnp.float32), axis=0)
        d_second = ALPHA * d_third + back_prod(d_pre, up_full)
        ffn_terms = (grad_up, grad_down, grad_bias_up)
        ffn_share = (
            lax.psum_scatter(
                ffn_terms[0].astype(jnp.bfloat16), "batch", scatter_dimension=0, tiled=True
            ).astype(jnp.float32),
            lax.psum_scatter(
                ffn_terms[1].astype(jnp.bfloat16), "batch", scatter_dimension=0, tiled=True
            ).astype(jnp.float32),
            lax.psum_scatter(
                ffn_terms[2].astype(jnp.bfloat16), "batch", scatter_dimension=0, tiled=True
            ).astype(jnp.float32),
        )
        ffn_total = add_terms(ffn_total, ffn_share)
        second_back = jax.vjp(layer_norm, second_sum, gain_full[1], shift_full[1])[1]
        d_second_sum, d_gain_two, d_shift_two = second_back(d_second)
        d_branch_two = d_second_sum.astype(jnp.bfloat16)
        grad_cross_out = weight_grad(cross_flat, d_branch_two)
        d_cross = (
            back_prod(d_branch_two, cross_out_full)
            .astype(jnp.bfloat16)
            .reshape(MB_ROWS, tokens_here, D)
        )
        d_cross_queries, d_memory_all = plain_attention_backward(
            cross_queries,
            memory_pairs[:, :, :D],
            memory_pairs[:, :, D:],
            cross_allowed,
            cross_peak,
            cross_total,
            d_cross,
        )
        d_memory_pairs = lax.psum_scatter(
            d_memory_all.astype(jnp.bfloat16), "blk", scatter_dimension=1, tiled=True
        ).reshape(token_count, 2 * D)
        grad_cross_kv = weight_grad(memory_flat, d_memory_pairs)
        memory_grads.append(
            back_prod(d_memory_pairs, cross_kv_full).reshape(MB_ROWS, tokens_here, D)
        )
        d_cross_low = d_cross_queries.astype(jnp.bfloat16).reshape(token_count, D)
        grad_cross_q = weight_grad(first_low, d_cross_low)
        d_first = ALPHA * d_second_sum + back_prod(d_cross_low, cross_q_full)
        first_back = jax.vjp(layer_norm, first_sum, gain_full[0], shift_full[0])[1]
        d_first_sum, d_gain_one, d_shift_one = first_back(d_first)
        d_branch_one = d_first_sum.astype(jnp.bfloat16)
        grad_self_out = weight_grad(mixed_flat, d_branch_one)
        d_self = (
            back_prod(d_branch_one, out_full).astype(jnp.bfloat16).reshape(MB_ROWS, tokens_here, D)
        )
        d_self_queries, d_key_all = plain_attention_backward(
            self_queries,
            key_pairs[:, :, :D],
            key_pairs[:, :, D:],
            self_allowed,
            self_peak,
            self_total,
            d_self,
        )
        d_self_pairs = lax.psum_scatter(
            d_key_all.astype(jnp.bfloat16), "blk", scatter_dimension=1, tiled=True
        )
        d_projected = jnp.concatenate(
            [d_self_queries.astype(jnp.bfloat16), d_self_pairs], axis=2
        ).reshape(token_count, 3 * D)
        grad_self_qkv = weight_grad(x_flat, d_projected)
        input_grads.append(
            (ALPHA * d_first_sum + back_prod(d_projected, qkv_full)).reshape(
                MB_ROWS, tokens_here, D
            )
        )
        grad_gains = jnp.stack([d_gain_one, d_gain_two, d_gain_three])
        grad_shifts = jnp.stack([d_shift_one, d_shift_two, d_shift_three, grad_bias_down])
        attn_terms = (
            grad_self_qkv,
            grad_self_out,
            grad_cross_q,
            grad_cross_kv,
            grad_cross_out,
            grad_gains,
            grad_shifts,
        )
        attn_share = (
            lax.psum_scatter(
                attn_terms[0].astype(jnp.bfloat16), "batch", scatter_dimension=0, tiled=True
            ).astype(jnp.float32),
            lax.psum_scatter(
                attn_terms[1].astype(jnp.bfloat16), "batch", scatter_dimension=0, tiled=True
            ).astype(jnp.float32),
            lax.psum_scatter(
                attn_terms[2].astype(jnp.bfloat16), "batch", scatter_dimension=0, tiled=True
            ).astype(jnp.float32),
            lax.psum_scatter(
                attn_terms[3].astype(jnp.bfloat16), "batch", scatter_dimension=0, tiled=True
            ).astype(jnp.float32),
            lax.psum_scatter(
                attn_terms[4].astype(jnp.bfloat16), "batch", scatter_dimension=0, tiled=True
            ).astype(jnp.float32),
            lax.psum_scatter(
                attn_terms[5].astype(jnp.bfloat16), "batch", scatter_dimension=1, tiled=True
            ).astype(jnp.float32),
            lax.psum_scatter(
                attn_terms[6].astype(jnp.bfloat16), "batch", scatter_dimension=1, tiled=True
            ).astype(jnp.float32),
        )
        attn_total = add_terms(attn_total, attn_share)
    grad_parts = tuple(attn_total) + tuple(ffn_total)
    totals = jax.tree.map(
        lambda part: part.astype(jnp.float32), lax.psum(shortened(grad_parts), "blk")
    )
    output = jnp.concatenate(outputs, axis=0)
    d_input = jnp.concatenate(input_grads, axis=0)
    d_memory = jnp.concatenate(memory_grads, axis=0)
    return (
        output,
        d_input,
        d_memory,
        totals[0],
        totals[1],
        totals[2],
        totals[3],
        totals[4],
        totals[7],
        totals[8],
        totals[9],
        totals[5],
        totals[6],
    )


def swap_pair(array):
    return lax.ppermute(array, "blk", [(0, 1), (1, 0)])


def rows_in(array):
    count = lax.axis_size("blk")
    here = array.shape[0] // count
    parts = array.reshape((count, here) + array.shape[1:])
    if count == 1:
        return parts[0]
    if count == 2:
        me = lax.axis_index("blk")
        kept = lax.dynamic_index_in_dim(parts, me, 0, keepdims=False)
        got = swap_pair(lax.dynamic_index_in_dim(parts, 1 - me, 0, keepdims=False))
        first = jnp.where(me == 0, kept, got)
        second = jnp.where(me == 0, got, kept)
        return jnp.concatenate([first, second], axis=1)
    moved = lax.all_to_all(parts, "blk", 0, 0)
    moved = jnp.moveaxis(moved, 0, 1)
    return moved.reshape((here, count * array.shape[1]) + array.shape[2:])


def rows_out(array, kind):
    count = lax.axis_size("blk")
    here, length = array.shape[:2]
    tokens = length // count
    parts = array.reshape((here, count, tokens) + array.shape[2:])
    if count == 1:
        return parts[:, 0].astype(kind)
    if count == 2:
        me = lax.axis_index("blk")
        kept = lax.dynamic_index_in_dim(parts, me, 1, keepdims=False).astype(kind)
        sent = lax.dynamic_index_in_dim(parts, 1 - me, 1, keepdims=False).astype(jnp.bfloat16)
        got = swap_pair(sent).astype(kind)
        first = jnp.where(me == 0, kept, got)
        second = jnp.where(me == 0, got, kept)
        return jnp.concatenate([first, second], axis=0)
    moved = lax.all_to_all(jnp.moveaxis(parts, 1, 0).astype(jnp.bfloat16), "blk", 0, 0)
    return moved.reshape((count * here, tokens) + array.shape[2:]).astype(kind)


def gathered(shard, axis=0):
    return lax.all_gather(shard, "batch", axis=axis, tiled=True)


def shared_out(grad, axis=0):
    part = lax.psum_scatter(
        grad.astype(jnp.bfloat16), "batch", scatter_dimension=axis, tiled=True
    )
    return lax.psum(part, "blk").astype(jnp.float32)


class Flight:
    def __init__(self, steps):
        self.steps = steps
        self.result = None
        self.wanted = next(steps)
        self.pending = None

    def launch(self):
        self.pending = [send(array) for send, array in self.wanted]

    def advance(self, arrived):
        try:
            self.wanted = self.steps.send(arrived)
        except StopIteration as stop:
            self.wanted, self.result = [], stop.value

    def finish(self):
        while self.result is None:
            if self.pending is None:
                self.launch()
            self.advance(self.pending)
            self.pending = None
        return self.result


def tick(value, *flights):
    flying = [f for f in flights if f.result is None]
    value, arrived = lax.optimization_barrier((value, [f.pending or [] for f in flying]))
    for flight, got in zip(flying, arrived):
        if flight.pending is not None:
            flight.advance(got)
    flying = [f for f in flying if f.result is None]
    value, ready = lax.optimization_barrier((value, [[a for _, a in f.wanted] for f in flying]))
    for flight, arrays in zip(flying, ready):
        flight.wanted = [(send, a) for (send, _), a in zip(flight.wanted, arrays)]
        flight.launch()
    return value


def grid_place():
    batch = lax.axis_index("batch")
    return batch // 4, batch // 2 % 2, batch % 2, lax.axis_index("blk")


def z_sender(step):
    return lambda array: to_z(array, step)


def to_core(array):
    return lax.ppermute(array, "batch", [(n, n ^ 1) for n in range(16)])


def to_x(array):
    return lax.ppermute(array, "batch", [(n, n ^ 2) for n in range(16)])


def to_z(array, step):
    return lax.ppermute(array, "batch", [(n, (n + 4 * step) % 16) for n in range(16)])


def to_core_blk(array):
    pairs = [(2 * n + m, 2 * (n ^ 1) + (1 - m)) for n in range(16) for m in range(2)]
    return lax.ppermute(array, ("batch", "blk"), pairs)


def piece(array, axis, at, size):
    return lax.dynamic_slice_in_dim(array, at * size, size, axis)


def summed_low(terms):
    total = terms[0].astype(jnp.float32)
    for term in terms[1:]:
        total = total + term.astype(jnp.float32)
    return total.astype(jnp.bfloat16)


def in_order(at, own, other, axis):
    first = jnp.where(at == 0, own, other)
    second = jnp.where(at == 0, other, own)
    return jnp.concatenate([first, second], axis=axis)


FLIP = {"x": (0, 1, 0, 0), "c": (0, 0, 1, 0), "y": (0, 0, 0, 1)}
SEND = {"x": to_x, "c": to_core, "y": swap_pair}


def weight_gather(shards, path):
    blk = lax.axis_index("blk")
    if "y" in path:
        shards = [piece(s, 1, blk, s.shape[1] // 2) for s in shards]
    held = [(jnp.concatenate(shards, axis=1)[None], [(0, 0, 0, 0)])]
    return (yield from gather_steps(held, [s.shape for s in shards], path, "y" in path))


def gather_steps(held, shapes, path, split):
    for axis in path:
        if axis == "/":
            (block, labels), count = held[0], (len(shapes) + 1) // 2
            wide = sum(shape[1] for shape in shapes[:count])
            ways = [
                gather_steps([(block[:, :, :wide], labels)], shapes[:count], "yxc", split),
                gather_steps([(block[:, :, wide:], labels)], shapes[count:], "xyc", split),
            ]
            return (yield from together(ways))
        if axis == "z":
            block = jnp.concatenate([a for a, _ in held], axis=0) if len(held) > 1 else held[0][0]
            labels = sum((near for _, near in held), [])
            got = yield [(z_sender(step), block) for step in (1, 2, 3)]
            block = jnp.concatenate([block] + list(got), axis=0)
            held = [(block, [(d, b, c, e) for d in range(4) for _, b, c, e in labels])]
        else:
            got = yield [(SEND[axis], a) for a, _ in held]
            flip = FLIP[axis]
            held = held + [
                (g, [tuple(p + f for p, f in zip(label, flip)) for label in near])
                for g, (_, near) in zip(got, held)
            ]
    return placed_blocks(held, shapes, split)


def together(ways):
    wanted = [next(way) for way in ways]
    results = []
    while not results:
        got = yield sum(wanted, [])
        for n, way in enumerate(ways):
            mine, got = got[: len(wanted[n])], got[len(wanted[n]) :]
            try:
                wanted[n] = way.send(mine)
            except StopIteration as stop:
                results += stop.value
    return results


def place_kernel(near_lists, shapes, split, place, *refs):
    sources, targets = refs[: len(near_lists)], refs[len(near_lists) :]
    for source, near in zip(sources, near_lists):
        for n, (dx, dc, dy) in enumerate(near):
            row = (place[1] + dx) % 2 * 2 + (place[2] + dc) % 2
            first = 0
            for target, (tall, wide) in zip(targets, shapes):
                at = pl.ds(pl.multiple_of(row * tall, tall), tall)
                block = source[n, :, first : first + wide]
                if split:
                    side = (place[3] + dy) % 2
                    target[at, pl.ds(pl.multiple_of(side * wide, wide), wide)] = block
                else:
                    target[at, :] = block
                first += wide


def placed_blocks(held, shapes, split):
    place = jnp.stack(grid_place()).astype(jnp.int32)
    counts = [len(near) // 4 for _, near in held]
    near_lists = [[label[1:] for label in near[:n]] for n, (_, near) in zip(counts, held)]
    outs = [(tall, wide * (2 if split else 1)) for tall, wide in shapes]
    return pl.pallas_call(
        functools.partial(place_kernel, near_lists, shapes, split),
        grid_spec=pltpu.PrefetchScalarGridSpec(
            num_scalar_prefetch=1,
            grid=(4,),
            in_specs=[
                pl.BlockSpec((n,) + a.shape[1:], lambda d, p: (d, 0, 0))
                for n, (a, _) in zip(counts, held)
            ],
            out_specs=[
                pl.BlockSpec((4 * tall, wide), lambda d, p: ((p[0] + 4 - d) % 4, 0))
                for tall, wide in outs
            ],
        ),
        out_shape=[jax.ShapeDtypeStruct((tall * 16, wide), jnp.bfloat16) for tall, wide in outs],
        compiler_params=pltpu.CompilerParams(vmem_limit_bytes=40 * 2**20),
        cost_estimate=SHORT,
        name="place_weights",
    )(place, *[a for a, _ in held])


def halves(terms, axis, at):
    size = terms[0].shape[axis] // 2
    return (
        summed_low([piece(t, axis, 1 - at, size) for t in terms]),
        [piece(t, axis, at, size) for t in terms],
    )


def grads_kernel(plan, halved, *refs):
    lefts = 1 + max(p[0] for p in plan)
    rights = 1 + max(p[1] for p in plan)
    outs = refs[-4 - (2 if halved else 1) : -4]
    extra = refs[lefts + rights : -4 - len(outs)]
    left_buf, right_buf, out_buf, sems = refs[-4:]
    core = lax.axis_index("batch") % 2

    def loads(n):
        left, right, first, wide = plan[n]
        copies = []
        if n == 0 or plan[n - 1][0] != left:
            slot = left % 2
            copies.append(pltpu.make_async_copy(refs[left], left_buf.at[slot], sems.at[0, slot]))
        source = refs[lefts + right].at[:, pl.ds(first, wide)]
        target = right_buf.at[n % 2, :, pl.ds(0, wide)]
        copies.append(pltpu.make_async_copy(source, target, sems.at[1, n % 2]))
        return copies

    def stores(n):
        wide = plan[n][3]
        at = sum(p[3] for p in plan[:n])
        held = out_buf.at[n % 2]
        if not halved:
            place = outs[0].at[:, pl.ds(at, wide)]
            return [pltpu.make_async_copy(held.at[:, pl.ds(0, wide)], place, sems.at[2, n % 2])]
        copies = []
        for side, out in enumerate(outs):
            first = pl.multiple_of((core + 1 - side) % 2 * (wide // 2), wide // 2)
            place = out.at[:, pl.ds(at // 2, wide // 2)]
            source = held.at[:, pl.ds(first, wide // 2)]
            copies.append(pltpu.make_async_copy(source, place, sems.at[2 + side, n % 2]))
        return copies

    for copy in loads(0):
        copy.start()
    if extra:
        wide = extra[0].shape[1]
        held = out_buf.at[0, :, pl.ds(0, wide)]
        place = outs[0].at[:, pl.ds(sum(p[3] for p in plan), wide)]
        for source, target in ((extra[0], held), (held, place)):
            copy = pltpu.make_async_copy(source, target, sems.at[3, 0])
            copy.start()
            copy.wait()
    for n, (left, _, _, wide) in enumerate(plan):
        if n + 1 < len(plan):
            for copy in loads(n + 1):
                copy.start()
        for copy in loads(n):
            copy.wait()
        if n >= 2:
            for copy in stores(n - 2):
                copy.wait()
        grad = lax.dot_general(
            left_buf[left % 2],
            right_buf[n % 2, :, :wide],
            (((0,), (0,)), ((), ())),
            preferred_element_type=jnp.float32,
        )
        out_buf[n % 2, :, :wide] = grad.astype(out_buf.dtype)
        for copy in stores(n):
            copy.start()
    for n in range(max(0, len(plan) - 2), len(plan)):
        for copy in stores(n):
            copy.wait()


def joined_grads(products, halved, extra=()):
    lefts, rights, plan = [], [], []
    for left, group in products:
        lefts.append(left)
        for right in group:
            rights.append(right)
            wide = min(right.shape[1], D)
            for first in range(0, right.shape[1], wide):
                plan.append((len(lefts) - 1, len(rights) - 1, first, wide))
    tokens, rows = lefts[0].shape
    total = sum(p[3] for p in plan) + sum(e.shape[1] for e in extra)
    shape = jax.ShapeDtypeStruct((rows, total // 2 if halved else total), jnp.bfloat16)
    anywhere = pl.BlockSpec(memory_space=pl.ANY)
    widest = max(p[3] for p in plan)
    return pl.pallas_call(
        functools.partial(grads_kernel, plan, halved),
        in_specs=[anywhere] * (len(lefts) + len(rights) + len(extra)),
        out_specs=[anywhere] * (2 if halved else 1),
        out_shape=[shape] * (2 if halved else 1),
        scratch_shapes=[
            pltpu.VMEM((2, tokens, rows), jnp.bfloat16),
            pltpu.VMEM((2, tokens, widest), jnp.bfloat16),
            pltpu.VMEM((2, rows, widest), jnp.bfloat16),
            pltpu.SemaphoreType.DMA((4, 2)),
        ],
        compiler_params=pltpu.CompilerParams(vmem_limit_bytes=48 * 2**20),
        cost_estimate=SHORT,
        name="joined_grads",
    )(*lefts, *rights, *extra)


def gradient_reduce(products, path):
    z, x, core, blk = grid_place()
    given, kept = joined_grads(products, True)
    (got,) = yield [(to_core, given)]
    rows, columns = kept.shape
    terms = [t.reshape(4, 2, rows // 8, columns) for t in (kept, got)]
    for axis in path:
        if axis == "z":
            out = []
            for step in (1, 2, 3):
                parts = [piece(t, 0, (z + step) % 4, 1) for t in terms]
                out.append((z_sender(step), summed_low(parts)))
            out = yield out
            terms = [piece(t, 0, z, 1) for t in terms] + list(out)
        else:
            out, terms = halves(terms, 1, x) if axis == "x" else halves(terms, 3, blk)
            out = yield [(to_x if axis == "x" else swap_pair, out)]
            terms = terms + list(out)
    total = summed_low(terms).reshape(rows // 8, columns // 2)
    mine = piece(total, 0, core, rows // 16)
    theirs = piece(total, 0, 1 - core, rows // 16)
    from_blk, from_core, from_both = yield [
        (swap_pair, mine),
        (to_core, theirs),
        (to_core_blk, theirs),
    ]
    near = in_order(blk, mine, from_blk, 1).astype(jnp.float32)
    far = in_order(blk, from_core, from_both, 1).astype(jnp.float32)
    left, right = jnp.where(core == 0, near, far), jnp.where(core == 0, far, near)
    results, first = [], 0
    for _, rights in products:
        for whole_wide in [r.shape[1] for r in rights]:
            blocks = []
            for _ in range(0, whole_wide, min(whole_wide, D)):
                wide = min(whole_wide, D) // 2
                blocks += [left[:, first : first + wide], right[:, first : first + wide]]
                first += wide
            results.append(jnp.concatenate(blocks, axis=1))
    return results


def over_batch(array):
    return lax.psum_scatter(array, "batch", scatter_dimension=0, tiled=True)


def whole_reduce(products, small=None):
    if not on_small_slice():
        yield []
        grads = [shared_out(weight_grad(left, r)) for left, rights in products for r in rights]
        grad = jnp.concatenate(grads, axis=1)
        return grad if small is None else (grad, shared_out(small[0], 1), shared_out(small[1]))
    extra = ()
    if small is not None:
        columns = jnp.concatenate([small[0].T, small[1].reshape(D, -1)], axis=1)
        columns = jnp.pad(columns, ((0, 0), (0, PAIR - columns.shape[1])))
        extra = (columns.astype(jnp.bfloat16),)
    if len(products) == 1:
        grad = weight_grad(products[0][0], products[0][1][0]).astype(jnp.bfloat16)
    else:
        (grad,) = joined_grads(products, False, extra)
    (part,) = yield [(over_batch, grad)]
    (got,) = yield [(swap_pair, part)]
    total = part.astype(jnp.float32) + got.astype(jnp.float32)
    if small is None:
        return total
    total, columns, count = total[:, :-PAIR], total[:, -PAIR:], small[0].shape[0]
    bias = columns[:, count : count + small[1].shape[0] // D]
    return total, columns[:, :count].T, bias.reshape(-1)


def batch_sender(bit):
    return lambda array: lax.ppermute(array, "batch", [(n, n ^ bit) for n in range(16)])


def total_of_all(array):
    for send in (to_core, to_x, swap_pair, batch_sender(4), batch_sender(8)):
        (got,) = yield [(send, array)]
        array = array + got
    return array


def small_gather(gains, shifts, bias):
    packed = jnp.concatenate([gains, shifts, bias.reshape(-1, gains.shape[1])], axis=0)
    place = jnp.arange(16)[:, None, None] == lax.axis_index("batch")
    held = jnp.where(place, packed[None], jnp.zeros_like(packed)[None])
    for bit in (1, 2, 4, 8):
        (got,) = yield [(batch_sender(bit), held)]
        held = held + got
    rows = jnp.moveaxis(held[:, :7], 0, 1).reshape(7, -1)
    return rows[:3], rows[3:], held[:, 7:].reshape(-1)


def rows_in_steps(array):
    if lax.axis_size("blk") != 2:
        yield []
        return rows_in(array)
    here = array.shape[0] // 2
    parts = array.reshape((2, here) + array.shape[1:])
    me = lax.axis_index("blk")
    (got,) = yield [(swap_pair, lax.dynamic_index_in_dim(parts, 1 - me, 0, keepdims=False))]
    return in_order(me, lax.dynamic_index_in_dim(parts, me, 0, keepdims=False), got, 1)


def rows_out_steps(array, kind):
    if lax.axis_size("blk") != 2:
        yield []
        return rows_out(array, kind)
    here, length = array.shape[:2]
    parts = array.reshape((here, 2, length // 2) + array.shape[2:])
    me = lax.axis_index("blk")
    sent = lax.dynamic_index_in_dim(parts, 1 - me, 1, keepdims=False).astype(jnp.bfloat16)
    (got,) = yield [(swap_pair, sent)]
    kept = lax.dynamic_index_in_dim(parts, me, 1, keepdims=False).astype(kind)
    return in_order(me, kept, got.astype(kind), 0)


def plain_gather(shards):
    yield []
    return [gathered(s) for s in shards]


def plain_small_gather(gains, shifts, bias):
    yield []
    return gathered(gains, 1), gathered(shifts, 1), gathered(bias)


def plain_reduce(products):
    yield []
    return [
        shared_out(weight_grad(left, right)) for left, rights in products for right in rights
    ]


def on_small_slice():
    return lax.axis_size("batch") == 16 and lax.axis_size("blk") == 2


def start_gather(shards, path):
    return Flight(weight_gather(shards, path) if on_small_slice() else plain_gather(shards))


def whole_gather(shard):
    (full,) = yield [(gathered, shard)]
    return [full]


def start_whole_gather(shard):
    return Flight(whole_gather(shard))


def start_reduce(products, path):
    return Flight(gradient_reduce(products, path) if on_small_slice() else plain_reduce(products))


def start_small(gains, shifts, bias):
    steps = small_gather if on_small_slice() else plain_small_gather
    return Flight(steps(gains, shifts, bias))


def small_reduce(rows, bias):
    if not on_small_slice():
        yield []
        return shared_out(rows, 1), shared_out(bias)
    packed = yield from total_of_all(jnp.concatenate([rows, bias.reshape(-1, D)], axis=0))
    me = lax.axis_index("batch")
    bias = packed[rows.shape[0] :].reshape(-1)
    return (
        piece(packed[: rows.shape[0]], 1, me, D // 16),
        piece(bias, 0, me, bias.shape[0] // 16),
    )


def each_row(function, rows, arrays):
    if rows == 1:
        return function(*arrays)

    def cut(array, n):
        size = array.shape[0] // rows
        return array[n * size : (n + 1) * size]

    results = [function(*(cut(a, n) for a in arrays)) for n in range(rows)]
    return [jnp.concatenate(group, axis=0) for group in zip(*results)]


def dot32(left, right):
    return jnp.dot(left, right, preferred_element_type=jnp.float32)


def whole_row_device(
    inputs,
    memory,
    target_ids,
    memory_ids,
    cotangent,
    w_self_qkv,
    w_self_out,
    w_cross_q,
    w_cross_kv,
    w_cross_out,
    w_up,
    w_down,
    b_up,
    gains,
    shifts,
):
    low = jnp.bfloat16
    half = NH // 4
    shard_rows = w_self_qkv.shape[0]
    columns = [w_self_qkv, w_self_out, w_cross_q, w_cross_kv, w_cross_out]
    columns += [gains.T, shifts.T, b_up.reshape(shard_rows, -1)]
    spare = -sum(c.shape[1] for c in columns) % PAIR
    columns.append(jnp.zeros((shard_rows, spare), low))
    attn_full = gathered(jnp.concatenate(columns, axis=1))
    at, fulls = 0, []
    for wide in [D] * 8 + [c.shape[1] for c in columns[5:8]]:
        fulls.append(attn_full[:, at : at + wide])
        at += wide
    qkv_full, (mk_full, mv_full) = fulls[:3], fulls[5:7]
    out_block, cross_q_block, cross_out_block = (column_block(attn_full, n) for n in (3, 4, 7))
    norms = jnp.concatenate([fulls[8].T, fulls[9].T, jnp.zeros((1, D), low)], axis=0)
    norms = norms.astype(jnp.float32)
    bias_full = fulls[10].reshape(-1).astype(jnp.float32)
    up_parts = [w_up[:, n : n + D] for n in range(0, w_up.shape[1], D)]
    down_rows = w_down.shape[0]
    ffn_shard = jnp.concatenate(up_parts + [w_down, jnp.zeros((8, D), low)], axis=0)
    ffn_full = lax.all_gather(ffn_shard, "batch", axis=0)
    x_rows = Flight(rows_in_steps(inputs))
    ids = Flight(rows_in_steps(jnp.stack([target_ids, memory_ids], axis=2)))
    memory = tick(memory, x_rows, ids)
    memory_rows = Flight(rows_in_steps(memory))
    cotangent = tick(cotangent, x_rows, ids, memory_rows)
    cot_rows = Flight(rows_in_steps(cotangent))
    x_rows = x_rows.finish()
    rows, length = x_rows.shape[:2]
    x_flat = lax.optimization_barrier(x_rows.reshape(-1, D))
    ids = ids.finish()
    target_flat = ids[:, :, 0].reshape(-1)
    memory_id_flat = ids[:, :, 1].reshape(-1)
    memory_flat = lax.optimization_barrier(memory_rows.finish().reshape(-1, D))
    full = jnp.float32

    def self_forward(q, k, v, id_row, pairs):
        fq, fk = document_features(id_row, id_row)
        return attention_forward(q, k, v, fq, fk, True, pairs)

    qkv = [dot32(x_flat, w).astype(low) for w in qkv_full]
    mixed_flat, self_lse = each_row(
        functools.partial(self_forward, pairs=(0, 2 * half)), rows, (*qkv, target_flat)
    )
    first_sum, first, first_low, cross_queries = row_tiles(
        first_norm_kernel,
        "first_norm",
        [mixed_flat, x_flat],
        [out_block, cross_q_block, small_block(norms)],
        [full, full, low, low],
    )
    cross_queries = tick(cross_queries, cot_rows)
    memory_keys = dot32(memory_flat, mk_full).astype(low)
    memory_values = dot32(memory_flat, mv_full).astype(low)

    def cross_forward(q, k, v, id_row, memory_id_row, pairs):
        fq, fk = document_features(id_row, memory_id_row)
        return attention_forward(q, k, v, fq, fk, False, pairs)

    arrays = (cross_queries, memory_keys, memory_values, target_flat, memory_id_flat)
    mixed = each_row(functools.partial(cross_forward, pairs=(0, 2 * half)), rows, arrays)
    cross_flat, cross_lse = tick(mixed, cot_rows)
    second_sum, second, second_low = row_tiles(
        second_norm_kernel,
        "second_norm",
        [cross_flat, first],
        [cross_out_block, small_block(norms)],
        [full, full, low],
    )
    hidden_low, slope = gelu_rows(second_low, ffn_full, bias_full)
    cot_flat = cot_rows.finish().reshape(-1, D)
    ffn_block = (ffn_full.shape[0], down_rows, D)
    result, d_third, d_branch_three, third_sums = row_tiles(
        third_norm_kernel,
        "third_norm",
        [hidden_low, second, cot_flat],
        [(ffn_full, ffn_block, (0, 1, 0)), small_block(norms)],
        [low, full, low],
        True,
    )

    output = Flight(rows_out_steps(result.reshape(rows, length, D), low))
    down_grad = Flight(whole_reduce([(hidden_low, [d_branch_three])]))
    d_branch_three, d_third = tick((d_branch_three, d_third), output, down_grad)
    d_pre, grad_bias_up = gelu_back_rows(d_branch_three, ffn_full, slope)
    up_grad = start_reduce([(second_low, [d_pre])], "xyz")
    d_pre = tick(d_pre, up_grad)
    d_second_sum, d_branch_two, d_cross, second_sums = row_tiles(
        second_back_kernel,
        "second_back",
        [d_pre, d_third, second_sum],
        [(ffn_full, ffn_block, (0, 0, 0)), cross_out_block, small_block(norms)],
        [full, low, low],
        True,
    )
    d_branch_two, d_cross = tick((d_branch_two, d_cross), up_grad)

    def cross_backward(id_row, memory_id_row, *arrays, pairs):
        fq, fk = document_features(id_row, memory_id_row)
        return attention_backward(fq, fk, *arrays, False, pairs)

    arrays = (target_flat, memory_id_flat, cross_queries, memory_keys, memory_values)
    arrays += (cross_flat, cross_lse, d_cross)
    grads = each_row(functools.partial(cross_backward, pairs=(0, 2 * half)), rows, arrays)
    d_cross_low, d_memory_keys, d_memory_values = tick(grads, output, up_grad)
    d_first_sum, d_branch_one, d_self, first_sums = row_tiles(
        first_back_kernel,
        "first_back",
        [d_cross_low, d_second_sum, first_sum],
        [cross_q_block, out_block, small_block(norms)],
        [full, low, low],
        True,
    )
    every = [first_sums[0], second_sums[0], third_sums[0]]
    grad_rows = every + [first_sums[1], second_sums[1], third_sums[1], third_sums[2]]
    cross_grad = Flight(
        whole_reduce(
            [
                (memory_flat, [d_memory_keys, d_memory_values]),
                (first_low, [d_cross_low]),
                (cross_flat, [d_branch_two]),
                (mixed_flat, [d_branch_one]),
            ],
            (jnp.stack(grad_rows), grad_bias_up),
        )
    )
    d_self = tick(d_self, cross_grad, up_grad)
    d_memory = back_prod(d_memory_keys, mk_full) + back_prod(d_memory_values, mv_full)
    d_self, d_memory = lax.optimization_barrier((d_self, d_memory))
    d_memory = Flight(rows_out_steps(d_memory.reshape(rows, length, D), jnp.float32))
    d_self = tick(d_self, down_grad, d_memory)

    def self_backward(id_row, *arrays, pairs):
        fq, fk = document_features(id_row, id_row)
        return attention_backward(fq, fk, *arrays, True, pairs)

    arrays = (target_flat, *qkv, mixed_flat, self_lse, d_self)
    grads_a = each_row(functools.partial(self_backward, pairs=(0, half)), rows, arrays)
    grads_a = tick(grads_a, up_grad, down_grad)
    early_grad = start_reduce([(x_flat, grads_a)], "xzy")
    d_self = tick(d_self, early_grad, d_memory)
    arrays = (target_flat, *qkv, mixed_flat, self_lse, d_self)
    grads_b = each_row(functools.partial(self_backward, pairs=(half, half)), rows, arrays)
    grads_b = tick(grads_b, early_grad, up_grad)
    d_input = ALPHA * d_first_sum
    for grad_a, grad_b, weight in zip(grads_a, grads_b, qkv_full):
        d_input = d_input + back_prod(jnp.concatenate([grad_a, grad_b], axis=1), weight)
    d_input = Flight(rows_out_steps(d_input.reshape(rows, length, D), jnp.float32))
    grads_b = tick(grads_b, d_input)
    late_grad = start_reduce([(x_flat, grads_b)], "xzy")
    token = tick(grads_b[0], late_grad, early_grad)
    token = tick(token, late_grad)
    flights = [late_grad, early_grad, d_input, cross_grad]
    while any(f.result is None for f in flights):
        token = tick(token, *flights)
    grads, grad_rows, grad_bias_up = cross_grad.finish()
    grad_kv, grad_cross_q, grad_cross_out, grad_self_out = jnp.split(
        grads, [2 * D, 3 * D, 4 * D], axis=1
    )
    grad_qa, grad_ka, grad_va = early_grad.finish()
    grad_qb, grad_kb, grad_vb = late_grad.finish()
    return (
        output.finish(),
        d_input.finish(),
        d_memory.finish(),
        jnp.concatenate([grad_qa, grad_qb, grad_ka, grad_kb, grad_va, grad_vb], axis=1),
        grad_self_out,
        grad_cross_q,
        grad_kv,
        grad_cross_out,
        up_grad.finish()[0],
        down_grad.finish(),
        grad_bias_up,
        grad_rows[:3],
        grad_rows[3:],
    )


def per_device(inputs, *others):
    if inputs.shape[0] % lax.axis_size("blk") == 0:
        return whole_row_device(inputs, *others)
    return split_row_device(inputs, *others)


def solution(mesh):
    return jax.shard_map(
        per_device,
        mesh=mesh,
        in_specs=(
            P("batch", "blk", None),
            P("batch", "blk", None),
            P("batch", "blk"),
            P("batch", "blk"),
            P("batch", "blk", None),
            P("batch", None),
            P("batch", None),
            P("batch", None),
            P("batch", None),
            P("batch", None),
            P("batch", None),
            P("batch", None),
            P("batch"),
            P(None, "batch"),
            P(None, "batch"),
        ),
        out_specs=(
            P("batch", "blk", None),
            P("batch", "blk", None),
            P("batch", "blk", None),
            P("batch", None),
            P("batch", None),
            P("batch", None),
            P("batch", None),
            P("batch", None),
            P("batch", None),
            P("batch", None),
            P("batch"),
            P(None, "batch"),
            P(None, "batch"),
        ),
        check_vma=False,
    )
```

```python
import functools

import jax
import jax.numpy as jnp
from jax import lax
from jax.experimental import pallas as pl
from jax.experimental.pallas import tpu as pltpu
from jax.sharding import PartitionSpec as P

D = 1024
NH = 16
HD = 64
MB_ROWS = 1
MICRO = 2
ALPHA = 300.0**0.25
MASKED = -1e30
EPSILON = 1e-05
PAIR = 2 * HD
MASK_STEP = -(2.0**100)


def nt(left, right):
    return lax.dot_general(left, right, (((1,), (1,)), ((), ())), preferred_element_type=jnp.float32)


def nn(left, right):
    return lax.dot_general(left, right, (((1,), (0,)), ((), ())), preferred_element_type=jnp.float32)


def lane_of(rows):
    return lax.broadcasted_iota(jnp.int32, (rows, PAIR), 1)


def attention_fwd_kernel(causal, q_ref, k_ref, v_ref, fq_ref, fk_ref, out_ref, lse_ref):
    block = 256
    length = q_ref.shape[0]
    mem = k_ref.shape[0]
    low_q = lane_of(length) < HD
    low_k = lane_of(mem) < HD
    q = q_ref[...] * jnp.bfloat16(HD**-0.5)
    k = k_ref[...]
    v = v_ref[...]
    fq = fq_ref[...]
    fk = fk_ref[...]
    ones = jnp.ones_like(v)
    queries = (jnp.where(low_q, q, fq), jnp.where(low_q, fq, q))
    keys = (jnp.where(low_k, k, fk), jnp.where(low_k, fk, k))
    values = (jnp.where(low_k, v, ones), jnp.where(low_k, ones, v))
    low_blk = lane_of(block) < HD
    units = [(i, h) for i in range(length // block) for h in range(2)]

    def score(unit):
        i, h = unit
        seen = (i + 1) * block if causal else mem
        scores = nt(queries[h][i * block : (i + 1) * block], keys[h][:seen])
        if causal:
            tri = lax.broadcasted_iota(jnp.int32, (block, block), 0) >= lax.broadcasted_iota(
                jnp.int32, (block, block), 1
            )
            diag = jnp.where(tri, scores[:, seen - block :], MASK_STEP)
            scores = diag if i == 0 else jnp.concatenate([scores[:, : seen - block], diag], axis=1)
        return scores

    ahead = score(units[0])
    accs, peaks = [], []
    for n, (i, h) in enumerate(units):
        rows = slice(i * block, (i + 1) * block)
        scores = ahead
        if n + 1 < len(units):
            ahead = score(units[n + 1])
        peak = jnp.max(scores, axis=1, keepdims=True)
        raised = jnp.exp(scores - peak).astype(jnp.bfloat16)
        accs.append(nn(raised, values[h][: scores.shape[1]]))
        peaks.append(peak)
        if h == 1:
            total = pltpu.roll(jnp.where(low_blk, accs[1], accs[0]), HD, 1)
            out_ref[rows, :] = (jnp.where(low_blk, accs[0], accs[1]) / total).astype(out_ref.dtype)
            lse_ref[rows, :] = jnp.where(low_blk, peaks[0], peaks[1]) + jnp.log(total)
            accs, peaks = [], []


def split3(value):
    hi = value.astype(jnp.bfloat16)
    rest = value - hi.astype(jnp.float32)
    mid = rest.astype(jnp.bfloat16)
    lo = (rest - mid.astype(jnp.float32)).astype(jnp.bfloat16)
    return hi, mid, lo


def placed(lane, start, pieces, other):
    for n, piece in enumerate(pieces):
        other = jnp.where(lane == start + n, piece, other)
    return other


def attention_bwd_kernel(causal, q_ref, k_ref, v_ref, fq_ref, fk_ref, out_ref, lse_ref, do_ref, dq_ref, dk_ref, dv_ref, dk_acc, dv_acc, dq_acc):
    block = 256 if causal else 512
    length = q_ref.shape[0]
    mem = k_ref.shape[0]
    lane_q = lane_of(length)
    lane_k = lane_of(mem)
    low_q = lane_q < HD
    low_k = lane_k < HD
    scale = jnp.bfloat16(HD**-0.5)
    q = q_ref[...] * scale
    k = k_ref[...]
    v = v_ref[...]
    do = do_ref[...]
    fq = fq_ref[...]
    fk = fk_ref[...]
    zero_q = jnp.zeros_like(q)
    zero_k = jnp.zeros_like(k)
    one_k = jnp.ones_like(k)
    prod = do.astype(jnp.float32) * out_ref[...].astype(jnp.float32)
    sum_a = jnp.sum(jnp.where(low_q, prod, 0.0), axis=1, keepdims=True)
    sum_b = jnp.sum(jnp.where(low_q, 0.0, prod), axis=1, keepdims=True)
    inner = jnp.where(low_q, sum_b, sum_a)
    lse = pltpu.roll(lse_ref[...], HD, 1)
    half_q = lane_q & (HD - 1)
    half_k = lane_k & (HD - 1)
    fq = placed(half_q, 2, split3(-lse), fq)
    fk = jnp.where((half_k >= 2) & (half_k < 5), one_k, fk)
    fd = placed(half_q, 0, split3(-inner), zero_q)
    fv = jnp.where(half_k < 3, one_k, zero_k)
    queries = (jnp.where(low_q, q, fq), jnp.where(low_q, fq, q))
    keys = (jnp.where(low_k, k, fk), jnp.where(low_k, fk, k))
    grads = (jnp.where(low_q, do, fd), jnp.where(low_q, fd, do))
    values = (jnp.where(low_k, v, fv), jnp.where(low_k, fv, v))
    plain_q = (jnp.where(low_q, q, zero_q), jnp.where(low_q, zero_q, q))
    plain_do = (jnp.where(low_q, do, zero_q), jnp.where(low_q, zero_q, do))
    k_t = k.T
    units = [(i, h) for i in range(length // block) for h in range(2)]

    def scores_of(unit):
        i, h = unit
        rows = slice(i * block, (i + 1) * block)
        seen = (i + 1) * block if causal else mem
        return nt(keys[h][:seen], queries[h][rows]), nt(values[h][:seen], grads[h][rows])

    ahead = scores_of(units[0])
    dv = dk = None
    for n, (i, h) in enumerate(units):
        rows = slice(i * block, (i + 1) * block)
        seen = (i + 1) * block if causal else mem
        s, dp = ahead
        if n + 1 < len(units):
            ahead = scores_of(units[n + 1])
        p = jnp.exp(s)
        if causal:
            tri = lax.broadcasted_iota(jnp.int32, (block, block), 0) <= lax.broadcasted_iota(
                jnp.int32, (block, block), 1
            )
            diag = jnp.where(tri, p[seen - block :], 0.0)
            p = diag if i == 0 else jnp.concatenate([p[: seen - block], diag], axis=0)
        ds = (p * dp).astype(jnp.bfloat16)
        dq_acc[h * HD : (h + 1) * HD, rows] = nn(k_t[h * HD : (h + 1) * HD, :seen], ds)
        dv_part = nn(p.astype(jnp.bfloat16), plain_do[h][rows])
        dk_part = nn(ds, plain_q[h][rows])
        if n == 0:
            dv_acc[:seen] = dv_part
            dk_acc[:seen] = dk_part
            if seen < mem:
                dv_acc[seen:] = jnp.zeros((mem - seen, PAIR), jnp.float32)
                dk_acc[seen:] = jnp.zeros((mem - seen, PAIR), jnp.float32)
        else:
            dv_acc[:seen] += dv_part
            dk_acc[:seen] += dk_part
    dq_ref[...] = (dq_acc[...].T * (HD**-0.5)).astype(dq_ref.dtype)
    dk_ref[...] = dk_acc[...].astype(dk_ref.dtype)
    dv_ref[...] = dv_acc[...].astype(dv_ref.dtype)


def cols(length, first):
    return pl.BlockSpec((length, PAIR), lambda j: (0, first + j))


def whole(length):
    return pl.BlockSpec((length, PAIR), lambda j: (0, 0))


SHORT = pl.CostEstimate(flops=1024, bytes_accessed=1024, transcendentals=0)


def attention_call(kernel, name, pairs, causal, arrays, shared, lengths, kinds, scratch):
    first, count = pairs

    return pl.pallas_call(
        functools.partial(kernel, causal),
        grid=(count,),
        in_specs=[cols(a.shape[0], first) for a in arrays[:3]]
        + [whole(a.shape[0]) for a in shared]
        + [cols(a.shape[0], first) for a in arrays[3:]],
        out_specs=[cols(n, 0) for n in lengths],
        out_shape=[
            jax.ShapeDtypeStruct((n, count * PAIR), kind) for n, kind in zip(lengths, kinds)
        ],
        scratch_shapes=scratch,
        compiler_params=pltpu.CompilerParams(vmem_limit_bytes=48 * 2**20),
        cost_estimate=SHORT,
        name=name,
    )(*arrays[:3], *shared, *arrays[3:])


def attention_forward(queries, keys, values, fq, fk, causal, pairs):
    lengths = (queries.shape[0],) * 2
    kinds = (jnp.bfloat16, jnp.float32)
    arrays, shared = (queries, keys, values), (fq, fk)
    return attention_call(
        attention_fwd_kernel, "attention_forward", pairs, causal, arrays, shared, lengths, kinds, []
    )


def attention_backward(fq, fk, queries, keys, values, mixed, lse, d_mixed, causal, pairs):
    length, mem = queries.shape[0], keys.shape[0]
    scratch = [
        pltpu.VMEM((mem, PAIR), jnp.float32),
        pltpu.VMEM((mem, PAIR), jnp.float32),
        pltpu.VMEM((PAIR, length), jnp.float32),
    ]
    return attention_call(
        attention_bwd_kernel,
        "attention_backward",
        pairs,
        causal,
        (queries, keys, values, mixed, lse, d_mixed),
        (fq, fk),
        (length, mem, mem),
        (jnp.bfloat16,) * 3,
        scratch,
    )


def gelu_kernel(left_ref, right_ref, bias_ref, hidden_ref, slope_ref):
    slope_in = 0.7978845608028654
    right = right_ref[...].reshape(-1, right_ref.shape[-1])
    bias = bias_ref[...]
    step = min(256, left_ref.shape[0])
    for first in range(0, left_ref.shape[0], step):
        rows = slice(first, first + step)
        pre = nn(left_ref[rows, :], right) + bias
        square = pre * pre
        bent = jnp.tanh(slope_in * (pre + 0.044715 * (square * pre)))
        gate = 0.5 * (1.0 + bent)
        hidden_ref[rows, :] = (pre * gate).astype(hidden_ref.dtype)
        bend = (1.0 - bent * bent) * (slope_in + (slope_in * 0.134145) * square)
        slope_ref[rows, :] = gate + (0.5 * pre) * bend


def gelu_rows(left, ffn, bias):
    rows, inner = left.shape
    count, wide = ffn.shape[0], ffn.shape[2]
    tall_shard = inner // count
    columns = bias.shape[0]
    tall = min(rows, 1024)
    return pl.pallas_call(
        gelu_kernel,
        grid=(rows // tall, columns // wide),
        in_specs=[
            pl.BlockSpec((tall, inner), lambda i, j: (i, 0)),
            pl.BlockSpec((count, tall_shard, wide), lambda i, j: (0, j, 0)),
            pl.BlockSpec((1, wide), lambda i, j: (0, j)),
        ],
        out_specs=[pl.BlockSpec((tall, wide), lambda i, j: (i, j))] * 2,
        out_shape=[
            jax.ShapeDtypeStruct((rows, columns), jnp.bfloat16),
            jax.ShapeDtypeStruct((rows, columns), jnp.float32),
        ],
        compiler_params=pltpu.CompilerParams(vmem_limit_bytes=56 * 2**20),
        cost_estimate=SHORT,
        name="gelu_rows",
    )(left, ffn, bias.reshape(1, columns))


def spread_rows(summed):
    centred = summed - jnp.mean(summed, axis=1, keepdims=True)
    scale = lax.rsqrt(jnp.mean(centred * centred, axis=1, keepdims=True) + EPSILON)
    return centred * scale, scale


def norm_back(unit, scale, gain, grad):
    inner = grad * gain
    lean = jnp.mean(inner, axis=1, keepdims=True)
    tilt = jnp.mean(inner * unit, axis=1, keepdims=True)
    return scale * (inner - lean - unit * tilt)


def add_column_sums(ref, terms):
    rows = [jnp.sum(t, axis=0, keepdims=True) for t in terms]
    rows.append(jnp.zeros((ref.shape[0] - len(rows), ref.shape[1]), jnp.float32))
    part = jnp.concatenate(rows, axis=0)

    @pl.when(pl.program_id(0) == 0)
    def _():
        ref[...] = part

    @pl.when(pl.program_id(0) > 0)
    def _():
        ref[...] += part


def row_tiles(kernel, name, tiled, fixed, outs, sums=False):
    rows = tiled[0].shape[0]
    tall = min(rows, 256)
    in_specs = [pl.BlockSpec((tall, a.shape[1]), lambda i: (i, 0)) for a in tiled]
    for _, block, index in fixed:
        in_specs.append(
            pl.BlockSpec(block, lambda i, at=index: at, pipeline_mode=pl.Buffered(1))
        )
    out_specs = [pl.BlockSpec((tall, D), lambda i: (i, 0)) for _ in outs]
    out_shape = [jax.ShapeDtypeStruct((rows, D), kind) for kind in outs]
    if sums:
        out_specs.append(pl.BlockSpec((8, D), lambda i: (0, 0)))
        out_shape.append(jax.ShapeDtypeStruct((8, D), jnp.float32))
    return pl.pallas_call(
        kernel,
        grid=(rows // tall,),
        in_specs=in_specs,
        out_specs=out_specs,
        out_shape=out_shape,
        compiler_params=pltpu.CompilerParams(vmem_limit_bytes=56 * 2**20),
        cost_estimate=SHORT,
        name=name,
    )(*tiled, *[array for array, _, _ in fixed])


def column_block(attn_full, block):
    return (attn_full, (D, D), (0, block))


def small_block(norms):
    return (norms, norms.shape, (0, 0))


def first_norm_kernel(mixed, x, out_w, cross_w, norms, sum_ref, normed_ref, low_ref, query_ref):
    summed = ALPHA * x[...].astype(jnp.float32) + nn(mixed[...], out_w[...])
    sum_ref[...] = summed
    normed = spread_rows(summed)[0] * norms[0:1, :] + norms[3:4, :]
    normed_ref[...] = normed
    low = normed.astype(jnp.bfloat16)
    low_ref[...] = low
    query_ref[...] = nn(low, cross_w[...]).astype(jnp.bfloat16)


def second_norm_kernel(mixed, first, out_w, norms, sum_ref, normed_ref, low_ref):
    summed = ALPHA * first[...] + nn(mixed[...], out_w[...])
    sum_ref[...] = summed
    normed = spread_rows(summed)[0] * norms[1:2, :] + norms[4:5, :]
    normed_ref[...] = normed
    low_ref[...] = normed.astype(jnp.bfloat16)


def third_norm_kernel(hidden, second, cot, down, norms, out_ref, grad_ref, low_ref, sums_ref):
    right = down[...].reshape(-1, down.shape[-1])
    summed = ALPHA * second[...] + nn(hidden[...], right) + norms[6:7, :]
    unit, scale = spread_rows(summed)
    out_ref[...] = (unit * norms[2:3, :] + norms[5:6, :]).astype(jnp.bfloat16)
    cotangent = cot[...].astype(jnp.float32)
    grad = norm_back(unit, scale, norms[2:3, :], cotangent)
    grad_ref[...] = grad
    low = grad.astype(jnp.bfloat16)
    low_ref[...] = low
    add_column_sums(sums_ref, [cotangent * unit, cotangent, low.astype(jnp.float32)])


def second_back_kernel(
    d_pre, d_third, summed, up, out_w, norms, grad_ref, low_ref, back_ref, sums_ref
):
    wide = up.shape[2]
    tall_shard = D // up.shape[0]
    grad = ALPHA * d_third[...]
    for n in range(up.shape[1] // tall_shard):
        right = up[:, n * tall_shard : (n + 1) * tall_shard].reshape(-1, wide)
        grad += nt(d_pre[:, n * wide : (n + 1) * wide], right)
    unit, scale = spread_rows(summed[...])
    d_sum = norm_back(unit, scale, norms[1:2, :], grad)
    grad_ref[...] = d_sum
    low = d_sum.astype(jnp.bfloat16)
    low_ref[...] = low
    back_ref[...] = nt(low, out_w[...]).astype(jnp.bfloat16)
    add_column_sums(sums_ref, [grad * unit, grad])


def first_back_kernel(
    d_query, d_second, summed, cross_w, out_w, norms, grad_ref, low_ref, back_ref, sums_ref
):
    grad = ALPHA * d_second[...] + nt(d_query[...], cross_w[...])
    unit, scale = spread_rows(summed[...])
    d_sum = norm_back(unit, scale, norms[0:1, :], grad)
    grad_ref[...] = d_sum
    low = d_sum.astype(jnp.bfloat16)
    low_ref[...] = low
    back_ref[...] = nt(low, out_w[...]).astype(jnp.bfloat16)
    add_column_sums(sums_ref, [grad * unit, grad])


def gelu_back_kernel(left_ref, right_ref, slope_ref, out_ref, sum_ref):
    right = right_ref[...].reshape(-1, right_ref.shape[-1])
    step = min(512, left_ref.shape[0])
    total = None
    for first in range(0, left_ref.shape[0], step):
        rows = slice(first, first + step)
        d_hidden = nt(left_ref[rows, :], right).astype(jnp.bfloat16).astype(jnp.float32)
        d_pre = (d_hidden * slope_ref[rows, :]).astype(jnp.bfloat16)
        out_ref[rows, :] = d_pre
        part = jnp.sum(d_pre.astype(jnp.float32), axis=0, keepdims=True)
        total = part if total is None else total + part
    sum_ref[...] = total[None]


def gelu_back_rows(left, ffn, slope):
    rows, inner = left.shape
    count, columns = ffn.shape[0], slope.shape[1]
    tall, group = min(rows, 1024), 4
    wide = columns // count * group
    out, sums = pl.pallas_call(
        gelu_back_kernel,
        grid=(rows // tall, columns // wide),
        in_specs=[
            pl.BlockSpec((tall, inner), lambda i, j: (i, 0)),
            pl.BlockSpec((group, columns // count, inner), lambda i, j: (j, 1, 0)),
            pl.BlockSpec((tall, wide), lambda i, j: (i, j)),
        ],
        out_specs=[
            pl.BlockSpec((tall, wide), lambda i, j: (i, j)),
            pl.BlockSpec((1, 1, wide), lambda i, j: (i, 0, j)),
        ],
        out_shape=[
            jax.ShapeDtypeStruct((rows, columns), jnp.bfloat16),
            jax.ShapeDtypeStruct((rows // tall, 1, columns), jnp.float32),
        ],
        compiler_params=pltpu.CompilerParams(vmem_limit_bytes=48 * 2**20),
        cost_estimate=SHORT,
        name="gelu_back_rows",
    )(left, ffn, slope)
    return out, jnp.sum(sums, axis=(0, 1))


def document_features(query_ids, key_ids):
    half = jnp.arange(PAIR, dtype=jnp.int32)[None, :] % HD
    fq = (half == query_ids[:, None]).astype(jnp.bfloat16)
    fk = jnp.where((half < 2) & (half != key_ids[:, None]), MASK_STEP, 0.0).astype(jnp.bfloat16)
    return fq, fk


def shortened(array):
    return jax.tree.map(lambda a: a.astype(jnp.bfloat16) if a.dtype == jnp.float32 else a, array)


def layer_norm(summed, gain_row, shift_row):
    average = jnp.mean(summed, axis=-1, keepdims=True)
    centred = summed - average
    spread = jnp.mean(centred * centred, axis=-1, keepdims=True)
    return centred * lax.rsqrt(spread + EPSILON) * gain_row + shift_row


def split_heads(array_in):
    return array_in.reshape(array_in.shape[0], array_in.shape[1], NH, HD)


def weight_grad(left_rows, right_rows):
    return jnp.einsum("tk,tn->kn", left_rows, right_rows, preferred_element_type=jnp.float32)


def back_prod(grad_rows, matrix):
    return jnp.einsum("tn,kn->tk", grad_rows, matrix, preferred_element_type=jnp.float32)


def attention_scores(queries, key_rows, allowed):
    scores = jnp.einsum(
        "rqhd,rkhd->rhqk",
        split_heads(queries),
        split_heads(key_rows),
        preferred_element_type=jnp.float32,
    ) * HD ** (-0.5)
    return jnp.where(allowed[:, None], scores, MASKED)


def plain_attention_forward(queries, key_rows, value_rows, allowed):
    scores = attention_scores(queries, key_rows, allowed)
    row_peak = jnp.max(scores, axis=-1, keepdims=True)
    raised = jnp.exp(scores - row_peak)
    row_total = jnp.sum(raised, axis=-1, keepdims=True)
    probabilities = (raised / row_total).astype(jnp.bfloat16)
    attended = jnp.einsum(
        "rhqk,rkhd->rqhd",
        probabilities,
        split_heads(value_rows),
        preferred_element_type=jnp.float32,
    )
    return (attended.reshape(queries.shape).astype(jnp.bfloat16), row_peak, row_total)


def plain_attention_backward(queries, key_rows, value_rows, allowed, row_peak, row_total, d_attended):
    scores = attention_scores(queries, key_rows, allowed)
    probabilities = jnp.exp(scores - row_peak) / row_total
    d_heads = split_heads(d_attended)
    d_values = jnp.einsum(
        "rhqk,rqhd->rkhd",
        probabilities.astype(jnp.bfloat16),
        d_heads,
        preferred_element_type=jnp.float32,
    )
    d_probs = jnp.einsum(
        "rqhd,rkhd->rhqk", d_heads, split_heads(value_rows), preferred_element_type=jnp.float32
    )
    inner_sum = jnp.sum(probabilities * d_probs, axis=-1, keepdims=True)
    d_scores = (probabilities * (d_probs - inner_sum)).astype(jnp.bfloat16)
    d_queries = jnp.einsum(
        "rhqk,rkhd->rqhd", d_scores, split_heads(key_rows), preferred_element_type=jnp.float32
    ) * HD ** (-0.5)
    d_keys = jnp.einsum(
        "rhqk,rqhd->rkhd", d_scores, split_heads(queries), preferred_element_type=jnp.float32
    ) * HD ** (-0.5)
    d_pairs = jnp.concatenate(
        [d_keys.reshape(key_rows.shape), d_values.reshape(value_rows.shape)], axis=2
    )
    return (d_queries.reshape(queries.shape), d_pairs)


def add_terms(running, fresh):
    if running is None:
        return fresh
    return tuple((first_term + second_term for first_term, second_term in zip(running, fresh)))


def split_row_device(
    inputs,
    memory,
    target_ids,
    memory_ids,
    cotangent,
    w_self_qkv,
    w_self_out,
    w_cross_q,
    w_cross_kv,
    w_cross_out,
    w_up,
    w_down,
    b_up,
    gains,
    shifts,
):
    tokens_here = inputs.shape[1]
    length = tokens_here * lax.axis_size("blk")
    token_count = MB_ROWS * tokens_here
    query_places = lax.axis_index("blk") * tokens_here + jnp.arange(tokens_here, dtype=jnp.int32)
    key_places = jnp.arange(length, dtype=jnp.int32)
    causal = key_places[None, :] <= query_places[:, None]
    outputs, input_grads, memory_grads = ([], [], [])
    attn_total = None
    ffn_total = None
    for micro_step in range(MICRO):
        row_range = slice(micro_step * MB_ROWS, (micro_step + 1) * MB_ROWS)
        qkv_full, out_full, cross_q_full, cross_kv_full, cross_out_full, gain_low, shift_low = (
            lax.all_gather(w_self_qkv, "batch", axis=0, tiled=True),
            lax.all_gather(w_self_out, "batch", axis=0, tiled=True),
            lax.all_gather(w_cross_q, "batch", axis=0, tiled=True),
            lax.all_gather(w_cross_kv, "batch", axis=0, tiled=True),
            lax.all_gather(w_cross_out, "batch", axis=0, tiled=True),
            lax.all_gather(gains, "batch", axis=1, tiled=True),
            lax.all_gather(shifts, "batch", axis=1, tiled=True),
        )
        gain_full = gain_low.astype(jnp.float32)
        shift_full = shift_low.astype(jnp.float32)
        x_flat = inputs[row_range].reshape(token_count, D)
        memory_flat = memory[row_range].reshape(token_count, D)
        seg_rows = target_ids[row_range]
        memory_seg_rows = memory_ids[row_range]
        projected = (
            jnp.dot(x_flat, qkv_full, preferred_element_type=jnp.float32)
            .astype(jnp.bfloat16)
            .reshape(MB_ROWS, tokens_here, 3 * D)
        )
        self_queries = projected[:, :, :D]
        key_pairs, key_segs = (
            lax.all_gather(projected[:, :, D:], "blk", axis=1, tiled=True),
            lax.all_gather(seg_rows, "blk", axis=1, tiled=True),
        )
        self_allowed = (seg_rows[:, :, None] == key_segs[:, None, :]) & causal[None]
        self_mixed, self_peak, self_total = plain_attention_forward(
            self_queries, key_pairs[:, :, :D], key_pairs[:, :, D:], self_allowed
        )
        mixed_flat = self_mixed.reshape(token_count, D)
        first_sum = ALPHA * x_flat.astype(jnp.float32) + jnp.dot(
            mixed_flat, out_full, preferred_element_type=jnp.float32
        )
        first = layer_norm(first_sum, gain_full[0], shift_full[0])
        first_low = first.astype(jnp.bfloat16)
        cross_queries = (
            jnp.dot(first_low, cross_q_full, preferred_element_type=jnp.float32)
            .astype(jnp.bfloat16)
            .reshape(MB_ROWS, tokens_here, D)
        )
        memory_local = (
            jnp.dot(memory_flat, cross_kv_full, preferred_element_type=jnp.float32)
            .astype(jnp.bfloat16)
            .reshape(MB_ROWS, tokens_here, 2 * D)
        )
        memory_pairs, memory_segs = (
            lax.all_gather(memory_local, "blk", axis=1, tiled=True),
            lax.all_gather(memory_seg_rows, "blk", axis=1, tiled=True),
        )
        cross_allowed = seg_rows[:, :, None] == memory_segs[:, None, :]
        cross_mixed, cross_peak, cross_total = plain_attention_forward(
            cross_queries, memory_pairs[:, :, :D], memory_pairs[:, :, D:], cross_allowed
        )
        cross_flat = cross_mixed.reshape(token_count, D)
        second_sum = ALPHA * first + jnp.dot(
            cross_flat, cross_out_full, preferred_element_type=jnp.float32
        )
        second = layer_norm(second_sum, gain_full[1], shift_full[1])
        second_low = second.astype(jnp.bfloat16)
        up_full, down_full, bias_full = (
            lax.all_gather(w_up, "batch", axis=0, tiled=True),
            lax.all_gather(w_down, "batch", axis=0, tiled=True),
            lax.all_gather(b_up, "batch", axis=0, tiled=True),
        )
        hidden_pre = jnp.dot(
            second_low, up_full, preferred_element_type=jnp.float32
        ) + bias_full.astype(jnp.float32)
        hidden_low = jax.nn.gelu(hidden_pre).astype(jnp.bfloat16)
        third_sum = (
            ALPHA * second
            + jnp.dot(hidden_low, down_full, preferred_element_type=jnp.float32)
            + shift_full[3]
        )
        result, third_back = jax.vjp(layer_norm, third_sum, gain_full[2], shift_full[2])
        outputs.append(result.astype(jnp.bfloat16).reshape(MB_ROWS, tokens_here, D))
        cot_flat = cotangent[row_range].reshape(token_count, D).astype(jnp.float32)
        d_third, d_gain_three, d_shift_three = third_back(cot_flat)
        d_branch_three = d_third.astype(jnp.bfloat16)
        grad_down = weight_grad(hidden_low, d_branch_three)
        grad_bias_down = jnp.sum(d_branch_three.astype(jnp.float32), axis=0)
        d_hidden = back_prod(d_branch_three, down_full).astype(jnp.bfloat16)
        gelu_back = jax.vjp(jax.nn.gelu, hidden_pre)[1]
        d_pre = gelu_back(d_hidden.astype(jnp.float32))[0].astype(jnp.bfloat16)
        grad_up = weight_grad(second_low, d_pre)
        grad_bias_up = jnp.sum(d_pre.astype(jnp.float32), axis=0)
        d_second = ALPHA * d_third + back_prod(d_pre, up_full)
        ffn_terms = (grad_up, grad_down, grad_bias_up)
        ffn_share = (
            lax.psum_scatter(
                ffn_terms[0].astype(jnp.bfloat16), "batch", scatter_dimension=0, tiled=True
            ).astype(jnp.float32),
            lax.psum_scatter(
                ffn_terms[1].astype(jnp.bfloat16), "batch", scatter_dimension=0, tiled=True
            ).astype(jnp.float32),
            lax.psum_scatter(
                ffn_terms[2].astype(jnp.bfloat16), "batch", scatter_dimension=0, tiled=True
            ).astype(jnp.float32),
        )
        ffn_total = add_terms(ffn_total, ffn_share)
        second_back = jax.vjp(layer_norm, second_sum, gain_full[1], shift_full[1])[1]
        d_second_sum, d_gain_two, d_shift_two = second_back(d_second)
        d_branch_two = d_second_sum.astype(jnp.bfloat16)
        grad_cross_out = weight_grad(cross_flat, d_branch_two)
        d_cross = (
            back_prod(d_branch_two, cross_out_full)
            .astype(jnp.bfloat16)
            .reshape(MB_ROWS, tokens_here, D)
        )
        d_cross_queries, d_memory_all = plain_attention_backward(
            cross_queries,
            memory_pairs[:, :, :D],
            memory_pairs[:, :, D:],
            cross_allowed,
            cross_peak,
            cross_total,
            d_cross,
        )
        d_memory_pairs = lax.psum_scatter(
            d_memory_all.astype(jnp.bfloat16), "blk", scatter_dimension=1, tiled=True
        ).reshape(token_count, 2 * D)
        grad_cross_kv = weight_grad(memory_flat, d_memory_pairs)
        memory_grads.append(
            back_prod(d_memory_pairs, cross_kv_full).reshape(MB_ROWS, tokens_here, D)
        )
        d_cross_low = d_cross_queries.astype(jnp.bfloat16).reshape(token_count, D)
        grad_cross_q = weight_grad(first_low, d_cross_low)
        d_first = ALPHA * d_second_sum + back_prod(d_cross_low, cross_q_full)
        first_back = jax.vjp(layer_norm, first_sum, gain_full[0], shift_full[0])[1]
        d_first_sum, d_gain_one, d_shift_one = first_back(d_first)
        d_branch_one = d_first_sum.astype(jnp.bfloat16)
        grad_self_out = weight_grad(mixed_flat, d_branch_one)
        d_self = (
            back_prod(d_branch_one, out_full).astype(jnp.bfloat16).reshape(MB_ROWS, tokens_here, D)
        )
        d_self_queries, d_key_all = plain_attention_backward(
            self_queries,
            key_pairs[:, :, :D],
            key_pairs[:, :, D:],
            self_allowed,
            self_peak,
            self_total,
            d_self,
        )
        d_self_pairs = lax.psum_scatter(
            d_key_all.astype(jnp.bfloat16), "blk", scatter_dimension=1, tiled=True
        )
        d_projected = jnp.concatenate(
            [d_self_queries.astype(jnp.bfloat16), d_self_pairs], axis=2
        ).reshape(token_count, 3 * D)
        grad_self_qkv = weight_grad(x_flat, d_projected)
        input_grads.append(
            (ALPHA * d_first_sum + back_prod(d_projected, qkv_full)).reshape(
                MB_ROWS, tokens_here, D
            )
        )
        grad_gains = jnp.stack([d_gain_one, d_gain_two, d_gain_three])
        grad_shifts = jnp.stack([d_shift_one, d_shift_two, d_shift_three, grad_bias_down])
        attn_terms = (
            grad_self_qkv,
            grad_self_out,
            grad_cross_q,
            grad_cross_kv,
            grad_cross_out,
            grad_gains,
            grad_shifts,
        )
        attn_share = (
            lax.psum_scatter(
                attn_terms[0].astype(jnp.bfloat16), "batch", scatter_dimension=0, tiled=True
            ).astype(jnp.float32),
            lax.psum_scatter(
                attn_terms[1].astype(jnp.bfloat16), "batch", scatter_dimension=0, tiled=True
            ).astype(jnp.float32),
            lax.psum_scatter(
                attn_terms[2].astype(jnp.bfloat16), "batch", scatter_dimension=0, tiled=True
            ).astype(jnp.float32),
            lax.psum_scatter(
                attn_terms[3].astype(jnp.bfloat16), "batch", scatter_dimension=0, tiled=True
            ).astype(jnp.float32),
            lax.psum_scatter(
                attn_terms[4].astype(jnp.bfloat16), "batch", scatter_dimension=0, tiled=True
            ).astype(jnp.float32),
            lax.psum_scatter(
                attn_terms[5].astype(jnp.bfloat16), "batch", scatter_dimension=1, tiled=True
            ).astype(jnp.float32),
            lax.psum_scatter(
                attn_terms[6].astype(jnp.bfloat16), "batch", scatter_dimension=1, tiled=True
            ).astype(jnp.float32),
        )
        attn_total = add_terms(attn_total, attn_share)
    grad_parts = tuple(attn_total) + tuple(ffn_total)
    totals = jax.tree.map(
        lambda part: part.astype(jnp.float32), lax.psum(shortened(grad_parts), "blk")
    )
    output = jnp.concatenate(outputs, axis=0)
    d_input = jnp.concatenate(input_grads, axis=0)
    d_memory = jnp.concatenate(memory_grads, axis=0)
    return (
        output,
        d_input,
        d_memory,
        totals[0],
        totals[1],
        totals[2],
        totals[3],
        totals[4],
        totals[7],
        totals[8],
        totals[9],
        totals[5],
        totals[6],
    )


def swap_pair(array):
    return lax.ppermute(array, "blk", [(0, 1), (1, 0)])


def rows_in(array):
    count = lax.axis_size("blk")
    here = array.shape[0] // count
    parts = array.reshape((count, here) + array.shape[1:])
    if count == 1:
        return parts[0]
    if count == 2:
        me = lax.axis_index("blk")
        kept = lax.dynamic_index_in_dim(parts, me, 0, keepdims=False)
        got = swap_pair(lax.dynamic_index_in_dim(parts, 1 - me, 0, keepdims=False))
        first = jnp.where(me == 0, kept, got)
        second = jnp.where(me == 0, got, kept)
        return jnp.concatenate([first, second], axis=1)
    moved = lax.all_to_all(parts, "blk", 0, 0)
    moved = jnp.moveaxis(moved, 0, 1)
    return moved.reshape((here, count * array.shape[1]) + array.shape[2:])


def rows_out(array, kind):
    count = lax.axis_size("blk")
    here, length = array.shape[:2]
    tokens = length // count
    parts = array.reshape((here, count, tokens) + array.shape[2:])
    if count == 1:
        return parts[:, 0].astype(kind)
    if count == 2:
        me = lax.axis_index("blk")
        kept = lax.dynamic_index_in_dim(parts, me, 1, keepdims=False).astype(kind)
        sent = lax.dynamic_index_in_dim(parts, 1 - me, 1, keepdims=False).astype(jnp.bfloat16)
        got = swap_pair(sent).astype(kind)
        first = jnp.where(me == 0, kept, got)
        second = jnp.where(me == 0, got, kept)
        return jnp.concatenate([first, second], axis=0)
    moved = lax.all_to_all(jnp.moveaxis(parts, 1, 0).astype(jnp.bfloat16), "blk", 0, 0)
    return moved.reshape((count * here, tokens) + array.shape[2:]).astype(kind)


def gathered(shard, axis=0):
    return lax.all_gather(shard, "batch", axis=axis, tiled=True)


def shared_out(grad, axis=0):
    part = lax.psum_scatter(
        grad.astype(jnp.bfloat16), "batch", scatter_dimension=axis, tiled=True
    )
    return lax.psum(part, "blk").astype(jnp.float32)


class Flight:
    def __init__(self, steps):
        self.steps = steps
        self.result = None
        self.wanted = next(steps)
        self.pending = None

    def launch(self):
        self.pending = [send(array) for send, array in self.wanted]

    def advance(self, arrived):
        try:
            self.wanted = self.steps.send(arrived)
        except StopIteration as stop:
            self.wanted, self.result = [], stop.value

    def finish(self):
        while self.result is None:
            if self.pending is None:
                self.launch()
            self.advance(self.pending)
            self.pending = None
        return self.result


def tick(value, *flights):
    flying = [f for f in flights if f.result is None]
    value, arrived = lax.optimization_barrier((value, [f.pending or [] for f in flying]))
    for flight, got in zip(flying, arrived):
        if flight.pending is not None:
            flight.advance(got)
    flying = [f for f in flying if f.result is None]
    value, ready = lax.optimization_barrier((value, [[a for _, a in f.wanted] for f in flying]))
    for flight, arrays in zip(flying, ready):
        flight.wanted = [(send, a) for (send, _), a in zip(flight.wanted, arrays)]
        flight.launch()
    return value


def grid_place():
    batch = lax.axis_index("batch")
    return batch // 4, batch // 2 % 2, batch % 2, lax.axis_index("blk")


def z_sender(step):
    return lambda array: to_z(array, step)


def to_core(array):
    return lax.ppermute(array, "batch", [(n, n ^ 1) for n in range(16)])


def to_x(array):
    return lax.ppermute(array, "batch", [(n, n ^ 2) for n in range(16)])


def to_z(array, step):
    return lax.ppermute(array, "batch", [(n, (n + 4 * step) % 16) for n in range(16)])


def to_core_blk(array):
    pairs = [(2 * n + m, 2 * (n ^ 1) + (1 - m)) for n in range(16) for m in range(2)]
    return lax.ppermute(array, ("batch", "blk"), pairs)


def piece(array, axis, at, size):
    return lax.dynamic_slice_in_dim(array, at * size, size, axis)


def summed_low(terms):
    total = terms[0].astype(jnp.float32)
    for term in terms[1:]:
        total = total + term.astype(jnp.float32)
    return total.astype(jnp.bfloat16)


def in_order(at, own, other, axis):
    first = jnp.where(at == 0, own, other)
    second = jnp.where(at == 0, other, own)
    return jnp.concatenate([first, second], axis=axis)


FLIP = {"x": (0, 1, 0, 0), "c": (0, 0, 1, 0), "y": (0, 0, 0, 1)}
SEND = {"x": to_x, "c": to_core, "y": swap_pair}


def weight_gather(shards, path):
    blk = lax.axis_index("blk")
    if "y" in path:
        shards = [piece(s, 1, blk, s.shape[1] // 2) for s in shards]
    held = [(jnp.concatenate(shards, axis=1)[None], [(0, 0, 0, 0)])]
    return (yield from gather_steps(held, [s.shape for s in shards], path, "y" in path))


def gather_steps(held, shapes, path, split):
    for axis in path:
        if axis == "/":
            (block, labels), count = held[0], (len(shapes) + 1) // 2
            wide = sum(shape[1] for shape in shapes[:count])
            ways = [
                gather_steps([(block[:, :, :wide], labels)], shapes[:count], "yxc", split),
                gather_steps([(block[:, :, wide:], labels)], shapes[count:], "xyc", split),
            ]
            return (yield from together(ways))
        if axis == "z":
            block = jnp.concatenate([a for a, _ in held], axis=0) if len(held) > 1 else held[0][0]
            labels = sum((near for _, near in held), [])
            got = yield [(z_sender(step), block) for step in (1, 2, 3)]
            block = jnp.concatenate([block] + list(got), axis=0)
            held = [(block, [(d, b, c, e) for d in range(4) for _, b, c, e in labels])]
        else:
            got = yield [(SEND[axis], a) for a, _ in held]
            flip = FLIP[axis]
            held = held + [
                (g, [tuple(p + f for p, f in zip(label, flip)) for label in near])
                for g, (_, near) in zip(got, held)
            ]
    return placed_blocks(held, shapes, split)


def together(ways):
    wanted = [next(way) for way in ways]
    results = []
    while not results:
        got = yield sum(wanted, [])
        for n, way in enumerate(ways):
            mine, got = got[: len(wanted[n])], got[len(wanted[n]) :]
            try:
                wanted[n] = way.send(mine)
            except StopIteration as stop:
                results += stop.value
    return results


def place_kernel(near_lists, shapes, split, place, *refs):
    sources, targets = refs[: len(near_lists)], refs[len(near_lists) :]
    for source, near in zip(sources, near_lists):
        for n, (dx, dc, dy) in enumerate(near):
            row = (place[1] + dx) % 2 * 2 + (place[2] + dc) % 2
            first = 0
            for target, (tall, wide) in zip(targets, shapes):
                at = pl.ds(pl.multiple_of(row * tall, tall), tall)
                block = source[n, :, first : first + wide]
                if split:
                    side = (place[3] + dy) % 2
                    target[at, pl.ds(pl.multiple_of(side * wide, wide), wide)] = block
                else:
                    target[at, :] = block
                first += wide


def placed_blocks(held, shapes, split):
    place = jnp.stack(grid_place()).astype(jnp.int32)
    counts = [len(near) // 4 for _, near in held]
    near_lists = [[label[1:] for label in near[:n]] for n, (_, near) in zip(counts, held)]
    outs = [(tall, wide * (2 if split else 1)) for tall, wide in shapes]
    return pl.pallas_call(
        functools.partial(place_kernel, near_lists, shapes, split),
        grid_spec=pltpu.PrefetchScalarGridSpec(
            num_scalar_prefetch=1,
            grid=(4,),
            in_specs=[
                pl.BlockSpec((n,) + a.shape[1:], lambda d, p: (d, 0, 0))
                for n, (a, _) in zip(counts, held)
            ],
            out_specs=[
                pl.BlockSpec((4 * tall, wide), lambda d, p: ((p[0] + 4 - d) % 4, 0))
                for tall, wide in outs
            ],
        ),
        out_shape=[jax.ShapeDtypeStruct((tall * 16, wide), jnp.bfloat16) for tall, wide in outs],
        compiler_params=pltpu.CompilerParams(vmem_limit_bytes=40 * 2**20),
        cost_estimate=SHORT,
        name="place_weights",
    )(place, *[a for a, _ in held])


def halves(terms, axis, at):
    size = terms[0].shape[axis] // 2
    return (
        summed_low([piece(t, axis, 1 - at, size) for t in terms]),
        [piece(t, axis, at, size) for t in terms],
    )


def grads_kernel(plan, halved, *refs):
    lefts = 1 + max(p[0] for p in plan)
    rights = 1 + max(p[1] for p in plan)
    outs = refs[-4 - (2 if halved else 1) : -4]
    extra = refs[lefts + rights : -4 - len(outs)]
    left_buf, right_buf, out_buf, sems = refs[-4:]
    core = lax.axis_index("batch") % 2

    def loads(n):
        left, right, first, wide = plan[n]
        copies = []
        if n == 0 or plan[n - 1][0] != left:
            slot = left % 2
            copies.append(pltpu.make_async_copy(refs[left], left_buf.at[slot], sems.at[0, slot]))
        source = refs[lefts + right].at[:, pl.ds(first, wide)]
        target = right_buf.at[n % 2, :, pl.ds(0, wide)]
        copies.append(pltpu.make_async_copy(source, target, sems.at[1, n % 2]))
        return copies

    def stores(n):
        wide = plan[n][3]
        at = sum(p[3] for p in plan[:n])
        held = out_buf.at[n % 2]
        if not halved:
            place = outs[0].at[:, pl.ds(at, wide)]
            return [pltpu.make_async_copy(held.at[:, pl.ds(0, wide)], place, sems.at[2, n % 2])]
        copies = []
        for side, out in enumerate(outs):
            first = pl.multiple_of((core + 1 - side) % 2 * (wide // 2), wide // 2)
            place = out.at[:, pl.ds(at // 2, wide // 2)]
            source = held.at[:, pl.ds(first, wide // 2)]
            copies.append(pltpu.make_async_copy(source, place, sems.at[2 + side, n % 2]))
        return copies

    for copy in loads(0):
        copy.start()
    if extra:
        wide = extra[0].shape[1]
        held = out_buf.at[0, :, pl.ds(0, wide)]
        place = outs[0].at[:, pl.ds(sum(p[3] for p in plan), wide)]
        for source, target in ((extra[0], held), (held, place)):
            copy = pltpu.make_async_copy(source, target, sems.at[3, 0])
            copy.start()
            copy.wait()
    for n, (left, _, _, wide) in enumerate(plan):
        if n + 1 < len(plan):
            for copy in loads(n + 1):
                copy.start()
        for copy in loads(n):
            copy.wait()
        if n >= 2:
            for copy in stores(n - 2):
                copy.wait()
        grad = lax.dot_general(
            left_buf[left % 2],
            right_buf[n % 2, :, :wide],
            (((0,), (0,)), ((), ())),
            preferred_element_type=jnp.float32,
        )
        out_buf[n % 2, :, :wide] = grad.astype(out_buf.dtype)
        for copy in stores(n):
            copy.start()
    for n in range(max(0, len(plan) - 2), len(plan)):
        for copy in stores(n):
            copy.wait()


def joined_grads(products, halved, extra=()):
    lefts, rights, plan = [], [], []
    for left, group in products:
        lefts.append(left)
        for right in group:
            rights.append(right)
            wide = min(right.shape[1], D)
            for first in range(0, right.shape[1], wide):
                plan.append((len(lefts) - 1, len(rights) - 1, first, wide))
    tokens, rows = lefts[0].shape
    total = sum(p[3] for p in plan) + sum(e.shape[1] for e in extra)
    shape = jax.ShapeDtypeStruct((rows, total // 2 if halved else total), jnp.bfloat16)
    anywhere = pl.BlockSpec(memory_space=pl.ANY)
    widest = max(p[3] for p in plan)
    return pl.pallas_call(
        functools.partial(grads_kernel, plan, halved),
        in_specs=[anywhere] * (len(lefts) + len(rights) + len(extra)),
        out_specs=[anywhere] * (2 if halved else 1),
        out_shape=[shape] * (2 if halved else 1),
        scratch_shapes=[
            pltpu.VMEM((2, tokens, rows), jnp.bfloat16),
            pltpu.VMEM((2, tokens, widest), jnp.bfloat16),
            pltpu.VMEM((2, rows, widest), jnp.bfloat16),
            pltpu.SemaphoreType.DMA((4, 2)),
        ],
        compiler_params=pltpu.CompilerParams(vmem_limit_bytes=48 * 2**20),
        cost_estimate=SHORT,
        name="joined_grads",
    )(*lefts, *rights, *extra)


def gradient_reduce(products, path):
    z, x, core, blk = grid_place()
    given, kept = joined_grads(products, True)
    (got,) = yield [(to_core, given)]
    rows, columns = kept.shape
    terms = [t.reshape(4, 2, rows // 8, columns) for t in (kept, got)]
    for axis in path:
        if axis == "z":
            out = []
            for step in (1, 2, 3):
                parts = [piece(t, 0, (z + step) % 4, 1) for t in terms]
                out.append((z_sender(step), summed_low(parts)))
            out = yield out
            terms = [piece(t, 0, z, 1) for t in terms] + list(out)
        else:
            out, terms = halves(terms, 1, x) if axis == "x" else halves(terms, 3, blk)
            out = yield [(to_x if axis == "x" else swap_pair, out)]
            terms = terms + list(out)
    total = summed_low(terms).reshape(rows // 8, columns // 2)
    mine = piece(total, 0, core, rows // 16)
    theirs = piece(total, 0, 1 - core, rows // 16)
    from_blk, from_core, from_both = yield [
        (swap_pair, mine),
        (to_core, theirs),
        (to_core_blk, theirs),
    ]
    near = in_order(blk, mine, from_blk, 1).astype(jnp.float32)
    far = in_order(blk, from_core, from_both, 1).astype(jnp.float32)
    left, right = jnp.where(core == 0, near, far), jnp.where(core == 0, far, near)
    results, first = [], 0
    for _, rights in products:
        for whole_wide in [r.shape[1] for r in rights]:
            blocks = []
            for _ in range(0, whole_wide, min(whole_wide, D)):
                wide = min(whole_wide, D) // 2
                blocks += [left[:, first : first + wide], right[:, first : first + wide]]
                first += wide
            results.append(jnp.concatenate(blocks, axis=1))
    return results


def over_batch(array):
    return lax.psum_scatter(array, "batch", scatter_dimension=0, tiled=True)


def whole_reduce(products, small=None):
    if not on_small_slice():
        yield []
        grads = [shared_out(weight_grad(left, r)) for left, rights in products for r in rights]
        grad = jnp.concatenate(grads, axis=1)
        return grad if small is None else (grad, shared_out(small[0], 1), shared_out(small[1]))
    extra = ()
    if small is not None:
        columns = jnp.concatenate([small[0].T, small[1].reshape(D, -1)], axis=1)
        columns = jnp.pad(columns, ((0, 0), (0, PAIR - columns.shape[1])))
        extra = (columns.astype(jnp.bfloat16),)
    if len(products) == 1:
        grad = weight_grad(products[0][0], products[0][1][0]).astype(jnp.bfloat16)
    else:
        (grad,) = joined_grads(products, False, extra)
    (part,) = yield [(over_batch, grad)]
    (got,) = yield [(swap_pair, part)]
    total = part.astype(jnp.float32) + got.astype(jnp.float32)
    if small is None:
        return total
    total, columns, count = total[:, :-PAIR], total[:, -PAIR:], small[0].shape[0]
    bias = columns[:, count : count + small[1].shape[0] // D]
    return total, columns[:, :count].T, bias.reshape(-1)


def batch_sender(bit):
    return lambda array: lax.ppermute(array, "batch", [(n, n ^ bit) for n in range(16)])


def total_of_all(array):
    for send in (to_core, to_x, swap_pair, batch_sender(4), batch_sender(8)):
        (got,) = yield [(send, array)]
        array = array + got
    return array


def small_gather(gains, shifts, bias):
    packed = jnp.concatenate([gains, shifts, bias.reshape(-1, gains.shape[1])], axis=0)
    place = jnp.arange(16)[:, None, None] == lax.axis_index("batch")
    held = jnp.where(place, packed[None], jnp.zeros_like(packed)[None])
    for bit in (1, 2, 4, 8):
        (got,) = yield [(batch_sender(bit), held)]
        held = held + got
    rows = jnp.moveaxis(held[:, :7], 0, 1).reshape(7, -1)
    return rows[:3], rows[3:], held[:, 7:].reshape(-1)


def rows_in_steps(array):
    if lax.axis_size("blk") != 2:
        yield []
        return rows_in(array)
    here = array.shape[0] // 2
    parts = array.reshape((2, here) + array.shape[1:])
    me = lax.axis_index("blk")
    (got,) = yield [(swap_pair, lax.dynamic_index_in_dim(parts, 1 - me, 0, keepdims=False))]
    return in_order(me, lax.dynamic_index_in_dim(parts, me, 0, keepdims=False), got, 1)


def rows_out_steps(array, kind):
    if lax.axis_size("blk") != 2:
        yield []
        return rows_out(array, kind)
    here, length = array.shape[:2]
    parts = array.reshape((here, 2, length // 2) + array.shape[2:])
    me = lax.axis_index("blk")
    sent = lax.dynamic_index_in_dim(parts, 1 - me, 1, keepdims=False).astype(jnp.bfloat16)
    (got,) = yield [(swap_pair, sent)]
    kept = lax.dynamic_index_in_dim(parts, me, 1, keepdims=False).astype(kind)
    return in_order(me, kept, got.astype(kind), 0)


def plain_gather(shards):
    yield []
    return [gathered(s) for s in shards]


def plain_small_gather(gains, shifts, bias):
    yield []
    return gathered(gains, 1), gathered(shifts, 1), gathered(bias)


def plain_reduce(products):
    yield []
    return [
        shared_out(weight_grad(left, right)) for left, rights in products for right in rights
    ]


def on_small_slice():
    return lax.axis_size("batch") == 16 and lax.axis_size("blk") == 2


def start_gather(shards, path):
    return Flight(weight_gather(shards, path) if on_small_slice() else plain_gather(shards))


def whole_gather(shard):
    (full,) = yield [(gathered, shard)]
    return [full]


def start_whole_gather(shard):
    return Flight(whole_gather(shard))


def start_reduce(products, path):
    return Flight(gradient_reduce(products, path) if on_small_slice() else plain_reduce(products))


def start_small(gains, shifts, bias):
    steps = small_gather if on_small_slice() else plain_small_gather
    return Flight(steps(gains, shifts, bias))


def small_reduce(rows, bias):
    if not on_small_slice():
        yield []
        return shared_out(rows, 1), shared_out(bias)
    packed = yield from total_of_all(jnp.concatenate([rows, bias.reshape(-1, D)], axis=0))
    me = lax.axis_index("batch")
    bias = packed[rows.shape[0] :].reshape(-1)
    return (
        piece(packed[: rows.shape[0]], 1, me, D // 16),
        piece(bias, 0, me, bias.shape[0] // 16),
    )


def each_row(function, rows, arrays):
    if rows == 1:
        return function(*arrays)

    def cut(array, n):
        size = array.shape[0] // rows
        return array[n * size : (n + 1) * size]

    results = [function(*(cut(a, n) for a in arrays)) for n in range(rows)]
    return [jnp.concatenate(group, axis=0) for group in zip(*results)]


def dot32(left, right):
    return jnp.dot(left, right, preferred_element_type=jnp.float32)


def whole_row_device(
    inputs,
    memory,
    target_ids,
    memory_ids,
    cotangent,
    w_self_qkv,
    w_self_out,
    w_cross_q,
    w_cross_kv,
    w_cross_out,
    w_up,
    w_down,
    b_up,
    gains,
    shifts,
):
    low = jnp.bfloat16
    half = NH // 4
    shard_rows = w_self_qkv.shape[0]
    columns = [w_self_qkv, w_self_out, w_cross_q, w_cross_kv, w_cross_out]
    columns += [gains.T, shifts.T, b_up.reshape(shard_rows, -1)]
    spare = -sum(c.shape[1] for c in columns) % PAIR
    columns.append(jnp.zeros((shard_rows, spare), low))
    attn_full = gathered(jnp.concatenate(columns, axis=1))
    at, fulls = 0, []
    for wide in [D] * 8 + [c.shape[1] for c in columns[5:8]]:
        fulls.append(attn_full[:, at : at + wide])
        at += wide
    qkv_full, (mk_full, mv_full) = fulls[:3], fulls[5:7]
    out_block, cross_q_block, cross_out_block = (column_block(attn_full, n) for n in (3, 4, 7))
    norms = jnp.concatenate([fulls[8].T, fulls[9].T, jnp.zeros((1, D), low)], axis=0)
    norms = norms.astype(jnp.float32)
    bias_full = fulls[10].reshape(-1).astype(jnp.float32)
    up_parts = [w_up[:, n : n + D] for n in range(0, w_up.shape[1], D)]
    down_rows = w_down.shape[0]
    ffn_shard = jnp.concatenate(up_parts + [w_down, jnp.zeros((8, D), low)], axis=0)
    ffn_full = lax.all_gather(ffn_shard, "batch", axis=0)
    x_rows = Flight(rows_in_steps(inputs))
    ids = Flight(rows_in_steps(jnp.stack([target_ids, memory_ids], axis=2)))
    memory = tick(memory, x_rows, ids)
    memory_rows = Flight(rows_in_steps(memory))
    cotangent = tick(cotangent, x_rows, ids, memory_rows)
    cot_rows = Flight(rows_in_steps(cotangent))
    x_rows = x_rows.finish()
    rows, length = x_rows.shape[:2]
    x_flat = lax.optimization_barrier(x_rows.reshape(-1, D))
    ids = ids.finish()
    target_flat = ids[:, :, 0].reshape(-1)
    memory_id_flat = ids[:, :, 1].reshape(-1)
    memory_flat = lax.optimization_barrier(memory_rows.finish().reshape(-1, D))
    full = jnp.float32

    def self_forward(q, k, v, id_row, pairs):
        fq, fk = document_features(id_row, id_row)
        return attention_forward(q, k, v, fq, fk, True, pairs)

    qkv = [dot32(x_flat, w).astype(low) for w in qkv_full]
    mixed_flat, self_lse = each_row(
        functools.partial(self_forward, pairs=(0, 2 * half)), rows, (*qkv, target_flat)
    )
    first_sum, first, first_low, cross_queries = row_tiles(
        first_norm_kernel,
        "first_norm",
        [mixed_flat, x_flat],
        [out_block, cross_q_block, small_block(norms)],
        [full, full, low, low],
    )
    cross_queries = tick(cross_queries, cot_rows)
    memory_keys = dot32(memory_flat, mk_full).astype(low)
    memory_values = dot32(memory_flat, mv_full).astype(low)

    def cross_forward(q, k, v, id_row, memory_id_row, pairs):
        fq, fk = document_features(id_row, memory_id_row)
        return attention_forward(q, k, v, fq, fk, False, pairs)

    arrays = (cross_queries, memory_keys, memory_values, target_flat, memory_id_flat)
    mixed = each_row(functools.partial(cross_forward, pairs=(0, 2 * half)), rows, arrays)
    cross_flat, cross_lse = tick(mixed, cot_rows)
    second_sum, second, second_low = row_tiles(
        second_norm_kernel,
        "second_norm",
        [cross_flat, first],
        [cross_out_block, small_block(norms)],
        [full, full, low],
    )
    hidden_low, slope = gelu_rows(second_low, ffn_full, bias_full)
    cot_flat = cot_rows.finish().reshape(-1, D)
    ffn_block = (ffn_full.shape[0], down_rows, D)
    result, d_third, d_branch_three, third_sums = row_tiles(
        third_norm_kernel,
        "third_norm",
        [hidden_low, second, cot_flat],
        [(ffn_full, ffn_block, (0, 1, 0)), small_block(norms)],
        [low, full, low],
        True,
    )

    output = Flight(rows_out_steps(result.reshape(rows, length, D), low))
    down_grad = Flight(whole_reduce([(hidden_low, [d_branch_three])]))
    d_branch_three, d_third = tick((d_branch_three, d_third), output, down_grad)
    d_pre, grad_bias_up = gelu_back_rows(d_branch_three, ffn_full, slope)
    up_grad = start_reduce([(second_low, [d_pre])], "xyz")
    d_pre = tick(d_pre, up_grad)
    d_second_sum, d_branch_two, d_cross, second_sums = row_tiles(
        second_back_kernel,
        "second_back",
        [d_pre, d_third, second_sum],
        [(ffn_full, ffn_block, (0, 0, 0)), cross_out_block, small_block(norms)],
        [full, low, low],
        True,
    )
    d_branch_two, d_cross = tick((d_branch_two, d_cross), up_grad)

    def cross_backward(id_row, memory_id_row, *arrays, pairs):
        fq, fk = document_features(id_row, memory_id_row)
        return attention_backward(fq, fk, *arrays, False, pairs)

    arrays = (target_flat, memory_id_flat, cross_queries, memory_keys, memory_values)
    arrays += (cross_flat, cross_lse, d_cross)
    grads = each_row(functools.partial(cross_backward, pairs=(0, 2 * half)), rows, arrays)
    d_cross_low, d_memory_keys, d_memory_values = tick(grads, output)
    d_first_sum, d_branch_one, d_self, first_sums = row_tiles(
        first_back_kernel,
        "first_back",
        [d_cross_low, d_second_sum, first_sum],
        [cross_q_block, out_block, small_block(norms)],
        [full, low, low],
        True,
    )
    d_branch_one, d_self = tick((d_branch_one, d_self), up_grad)
    every = [first_sums[0], second_sums[0], third_sums[0]]
    grad_rows = every + [first_sums[1], second_sums[1], third_sums[1], third_sums[2]]
    cross_grad = Flight(
        whole_reduce(
            [
                (memory_flat, [d_memory_keys, d_memory_values]),
                (first_low, [d_cross_low]),
                (cross_flat, [d_branch_two]),
                (mixed_flat, [d_branch_one]),
            ],
            (jnp.stack(grad_rows), grad_bias_up),
        )
    )
    d_self = tick(d_self, cross_grad)
    d_memory = back_prod(d_memory_keys, mk_full) + back_prod(d_memory_values, mv_full)
    d_self, d_memory = lax.optimization_barrier((d_self, d_memory))
    d_memory = Flight(rows_out_steps(d_memory.reshape(rows, length, D), jnp.float32))
    d_self = tick(d_self, down_grad, d_memory, up_grad)

    def self_backward(id_row, *arrays, pairs):
        fq, fk = document_features(id_row, id_row)
        return attention_backward(fq, fk, *arrays, True, pairs)

    arrays = (target_flat, *qkv, mixed_flat, self_lse, d_self)
    grads_a = each_row(functools.partial(self_backward, pairs=(0, half)), rows, arrays)
    grads_a = tick(grads_a, up_grad, down_grad)
    early_grad = start_reduce([(x_flat, grads_a)], "xzy")
    d_self = tick(d_self, early_grad, d_memory)
    arrays = (target_flat, *qkv, mixed_flat, self_lse, d_self)
    grads_b = each_row(functools.partial(self_backward, pairs=(half, half)), rows, arrays)
    grads_b = tick(grads_b, early_grad, up_grad)
    d_input = ALPHA * d_first_sum
    for grad_a, grad_b, weight in zip(grads_a, grads_b, qkv_full):
        d_input = d_input + back_prod(jnp.concatenate([grad_a, grad_b], axis=1), weight)
    d_input = Flight(rows_out_steps(d_input.reshape(rows, length, D), jnp.float32))
    grads_b = tick(grads_b, d_input)
    late_grad = start_reduce([(x_flat, grads_b)], "xzy")
    token = tick(grads_b[0], late_grad, early_grad)
    token = tick(token, late_grad)
    flights = [late_grad, early_grad, d_input, cross_grad]
    while any(f.result is None for f in flights):
        token = tick(token, *flights)
    grads, grad_rows, grad_bias_up = cross_grad.finish()
    grad_kv, grad_cross_q, grad_cross_out, grad_self_out = jnp.split(
        grads, [2 * D, 3 * D, 4 * D], axis=1
    )
    grad_qa, grad_ka, grad_va = early_grad.finish()
    grad_qb, grad_kb, grad_vb = late_grad.finish()
    return (
        output.finish(),
        d_input.finish(),
        d_memory.finish(),
        jnp.concatenate([grad_qa, grad_qb, grad_ka, grad_kb, grad_va, grad_vb], axis=1),
        grad_self_out,
        grad_cross_q,
        grad_kv,
        grad_cross_out,
        up_grad.finish()[0],
        down_grad.finish(),
        grad_bias_up,
        grad_rows[:3],
        grad_rows[3:],
    )


def per_device(inputs, *others):
    if inputs.shape[0] % lax.axis_size("blk") == 0:
        return whole_row_device(inputs, *others)
    return split_row_device(inputs, *others)


def solution(mesh):
    return jax.shard_map(
        per_device,
        mesh=mesh,
        in_specs=(
            P("batch", "blk", None),
            P("batch", "blk", None),
            P("batch", "blk"),
            P("batch", "blk"),
            P("batch", "blk", None),
            P("batch", None),
            P("batch", None),
            P("batch", None),
            P("batch", None),
            P("batch", None),
            P("batch", None),
            P("batch", None),
            P("batch"),
            P(None, "batch"),
            P(None, "batch"),
        ),
        out_specs=(
            P("batch", "blk", None),
            P("batch", "blk", None),
            P("batch", "blk", None),
            P("batch", None),
            P("batch", None),
            P("batch", None),
            P("batch", None),
            P("batch", None),
            P("batch", None),
            P("batch", None),
            P("batch"),
            P(None, "batch"),
            P(None, "batch"),
        ),
        check_vma=False,
    )
```
